256 devices in a mesh: dp: 32 (over z, y_lo, core), node: 8 (over y_hi, x).
Axes of the slice: x: 4, y: 4 (y_hi: 2, y_lo: 2; y = y_hi * 2 + y_lo), z: 8, core: 2. Of those that a mesh axis runs over, the one named last changes fastest.
Arguments:
- tokens: bfloat16 [32768, 3072], P(('dp', 'node')), may hold values from -6 to 6
- cotangent: bfloat16 [32768, 3072], P(('dp', 'node')), may hold values from -6 to 6
- levels: bfloat16 [3072, 3072], P('node'), may hold values from -127 to 127, as said below
- scales: float32 [3072, 12], P('node'), may hold values from 0.00012 to 0.00048
Outputs:
- forward: bfloat16 [32768, 3072], P(('dp', 'node'))
- grad_input: bfloat16 [32768, 3072], P(('dp', 'node'))
- grad_weight: float32 [3072, 3072], P(('dp', 'node'))
The draws below stay inside these ranges and needn't reach their ends.
Inputs may be any that keep to these rules, and one draw needn't show every extreme that they name: `levels`: every entry is a whole number.
All inputs are finite; a program needn't handle non-finite values.
Results may differ from the reference program's by a relative error of at most 0.0049.
Values may be sent and summed in bfloat16 or wider, within the bound.
No kernel may reach another device: no remote copies, remote signals or barrier semaphores. Data moves between devices by JAX's collectives and lax.ppermute only.
A program may use at most 192 MiB of HBM per device.

```python
import math
import jax
import jax.numpy as jnp
from jax import lax

DIN = 3072
BLOCK = 256
TOK_DEV = 128
DOUT = 3072
TOKENS = 32768
N_DP = 32
N_NODE = 8


def draw_levels(key, part):
    key = jax.random.fold_in(key, 5)
    values = jax.random.randint(key, (DIN, DOUT), -127, 128)
    return values.astype(jnp.float32).astype(jnp.bfloat16)


def steps_of(rng, shape, cuts, smallest, largest):
    def one(position, shards_of):
        heights = jax.random.uniform(jax.random.fold_in(jax.random.fold_in(rng, 6), position), (shards_of,), jnp.float32, smallest / len(cuts), largest / len(cuts))
        return jnp.repeat(jnp.exp(heights), shape[position] // shards_of).reshape((-1,) + (1,) * (len(shape) - position - 1))

    loudness = one(*cuts[0])
    for cut in cuts[1:]:
        loudness = loudness * one(*cut)
    return loudness


def gaussian(stream_key, extent, scale, limit, cuts=(), kind=jnp.bfloat16):
    gain = steps_of(stream_key, extent, cuts, -0.22, 0.18) if cuts else 1.0
    drawn = jax.random.normal(stream_key, extent, jnp.float32) * scale * gain
    return jnp.minimum(jnp.maximum(drawn, -limit), limit).astype(kind)


def setup_inputs(seed: int = 0) -> dict:
    key_of = jax.random.split(jax.random.key(seed), 5)
    return {
        "tokens": gaussian(key_of[0], (TOKENS, DIN), 1.0, 6.0, ((0, 256),)),
        "cotangent": gaussian(key_of[1], (TOKENS, DOUT), 1.0, 6.0, ((0, 256),)),
        "levels": draw_levels(jax.random.fold_in(key_of[4], 71), 0),
        "scales": jnp.clip(jnp.exp(math.log(0.00048) - 1.3862944 * jax.random.uniform(key_of[3], (DIN, DOUT // BLOCK), jnp.float32) ** steps_of(key_of[3], (DIN, DOUT // BLOCK), ((0, 8),), -0.2, 0.2)), 0.00012, 0.00048),
    }


def dequantize(level_rows, scale_rows):
    row_count, width = level_rows.shape
    blocked = level_rows.astype(jnp.float32).reshape(row_count, scale_rows.shape[1], width // scale_rows.shape[1])
    return (blocked * scale_rows[:, :, None]).reshape(row_count, width).astype(jnp.bfloat16)


def reference(tokens, cotangent, levels, scales):
    weight = dequantize(levels, scales)
    forward = jnp.dot(tokens, weight, preferred_element_type=jnp.float32).astype(jnp.bfloat16)
    grad_input = jnp.dot(cotangent, weight.T, preferred_element_type=jnp.float32).astype(jnp.bfloat16)
    group_rows = N_NODE * TOK_DEV
    token_groups = tokens.reshape(N_DP, group_rows, DIN)
    cotangent_groups = cotangent.reshape(N_DP, group_rows, DOUT)
    factor = TOKENS ** -0.5

    def add_group(running, paired):
        partial_value = jnp.dot(paired[0].T, paired[1], preferred_element_type=jnp.float32) * factor
        return running + partial_value, None

    grad_weight, unused = lax.scan(add_group, jnp.zeros((DIN, DOUT), jnp.float32), (token_groups, cotangent_groups))
    return forward, grad_input, grad_weight
```

```python
import jax
import jax.numpy as jnp
from jax import lax
from jax.sharding import Mesh, PartitionSpec as P

AXES = ("z", "yl", "c", "yh", "x")
SIZES = (8, 2, 2, 2, 4)
CHUNKS = 2


def table(move):
    pairs = []
    for z in range(8):
        for yl in range(2):
            for c in range(2):
                for yh in range(2):
                    for x in range(4):
                        pairs.append((place(z, yl, c, yh, x), place(*move(z, yl, c, yh, x))))
    return pairs


def place(z, yl, c, yh, x):
    return (((z % 8 * 2 + yl % 2) * 2 + c % 2) * 2 + yh % 2) * 4 + x % 4


def owner(z, yl, yh, x, k):
    return 4 * yh + z // 2, z % 2, yl, x // 2, x % 2 * 2 + k


X_UP = table(lambda z, yl, c, yh, x: (z, yl, c, yh, x + 1))
X_DOWN = table(lambda z, yl, c, yh, x: (z, yl, c, yh, x - 1))
Z_UP = table(lambda z, yl, c, yh, x: (z + 1, yl, c, yh, x))
Z_DOWN = table(lambda z, yl, c, yh, x: (z - 1, yl, c, yh, x))
CORE = table(lambda z, yl, c, yh, x: (z, yl, c + 1, yh, x))
PAIR = table(lambda z, yl, c, yh, x: (z, yl + 1, c, yh + 1, x))
OWNER_SAME = table(lambda z, yl, c, yh, x: owner(z, yl, yh, x, c))
OWNER_OTHER = table(lambda z, yl, c, yh, x: owner(z, yl, yh, x, 1 - c))


def send(value, pairs):
    return lax.ppermute(value, AXES, pairs)


def cols(value, start, size):
    return lax.dynamic_slice_in_dim(value, start, size, 1)


def rows(value, start, size):
    return lax.dynamic_slice_in_dim(value, start, size, 0)


def dequantize(level_rows, scale_rows):
    row_count, width = level_rows.shape
    blocked = level_rows.astype(jnp.float32).reshape(
        row_count, scale_rows.shape[1], width // scale_rows.shape[1]
    )
    return (blocked * scale_rows[:, :, None]).reshape(row_count, width).astype(jnp.bfloat16)


def f32(value):
    return value.astype(jnp.float32)


def bf16(value):
    return value.astype(jnp.bfloat16)


def reduce_over_z(part, z):
    size = part.shape[0] // 8
    half = size // 2

    def chunk(k):
        return rows(part, (z + k + 8) % 8 * size, size)

    far = chunk(4)
    up, down = bf16(far[:half]), bf16(far[half:])
    for step in range(4):
        up, down = send(up, Z_UP), send(down, Z_DOWN)
        near_up, near_down = chunk(3 - step), chunk(step - 3)
        if step == 0:
            up = jnp.concatenate([bf16(near_up[:half] + f32(up)), bf16(near_up[half:])])
            down = jnp.concatenate([bf16(near_down[:half]), bf16(near_down[half:] + f32(down))])
        elif step < 3:
            up, down = bf16(near_up + f32(up)), bf16(near_down + f32(down))
        else:
            return near_up + f32(up) + f32(down)


def reduce_over_x_yl(part, x, yl):
    size = part.shape[0] // 8
    total = rows(part, (yl * 4 + x) * size, size)
    for dy in range(2):
        for dx in range(4):
            if dy or dx:
                piece = bf16(rows(part, ((yl + dy) % 2 * 4 + (x + dx) % 4) * size, size))
                to = table(lambda z, yl, c, yh, x: (z, yl + dy, c, yh, x + dx))
                total = total + f32(send(piece, to))
    return total


def on_device(tokens, cotangent, levels, scales):
    z, yl, c, yh, x = (lax.axis_index(name) for name in AXES)
    count, features = tokens.shape
    shard, outputs = levels.shape
    kh, nh = features // 2, outputs // 2
    width = nh // CHUNKS
    factor = float(count * 256) ** -0.5

    from_pair = send(cols(tokens, (1 - yh) * kh, kh), PAIR)
    mine = jnp.concatenate([cols(tokens, yh * kh, kh), from_pair])
    token4 = jnp.concatenate([mine, send(mine, CORE)])

    own = dequantize(cols(levels, c * nh, nh), cols(scales, c * (scales.shape[1] // 2), scales.shape[1] // 2))

    cot4, weight, forward, other_forward, grads = [], [], [], [], []
    for j in range(CHUNKS):
        parts = [cotangent[:, h * nh + j * width : h * nh + (j + 1) * width] for h in range(2)]
        local = jnp.concatenate(parts, axis=1)
        both = jnp.concatenate([local, send(local, PAIR)])
        swapped = send(cols(both, (1 - c) * width, width), CORE)
        cot4.append(jnp.concatenate([cols(both, c * width, width), swapped]))

        w = own[:, j * width : (j + 1) * width]
        left, right = send(w, X_UP), send(w, X_DOWN)
        far = jnp.concatenate([send(left[: shard // 2], X_UP), send(right[shard // 2 :], X_DOWN)])
        whole = jnp.zeros((4 * shard, width), jnp.bfloat16)
        for k, block in ((0, w), (3, left), (1, right), (2, far)):
            whole = lax.dynamic_update_slice_in_dim(whole, block, (x + k) % 4 * shard, 0)
        weight.append(whole)

    for j in range(CHUNKS):
        part = lax.dot_general(
            token4, cot4[j], (((0,), (0,)), ((), ())), preferred_element_type=jnp.float32
        )
        grads.append(reduce_over_x_yl(reduce_over_z(part, z), x, yl))

    grad4 = 0.0
    for j in range(CHUNKS):
        out = jnp.dot(token4, weight[j], preferred_element_type=jnp.float32)
        away = bf16(jnp.concatenate([out[count : 2 * count], out[3 * count :]]))
        back = f32(send(away, PAIR))
        forward.append(bf16(out[:count] + back[:count]))
        other_forward.append(send(bf16(out[2 * count : 3 * count] + back[count:]), CORE))
        grad4 = grad4 + lax.dot_general(
            cot4[j], weight[j], (((1,), (1,)), ((), ())), preferred_element_type=jnp.float32
        )

    here, there = jnp.concatenate(forward, axis=1), jnp.concatenate(other_forward, axis=1)
    forward = jnp.where(
        c == 0, jnp.concatenate([here, there], axis=1), jnp.concatenate([there, here], axis=1)
    )

    grad2 = grad4[: 2 * count] + f32(send(bf16(grad4[2 * count :]), CORE))
    here, there = bf16(grad2[:count]), send(bf16(grad2[count:]), PAIR)
    grad_input = jnp.where(
        yh == 0, jnp.concatenate([here, there], axis=1), jnp.concatenate([there, here], axis=1)
    )

    total = jnp.concatenate(grads, axis=1) * factor
    size = total.shape[0] // 2
    same = send(rows(total, c * size, size), OWNER_SAME)
    other = send(rows(total, (1 - c) * size, size), OWNER_OTHER)
    grad_weight = jnp.where(
        x % 2 == 0, jnp.concatenate([same, other], axis=1), jnp.concatenate([other, same], axis=1)
    )
    return forward, grad_input, grad_weight


def solution(mesh):
    fine = Mesh(mesh.devices.reshape(SIZES), AXES)
    token_spec, node_spec = P(AXES, None), P(("yh", "x"), None)
    return jax.shard_map(
        on_device,
        mesh=fine,
        in_specs=(token_spec, token_spec, node_spec, node_spec),
        out_specs=(token_spec, token_spec, token_spec),
        check_vma=False,
    )
```

```python
import jax
import jax.numpy as jnp
from jax import lax
from jax.sharding import Mesh, PartitionSpec as P

AXES = ("z", "yl", "c", "yh", "x")
SIZES = (8, 2, 2, 2, 4)
CHUNKS = 2


def table(move):
    pairs = []
    for z in range(8):
        for yl in range(2):
            for c in range(2):
                for yh in range(2):
                    for x in range(4):
                        pairs.append((place(z, yl, c, yh, x), place(*move(z, yl, c, yh, x))))
    return pairs


def place(z, yl, c, yh, x):
    return (((z % 8 * 2 + yl % 2) * 2 + c % 2) * 2 + yh % 2) * 4 + x % 4


def owner(z, yl, yh, x, k):
    return 4 * yh + z // 2, z % 2, yl, x // 2, x % 2 * 2 + k


X_UP = table(lambda z, yl, c, yh, x: (z, yl, c, yh, x + 1))
X_DOWN = table(lambda z, yl, c, yh, x: (z, yl, c, yh, x - 1))
Z_UP = table(lambda z, yl, c, yh, x: (z + 1, yl, c, yh, x))
Z_DOWN = table(lambda z, yl, c, yh, x: (z - 1, yl, c, yh, x))
CORE = table(lambda z, yl, c, yh, x: (z, yl, c + 1, yh, x))
PAIR = table(lambda z, yl, c, yh, x: (z, yl + 1, c, yh + 1, x))
OWNER_SAME = table(lambda z, yl, c, yh, x: owner(z, yl, yh, x, c))
OWNER_OTHER = table(lambda z, yl, c, yh, x: owner(z, yl, yh, x, 1 - c))


def send(value, pairs):
    return lax.ppermute(value, AXES, pairs)


def cols(value, start, size):
    return lax.dynamic_slice_in_dim(value, start, size, 1)


def rows(value, start, size):
    return lax.dynamic_slice_in_dim(value, start, size, 0)


def after(values, *earlier):
    return lax.optimization_barrier((values, earlier))[0]


def dequantize(level_rows, scale_rows):
    row_count, width = level_rows.shape
    blocked = level_rows.astype(jnp.float32).reshape(
        row_count, scale_rows.shape[1], width // scale_rows.shape[1]
    )
    return (blocked * scale_rows[:, :, None]).reshape(row_count, width).astype(jnp.bfloat16)


def f32(value):
    return value.astype(jnp.float32)


def bf16(value):
    return value.astype(jnp.bfloat16)


def reduce_over_z(part, z):
    size = part.shape[0] // 8
    half = size // 2

    def chunk(k):
        return rows(part, (z + k + 8) % 8 * size, size)

    far = chunk(4)
    up, down = bf16(far[:half]), bf16(far[half:])
    for step in range(4):
        up, down = send(up, Z_UP), send(down, Z_DOWN)
        near_up, near_down = chunk(3 - step), chunk(step - 3)
        if step == 0:
            up = jnp.concatenate([bf16(near_up[:half] + f32(up)), bf16(near_up[half:])])
            down = jnp.concatenate([bf16(near_down[:half]), bf16(near_down[half:] + f32(down))])
        elif step < 3:
            up, down = bf16(near_up + f32(up)), bf16(near_down + f32(down))
        else:
            return near_up + f32(up) + f32(down)


def reduce_over_x_yl(part, x, yl):
    size = part.shape[0] // 8
    total = rows(part, (yl * 4 + x) * size, size)
    for dy in range(2):
        for dx in range(4):
            if dy or dx:
                piece = bf16(rows(part, ((yl + dy) % 2 * 4 + (x + dx) % 4) * size, size))
                to = table(lambda z, yl, c, yh, x: (z, yl + dy, c, yh, x + dx))
                total = total + f32(send(piece, to))
    return total


def on_device(tokens, cotangent, levels, scales):
    z, yl, c, yh, x = (lax.axis_index(name) for name in AXES)
    count, features = tokens.shape
    shard, outputs = levels.shape
    kh, nh = features // 2, outputs // 2
    width = nh // CHUNKS
    factor = float(count * 256) ** -0.5

    from_pair = send(cols(tokens, (1 - yh) * kh, kh), PAIR)
    mine = jnp.concatenate([cols(tokens, yh * kh, kh), from_pair])
    token4 = jnp.concatenate([mine, send(mine, CORE)])

    cot4 = []
    for j in range(CHUNKS):
        parts = [cotangent[:, h * nh + j * width : h * nh + (j + 1) * width] for h in range(2)]
        local = jnp.concatenate(parts, axis=1)
        both = jnp.concatenate([local, send(local, PAIR)])
        swapped = send(cols(both, (1 - c) * width, width), CORE)
        cot4.append(jnp.concatenate([cols(both, c * width, width), swapped]))

    half_scales = scales.shape[1] // 2
    own = dequantize(cols(levels, c * nh, nh), cols(scales, c * half_scales, half_scales))
    left, right = send(own, X_UP), send(own, X_DOWN)

    grads = []
    for j in range(CHUNKS):
        grads.append(
            lax.dot_general(
                token4, cot4[j], (((0,), (0,)), ((), ())), preferred_element_type=jnp.float32
            )
        )
    left, right = after((left, right), grads[0])
    far = jnp.concatenate([send(left[: shard // 2], X_UP), send(right[shard // 2 :], X_DOWN)])
    far, token4 = after((far, token4), grads[-1])
    sums = [reduce_over_z(part, z) for part in grads]

    weight = jnp.zeros((4 * shard, nh), jnp.bfloat16)
    for k, block in ((0, own), (3, left), (1, right), (2, far)):
        weight = lax.dynamic_update_slice_in_dim(weight, block, (x + k) % 4 * shard, 0)

    out = jnp.dot(token4, weight, preferred_element_type=jnp.float32)
    away = bf16(jnp.concatenate([out[count : 2 * count], out[3 * count :]]))
    back = f32(send(away, PAIR))
    here = bf16(out[:count] + back[:count])
    there = send(bf16(out[2 * count : 3 * count] + back[count:]), CORE)
    forward = jnp.where(
        c == 0, jnp.concatenate([here, there], axis=1), jnp.concatenate([there, here], axis=1)
    )

    weight, _ = after((weight, cot4[0]), away)
    grad4 = lax.dot_general(
        jnp.concatenate(cot4, axis=1), weight, (((1,), (1,)), ((), ())), preferred_element_type=jnp.float32
    )
    grad2 = grad4[: 2 * count] + f32(send(bf16(grad4[2 * count :]), CORE))
    here, there = bf16(grad2[:count]), send(bf16(grad2[count:]), PAIR)
    grad_input = jnp.where(
        yh == 0, jnp.concatenate([here, there], axis=1), jnp.concatenate([there, here], axis=1)
    )

    grads = [reduce_over_x_yl(jnp.concatenate(sums, axis=1), x, yl)]
    total = jnp.concatenate(grads, axis=1) * factor
    size = total.shape[0] // 2
    same = send(rows(total, c * size, size), OWNER_SAME)
    other = send(rows(total, (1 - c) * size, size), OWNER_OTHER)
    grad_weight = jnp.where(
        x % 2 == 0, jnp.concatenate([same, other], axis=1), jnp.concatenate([other, same], axis=1)
    )
    return forward, grad_input, grad_weight


def solution(mesh):
    fine = Mesh(mesh.devices.reshape(SIZES), AXES)
    token_spec, node_spec = P(AXES, None), P(("yh", "x"), None)
    return jax.shard_map(
        on_device,
        mesh=fine,
        in_specs=(token_spec, token_spec, node_spec, node_spec),
        out_specs=(token_spec, token_spec, token_spec),
        check_vma=False,
    )
```

```python
import jax
import jax.numpy as jnp
from jax import lax
from jax.sharding import Mesh, PartitionSpec as P

AXES = ("z", "yl", "c", "yh", "x")
SIZES = (8, 2, 2, 2, 4)
SHARES = (4, 2)


def table(move):
    pairs = []
    for z in range(8):
        for yl in range(2):
            for c in range(2):
                for yh in range(2):
                    for x in range(4):
                        pairs.append((place(z, yl, c, yh, x), place(*move(z, yl, c, yh, x))))
    return pairs


def place(z, yl, c, yh, x):
    return (((z % 8 * 2 + yl % 2) * 2 + c % 2) * 2 + yh % 2) * 4 + x % 4


def owner(z, yl, c, yh, x, message):
    return 4 * yh + (z // 2 + 1 + 2 * yh) % 4, z % 2, x // 2, x % 2, (2 * yl + c) ^ message


X_UP = table(lambda z, yl, c, yh, x: (z, yl, c, yh, x + 1))
X_DOWN = table(lambda z, yl, c, yh, x: (z, yl, c, yh, x - 1))
Z_UP = table(lambda z, yl, c, yh, x: (z + 1, yl, c, yh, x))
Z_DOWN = table(lambda z, yl, c, yh, x: (z - 1, yl, c, yh, x))
CORE = table(lambda z, yl, c, yh, x: (z, yl, c + 1, yh, x))
PAIR = table(lambda z, yl, c, yh, x: (z, yl + 1, c, yh + 1, x))
OWNERS = [
    table(lambda z, yl, c, yh, x: owner(z, yl, c, yh, x, message)) for message in range(4)
]


def send(value, pairs):
    return lax.ppermute(value, AXES, pairs)


def cols(value, start, size):
    return lax.dynamic_slice_in_dim(value, start, size, 1)


def rows(value, start, size):
    return lax.dynamic_slice_in_dim(value, start, size, 0)


def after(values, *earlier):
    return lax.optimization_barrier((values, earlier))[0]


def dequantize(level_rows, scale_rows):
    row_count, width = level_rows.shape
    blocked = level_rows.astype(jnp.float32).reshape(
        row_count, scale_rows.shape[1], width // scale_rows.shape[1]
    )
    return (blocked * scale_rows[:, :, None]).reshape(row_count, width).astype(jnp.bfloat16)


def f32(value):
    return value.astype(jnp.float32)


def bf16(value):
    return value.astype(jnp.bfloat16)


def reduce_over_z(part, z):
    size = part.shape[0] // 8
    half = size // 2

    def chunk(k):
        return rows(part, (z + k + 8) % 8 * size, size)

    far = chunk(4)
    up, down = bf16(far[:half]), bf16(far[half:])
    for step in range(4):
        up, down = send(up, Z_UP), send(down, Z_DOWN)
        near_up, near_down = chunk(3 - step), chunk(step - 3)
        if step == 0:
            up = jnp.concatenate([bf16(near_up[:half] + f32(up)), bf16(near_up[half:])])
            down = jnp.concatenate([bf16(near_down[:half]), bf16(near_down[half:] + f32(down))])
        elif step < 3:
            up, down = bf16(near_up + f32(up)), bf16(near_down + f32(down))
        else:
            return near_up + f32(up) + f32(down)


def reduce_over_x(part, x):
    size = part.shape[0] // 4
    total = rows(part, x * size, size)
    for dx in range(1, 4):
        to = table(lambda z, yl, c, yh, x: (z, yl, c, yh, x + dx))
        total = total + f32(send(bf16(rows(part, (x + dx) % 4 * size, size)), to))
    return total


def rolled(value, start):
    return cols(jnp.concatenate([value, value], axis=1), start, value.shape[1])


def on_device(tokens, cotangent, levels, scales):
    z, yl, c, yh, x = (lax.axis_index(name) for name in AXES)
    count, features = tokens.shape
    shard, outputs = levels.shape
    kh, nh = features // 2, outputs // 2
    factor = float(count * 256) ** -0.5
    widths = [nh // 6 * share for share in SHARES]
    edges = [0, widths[0], nh]

    token_out = cols(tokens, (1 - yh) * kh, kh)
    cot_out = [
        jnp.concatenate(
            [cotangent[:, h * nh + edges[j] : h * nh + edges[j + 1]] for h in range(2)], axis=1
        )
        for j in range(2)
    ]
    token_in = send(token_out, PAIR)
    cot_in = [send(cot_out[0], PAIR)]
    cot_in.append(send(after(cot_out[1], token_in), PAIR))

    levels, scales = after((levels, scales), token_out, *cot_out)
    half_scales = scales.shape[1] // 2
    own = dequantize(cols(levels, c * nh, nh), cols(scales, c * half_scales, half_scales))
    left, right = send(own, X_UP), send(own, X_DOWN)

    mine = jnp.concatenate([cols(tokens, yh * kh, kh), token_in])
    token4 = jnp.concatenate([mine, send(mine, CORE)])
    cot4 = []
    for j in range(2):
        arrived = cot_in[j] if j == 0 else after(cot_in[j], away)
        both = jnp.concatenate([cot_out[j], arrived])
        away = cols(both, (1 - c) * widths[j], widths[j])
        swapped = send(away, CORE)
        cot4.append(jnp.concatenate([cols(both, c * widths[j], widths[j]), swapped]))

    turned = rolled(token4, (1 + 2 * yh) * shard)
    grads = []
    for j in range(2):
        grads.append(
            lax.dot_general(
                turned, cot4[j], (((0,), (0,)), ((), ())), preferred_element_type=jnp.float32
            )
        )
    first = lax.psum_scatter(bf16(grads[0]), "z", scatter_dimension=0, tiled=True)
    left, right = after((left, right), grads[0])
    far = jnp.concatenate([send(left[: shard // 2], X_UP), send(right[shard // 2 :], X_DOWN)])
    far, token4 = after((far, token4), grads[1])
    second = reduce_over_z(grads[1], z)

    weight = jnp.zeros((4 * shard, nh), jnp.bfloat16)
    for k, block in ((0, own), (3, left), (1, right), (2, far)):
        weight = lax.dynamic_update_slice_in_dim(weight, block, (x + k) % 4 * shard, 0)

    out = jnp.dot(token4, weight, preferred_element_type=jnp.float32)
    away = bf16(jnp.concatenate([out[count : 2 * count], out[3 * count :]]))
    back = f32(send(away, PAIR))
    here = bf16(out[:count] + back[:count])
    there = send(bf16(out[2 * count : 3 * count] + back[count:]), CORE)
    forward = jnp.where(
        c == 0, jnp.concatenate([here, there], axis=1), jnp.concatenate([there, here], axis=1)
    )

    weight, _ = after((weight, cot4[0]), away)
    grad4 = lax.dot_general(
        jnp.concatenate(cot4, axis=1), weight, (((1,), (1,)), ((), ())), preferred_element_type=jnp.float32
    )
    grad2 = grad4[: 2 * count] + f32(send(bf16(grad4[2 * count :]), CORE))
    here, there = bf16(grad2[:count]), send(bf16(grad2[count:]), PAIR)
    grad_input = jnp.where(
        yh == 0, jnp.concatenate([here, there], axis=1), jnp.concatenate([there, here], axis=1)
    )

    total = reduce_over_x(jnp.concatenate([f32(first), second], axis=1), x) * factor
    size = total.shape[0] // 4
    got = [
        f32(send(rows(total, (2 * yl + c ^ message) * size, size), OWNERS[message]))
        for message in range(4)
    ]
    same, other = got[0] + got[2], got[1] + got[3]
    grad_weight = jnp.where(
        x % 2 == 0, jnp.concatenate([same, other], axis=1), jnp.concatenate([other, same], axis=1)
    )
    return forward, grad_input, grad_weight


def solution(mesh):
    fine = Mesh(mesh.devices.reshape(SIZES), AXES)
    token_spec, node_spec = P(AXES, None), P(("yh", "x"), None)
    return jax.shard_map(
        on_device,
        mesh=fine,
        in_specs=(token_spec, token_spec, node_spec, node_spec),
        out_specs=(token_spec, token_spec, token_spec),
        check_vma=False,
    )
```

```python
import jax
import jax.numpy as jnp
from jax import lax
from jax.experimental import pallas as pl
from jax.experimental.pallas import tpu as pltpu
from jax.sharding import Mesh, PartitionSpec as P

AXES = ("z", "yl", "c", "yh", "x")
SIZES = (8, 2, 2, 2, 4)
BLOCK_STEPS = (0, 3, 1, 2)


def table(move):
    pairs = []
    for z in range(8):
        for yl in range(2):
            for c in range(2):
                for yh in range(2):
                    for x in range(4):
                        pairs.append((place(z, yl, c, yh, x), place(*move(z, yl, c, yh, x))))
    return pairs


def place(z, yl, c, yh, x):
    return (((z % 8 * 2 + yl % 2) * 2 + c % 2) * 2 + yh % 2) * 4 + x % 4


def turn(yh, c):
    return 1 - (yh + c) % 2


def owner(z, yl, c, yh, x, message):
    z_owner = 4 * yh + 2 * c + (z // 4 + turn(yh, c)) % 2
    return z_owner, z % 4 // 2, z % 2, x // 2, x % 2 * 2 + (yl ^ message)


X_UP = table(lambda z, yl, c, yh, x: (z, yl, c, yh, x + 1))
X_DOWN = table(lambda z, yl, c, yh, x: (z, yl, c, yh, x - 1))
CORE = table(lambda z, yl, c, yh, x: (z, yl, c + 1, yh, x))
PAIR = table(lambda z, yl, c, yh, x: (z, yl + 1, c, yh + 1, x))
PAIR_CROSS = table(lambda z, yl, c, yh, x: (z, yl + 1, c + 1, yh + 1, x))
OWNERS = [
    table(lambda z, yl, c, yh, x: owner(z, yl, c, yh, x, message)) for message in range(2)
]


def send(value, pairs):
    return lax.ppermute(value, AXES, pairs)


def after(values, *earlier):
    return lax.optimization_barrier((values, earlier))[0]


def f32(value):
    return value.astype(jnp.float32)


def bf16(value):
    return value.astype(jnp.bfloat16)


def call(kernel, name, where, grid, in_specs, out_specs, out_shape, scratch, flops, operands):
    moved = sum(v.size * v.dtype.itemsize for v in operands)
    moved += sum(v.size * v.dtype.itemsize for v in jax.tree.leaves(out_shape))
    return pl.pallas_call(
        kernel,
        name=name,
        grid_spec=pltpu.PrefetchScalarGridSpec(
            num_scalar_prefetch=1,
            grid=grid,
            in_specs=in_specs,
            out_specs=out_specs,
            scratch_shapes=scratch,
        ),
        out_shape=out_shape,
        compiler_params=pltpu.CompilerParams(vmem_limit_bytes=48 * 2**20),
        cost_estimate=pl.CostEstimate(flops=flops, bytes_accessed=moved, transcendentals=0),
    )(where, *operands)


def fixed(shape, at=lambda where: (0, 0)):
    return pl.BlockSpec(shape, lambda i, where: at(where))


def dequantize_kernel(where, levels, scales, out):
    c = where[0]
    count = scales.shape[1] // 2
    width = out.shape[1] // count
    for b in range(count):
        scale = jnp.where(c == 0, scales[:, b : b + 1], scales[:, count + b : count + b + 1])
        span = slice(b * width, (b + 1) * width)
        out[:, span] = bf16(f32(levels[:, span]) * scale)


def dequantize(where, levels, scales):
    row_count, nh = levels.shape[0], levels.shape[1] // 2
    size = row_count // 3
    return call(
        dequantize_kernel,
        "dequantize",
        where,
        (3,),
        [
            pl.BlockSpec((size, nh), lambda i, where: (i, where[0])),
            pl.BlockSpec((size, scales.shape[1]), lambda i, where: (i, 0)),
        ],
        pl.BlockSpec((size, nh), lambda i, where: (i, 0)),
        jax.ShapeDtypeStruct((row_count, nh), jnp.bfloat16),
        [],
        row_count * nh,
        (levels, scales),
    )


def columns(ref, start, size):
    return ref[:, pl.ds(pl.multiple_of(start, 128), size)]


def gradient_kernel(where, own, sib, pair, psib, cot0, cot1, cot2, cot3, out, lhs):
    c, yh = where[0], where[1]
    half = lhs.shape[0] // 2
    count = own.shape[0]

    @pl.when(pl.program_id(0) == 0)
    def _():
        for r, (ref, base) in enumerate(((own, yh), (sib, yh), (pair, 0), (psib, 0))):
            for h in range(2):
                start = base * 4 * half + c * 2 * half + (h + 1 - (yh + c) % 2) % 2 * half
                block = f32(columns(ref, start, half))
                lhs[h * half : (h + 1) * half, r * count : (r + 1) * count] = bf16(block.T)

    rhs = jnp.concatenate([cot0[...], cot1[...], cot2[...], cot3[...]])
    out[...] = bf16(jnp.dot(lhs[...], rhs, preferred_element_type=jnp.float32))


def gradient(where, token_parts, cot_parts):
    count, outputs = cot_parts[0].shape
    size = token_parts[0].shape[1] // 4
    width = outputs // 6
    return call(
        gradient_kernel,
        "gradient",
        where,
        (6,),
        [fixed(v.shape) for v in token_parts]
        + [pl.BlockSpec((count, width), lambda i, where: (0, i)) for _ in cot_parts],
        pl.BlockSpec((size, width), lambda i, where: (0, i)),
        jax.ShapeDtypeStruct((size, outputs), jnp.bfloat16),
        [pltpu.VMEM((size, 4 * count), jnp.bfloat16)],
        8 * count * size * outputs,
        (*token_parts, *cot_parts),
    )


def forward_kernel(where, own, sib, pair, psib, w0, w1, w2, w3, w4, mine, other, away, cross, lhs):
    yh, x = where[1], where[2]
    count, shard = own.shape[0], w0.shape[0]

    @pl.when(pl.program_id(0) == 0)
    def _():
        for r, (ref, base) in enumerate(((own, yh), (sib, yh), (pair, 0), (psib, 0))):
            for p, step in enumerate(BLOCK_STEPS):
                start = base * 4 * shard + (x + step) % 4 * shard
                lhs[r * count : (r + 1) * count, p * shard : (p + 1) * shard] = columns(
                    ref, start, shard
                )

    far = jnp.where(pl.program_id(0) == 0, w3[...], w4[...])
    rhs = jnp.concatenate([w0[...], w1[...], w2[...], far])
    out = jnp.dot(lhs[...], rhs, preferred_element_type=jnp.float32)
    mine[...] = out[:count]
    other[...] = out[count : 2 * count]
    away[...] = bf16(out[2 * count : 3 * count])
    cross[...] = bf16(out[3 * count :])


def forward_parts(where, token_parts, blocks):
    count = token_parts[0].shape[0]
    shard, nh = blocks[0].shape
    width = nh // 2
    types = (jnp.float32, jnp.float32, jnp.bfloat16, jnp.bfloat16)
    return call(
        forward_kernel,
        "forward",
        where,
        (2,),
        [fixed(v.shape) for v in token_parts]
        + [pl.BlockSpec((shard, width), lambda i, where: (0, i))] * 3
        + [fixed((shard, width))] * 2,
        [pl.BlockSpec((count, width), lambda i, where: (0, i))] * 4,
        [jax.ShapeDtypeStruct((count, nh), kind) for kind in types],
        [pltpu.VMEM((4 * count, 4 * shard), jnp.bfloat16)],
        32 * count * shard * nh,
        (*token_parts, *blocks),
    )


def backward_kernel(where, cot0, cot1, cot2, cot3, w0, w1, w2, w3, w4, mine, give, lhs):
    x = where[2]
    i = pl.program_id(0)
    count = cot0.shape[0]
    size, half = w3.shape

    @pl.when(i == 0)
    def _():
        for r, ref in enumerate((cot0, cot2, cot1, cot3)):
            lhs[r * count : (r + 1) * count] = ref[...]

    far = jnp.concatenate([w3[...], w4[...]], axis=1)
    rhs = jnp.concatenate([w0[...], w1[...], w2[...], far])
    out = lax.dot_general(
        lhs[...], rhs, (((1,), (1,)), ((), ())), preferred_element_type=jnp.float32
    )
    for p, step in enumerate(BLOCK_STEPS):
        start = pl.multiple_of((x + step) % 4 * 3 * size + i * size, 128)
        part = out[:, p * size : (p + 1) * size]
        mine[:, pl.ds(start, size)] = part[: 2 * count]
        give[:, pl.ds(start, size)] = bf16(part[2 * count :])


def backward_parts(where, cot_parts, blocks):
    count = cot_parts[0].shape[0]
    shard, nh = blocks[0].shape
    size = shard // 3
    types = (jnp.float32, jnp.bfloat16)
    return call(
        backward_kernel,
        "backward",
        where,
        (3,),
        [fixed((count, nh), lambda where: (0, where[0])) for _ in cot_parts]
        + [pl.BlockSpec((size, nh), lambda i, where: (i, 0))] * 3
        + [pl.BlockSpec((size, nh // 2), lambda i, where: (i, 0))] * 2,
        [fixed((2 * count, 4 * shard))] * 2,
        [jax.ShapeDtypeStruct((2 * count, 4 * shard), kind) for kind in types],
        [pltpu.VMEM((4 * count, nh), jnp.bfloat16)],
        32 * count * shard * nh,
        (*cot_parts, *blocks),
    )


def rows(value, start, size):
    return lax.dynamic_slice_in_dim(value, start, size, 0)


def joined(here, there, flag):
    return jnp.where(
        flag == 0, jnp.concatenate([here, there], axis=1), jnp.concatenate([there, here], axis=1)
    )


def reduce_over_x(part, x):
    size = part.shape[0] // 4
    total = f32(rows(part, x * size, size))
    for dx in range(1, 4):
        to = table(lambda z, yl, c, yh, x: (z, yl, c, yh, x + dx))
        total = total + f32(send(rows(part, (x + dx) % 4 * size, size), to))
    return total


def on_device(tokens, cotangent, levels, scales):
    z, yl, c, yh, x = (lax.axis_index(name) for name in AXES)
    where = jnp.stack([c, yh, x]).astype(jnp.int32)
    count, features = tokens.shape
    kh = features // 2
    factor = float(count * 256) ** -0.5

    cot_pair = send(cotangent, PAIR)
    token_out = lax.dynamic_slice_in_dim(tokens, (1 - yh) * kh, kh, 1)
    token_pair = send(token_out, PAIR)

    levels, scales = after((levels, scales), token_out)
    own = dequantize(where, levels, scales)
    left, right = send(own, X_UP), send(own, X_DOWN)

    token_pair, cot_pair = after((token_pair, cot_pair), own)
    cot_sib, token_sib = send(cotangent, CORE), send(tokens, CORE)
    token_parts = (tokens, token_sib, token_pair, send(token_pair, CORE))
    cot_parts = (cotangent, cot_sib, cot_pair, send(cot_pair, CORE))

    part = gradient(where, token_parts, after(cot_parts, left, right))
    part = lax.psum_scatter(part, "z", scatter_dimension=0, tiled=True)

    half = own.shape[1] // 2
    blocks = (own, left, right, send(left[:, :half], X_UP), send(right[:, half:], X_DOWN))
    mine, other, away, cross = forward_parts(where, token_parts, blocks)
    back, back_cross, here = send(away, PAIR), send(cross, PAIR_CROSS), send(other, CORE)
    forward = joined(bf16(mine + f32(back)), bf16(here + f32(back_cross)), c)

    cot_parts = after(cot_parts, away)
    mine, give = backward_parts(where, cot_parts, blocks)
    mine = mine + f32(send(give, CORE))
    grad_input = joined(bf16(mine[:count]), send(bf16(mine[count:]), PAIR), yh)

    total = reduce_over_x(part, x) * factor
    size = total.shape[0] // 2
    got = [send(rows(total, (yl ^ m) * size, size), OWNERS[m]) for m in range(2)]
    return forward, grad_input, got[0] + got[1]


def solution(mesh):
    fine = Mesh(mesh.devices.reshape(SIZES), AXES)
    token_spec, node_spec = P(AXES, None), P(("yh", "x"), None)
    return jax.shard_map(
        on_device,
        mesh=fine,
        in_specs=(token_spec, token_spec, node_spec, node_spec),
        out_specs=(token_spec, token_spec, token_spec),
        check_vma=False,
    )
```

```python
import jax
import jax.numpy as jnp
from jax import lax
from jax.experimental import pallas as pl
from jax.experimental.pallas import tpu as pltpu
from jax.sharding import Mesh, PartitionSpec as P

AXES = ("z", "yl", "c", "yh", "x")
SIZES = (8, 2, 2, 2, 4)
BLOCK_STEPS = (0, 3, 1, 2)


def table(move):
    pairs = []
    for z in range(8):
        for yl in range(2):
            for c in range(2):
                for yh in range(2):
                    for x in range(4):
                        pairs.append((place(z, yl, c, yh, x), place(*move(z, yl, c, yh, x))))
    return pairs


def place(z, yl, c, yh, x):
    return (((z % 8 * 2 + yl % 2) * 2 + c % 2) * 2 + yh % 2) * 4 + x % 4


def window(z, c, yh):
    return (z + 11 - 4 * yh - 2 * c) % 8


def owner(z, yl, c, yh, x, message):
    chunk = window(z, c, yh)
    return 4 * yh + 2 * c + chunk // 4, chunk % 4 // 2, chunk % 2, x // 2, x % 2 * 2 + (yl ^ message)


X_UP = table(lambda z, yl, c, yh, x: (z, yl, c, yh, x + 1))
X_DOWN = table(lambda z, yl, c, yh, x: (z, yl, c, yh, x - 1))
Z_UP = table(lambda z, yl, c, yh, x: (z + 1, yl, c, yh, x))
Z_DOWN = table(lambda z, yl, c, yh, x: (z - 1, yl, c, yh, x))
CORE = table(lambda z, yl, c, yh, x: (z, yl, c + 1, yh, x))
PAIR = table(lambda z, yl, c, yh, x: (z, yl + 1, c, yh + 1, x))
OWNERS = [
    table(lambda z, yl, c, yh, x: owner(z, yl, c, yh, x, message)) for message in range(2)
]


def send(value, pairs):
    return lax.ppermute(value, AXES, pairs)


def after(values, *earlier):
    return lax.optimization_barrier((values, earlier))[0]


def f32(value):
    return value.astype(jnp.float32)


def bf16(value):
    return value.astype(jnp.bfloat16)


def call(kernel, name, mib, where, grid, in_specs, out_specs, out_shape, scratch, flops, operands):
    moved = sum(v.size * v.dtype.itemsize for v in operands)
    moved += sum(v.size * v.dtype.itemsize for v in jax.tree.leaves(out_shape))
    return pl.pallas_call(
        kernel,
        name=name,
        grid_spec=pltpu.PrefetchScalarGridSpec(
            num_scalar_prefetch=1,
            grid=grid,
            in_specs=in_specs,
            out_specs=out_specs,
            scratch_shapes=scratch,
        ),
        out_shape=out_shape,
        compiler_params=pltpu.CompilerParams(vmem_limit_bytes=mib * 2**20),
        cost_estimate=pl.CostEstimate(flops=flops, bytes_accessed=moved, transcendentals=0),
    )(where, *operands)


def fixed(shape, at=lambda where: (0, 0)):
    return pl.BlockSpec(shape, lambda i, where: at(where))


def dequantize_kernel(where, levels, scales, out):
    c = where[0]
    count = scales.shape[1] // 2
    width = out.shape[1] // count
    for b in range(count):
        scale = jnp.where(c == 0, scales[:, b : b + 1], scales[:, count + b : count + b + 1])
        span = slice(b * width, (b + 1) * width)
        out[:, span] = bf16(f32(levels[:, span]) * scale)


def dequantize(where, levels, scales):
    row_count, nh = levels.shape[0], levels.shape[1] // 2
    size = row_count // 3
    return call(
        dequantize_kernel,
        "dequantize",
        12,
        where,
        (3,),
        [
            pl.BlockSpec((size, nh), lambda i, where: (i, where[0])),
            pl.BlockSpec((size, scales.shape[1]), lambda i, where: (i, 0)),
        ],
        pl.BlockSpec((size, nh), lambda i, where: (i, 0)),
        jax.ShapeDtypeStruct((row_count, nh), jnp.bfloat16),
        [],
        row_count * nh,
        (levels, scales),
    )


def columns(ref, start, size):
    return ref[:, pl.ds(pl.multiple_of(start, 128), size)]


def gradient_kernel(where, own, sib, pair, psib, cot0, cot1, cot2, cot3, out, up, down, lhs):
    c, yh = where[0], where[1]
    count, size = own.shape[0], lhs.shape[1]

    @pl.when(pl.program_id(0) == 0)
    def _():
        for r, (ref, base) in enumerate(((own, yh), (sib, yh), (pair, 0), (psib, 0))):
            start = base * 2 * size + c * size
            lhs[r * count : (r + 1) * count] = columns(ref, start, size)

    rhs = jnp.concatenate([cot0[...], cot1[...], cot2[...], cot3[...]])
    out[...] = bf16(
        lax.dot_general(
            lhs[...], rhs, (((0,), (0,)), ((), ())), preferred_element_type=jnp.float32
        )
    )
    half = up.shape[0]
    start = pl.multiple_of((where[3] + 4) % 8 * (2 * half), 2 * half)
    up[...] = out[pl.ds(start, half)]
    down[...] = out[pl.ds(start + half, half)]


def gradient(where, token_parts, cot_parts, j):
    count, outputs = cot_parts[0].shape
    size = token_parts[0].shape[1] // 4
    width = outputs // 4
    heights = (size, size // 16, size // 16)
    return call(
        gradient_kernel,
        "gradient",
        24,
        where,
        (2,),
        [fixed(v.shape) for v in token_parts]
        + [pl.BlockSpec((count, width), lambda i, where: (0, 2 * j + i)) for _ in cot_parts],
        [pl.BlockSpec((height, width), lambda i, where: (0, i)) for height in heights],
        [jax.ShapeDtypeStruct((height, 2 * width), jnp.bfloat16) for height in heights],
        [pltpu.VMEM((4 * count, size), jnp.bfloat16)],
        4 * count * size * outputs,
        (*token_parts, *cot_parts),
    )


def hop_kernel(where, up, down, near_up, near_down, *outs):
    half = near_up.shape[0] // 2
    if up.shape[0] == half:
        outs[0][:half] = bf16(f32(near_up[:half]) + f32(up[...]))
        outs[0][half:] = near_up[half:]
        outs[1][:half] = near_down[:half]
        outs[1][half:] = bf16(f32(near_down[half:]) + f32(down[...]))
    elif len(outs) == 2:
        outs[0][...] = bf16(f32(near_up[...]) + f32(up[...]))
        outs[1][...] = bf16(f32(near_down[...]) + f32(down[...]))
    else:
        outs[0][...] = f32(near_up[...]) + f32(up[...]) + f32(down[...])


def hop(where, step, up, down, part):
    size, width = part.shape[0] // 8, part.shape[1]
    kinds = [jnp.float32] if step == 3 else [jnp.bfloat16] * 2
    return call(
        hop_kernel,
        "hop",
        8,
        where,
        (1,),
        [fixed(up.shape), fixed(down.shape)]
        + [
            fixed((size, width), lambda where, k=k: ((where[3] + 8 + k) % 8, 0))
            for k in (3 - step, step - 3)
        ],
        [fixed((size, width)) for _ in kinds],
        [jax.ShapeDtypeStruct((size, width), kind) for kind in kinds],
        [],
        2 * size * width,
        (up, down, part, part),
    )


def forward_kernel(where, own, sib, pair, psib, w0, w1, w2, w3, w4, mine, other, away, lhs):
    yh, x = where[1], where[2]
    count, shard = own.shape[0], w0.shape[0]

    @pl.when(pl.program_id(0) == 0)
    def _():
        for r, (ref, base) in enumerate(((own, yh), (sib, yh), (pair, 0), (psib, 0))):
            for p, step in enumerate(BLOCK_STEPS):
                start = base * 4 * shard + (x + step) % 4 * shard
                lhs[r * count : (r + 1) * count, p * shard : (p + 1) * shard] = columns(
                    ref, start, shard
                )

    far = jnp.where(pl.program_id(0) == 0, w3[...], w4[...])
    rhs = jnp.concatenate([w0[...], w1[...], w2[...], far])
    out = jnp.dot(lhs[...], rhs, preferred_element_type=jnp.float32)
    mine[...] = out[:count]
    other[...] = out[count : 2 * count]
    away[...] = bf16(out[2 * count :])


def forward_parts(where, token_parts, blocks):
    count = token_parts[0].shape[0]
    shard, nh = blocks[0].shape
    width = nh // 2
    kinds = ((count, jnp.float32), (count, jnp.float32), (2 * count, jnp.bfloat16))
    return call(
        forward_kernel,
        "forward",
        28,
        where,
        (2,),
        [fixed(v.shape) for v in token_parts]
        + [pl.BlockSpec((shard, width), lambda i, where: (0, i))] * 3
        + [fixed((shard, width))] * 2,
        [pl.BlockSpec((height, width), lambda i, where: (0, i)) for height, _ in kinds],
        [jax.ShapeDtypeStruct((height, nh), kind) for height, kind in kinds],
        [pltpu.VMEM((4 * count, 4 * shard), jnp.bfloat16)],
        32 * count * shard * nh,
        (*token_parts, *blocks),
    )


def backward_kernel(where, cot0, cot1, cot2, cot3, w0, w1, w2, w3, w4, mine, give, lhs):
    x = where[2]
    i = pl.program_id(0)
    count = cot0.shape[0]
    size, half = w3.shape

    @pl.when(i == 0)
    def _():
        for r, ref in enumerate((cot0, cot2, cot1, cot3)):
            lhs[r * count : (r + 1) * count] = ref[...]

    far = jnp.concatenate([w3[...], w4[...]], axis=1)
    rhs = jnp.concatenate([w0[...], w1[...], w2[...], far])
    out = lax.dot_general(
        lhs[...], rhs, (((1,), (1,)), ((), ())), preferred_element_type=jnp.float32
    )
    for p, step in enumerate(BLOCK_STEPS):
        start = pl.multiple_of((x + step) % 4 * 3 * size + i * size, 128)
        part = out[:, p * size : (p + 1) * size]
        mine[:, pl.ds(start, size)] = part[: 2 * count]
        give[:, pl.ds(start, size)] = bf16(part[2 * count :])


def backward_parts(where, cot_parts, blocks):
    count = cot_parts[0].shape[0]
    shard, nh = blocks[0].shape
    size = shard // 3
    types = (jnp.float32, jnp.bfloat16)
    return call(
        backward_kernel,
        "backward",
        28,
        where,
        (3,),
        [fixed((count, nh), lambda where: (0, where[0])) for _ in cot_parts]
        + [pl.BlockSpec((size, nh), lambda i, where: (i, 0))] * 3
        + [pl.BlockSpec((size, nh // 2), lambda i, where: (i, 0))] * 2,
        [fixed((2 * count, 4 * shard))] * 2,
        [jax.ShapeDtypeStruct((2 * count, 4 * shard), kind) for kind in types],
        [pltpu.VMEM((4 * count, nh), jnp.bfloat16)],
        32 * count * shard * nh,
        (*cot_parts, *blocks),
    )


def rows(value, start, size):
    return lax.dynamic_slice_in_dim(value, start, size, 0)


def joined(here, there, flag):
    return jnp.where(
        flag == 0, jnp.concatenate([here, there], axis=1), jnp.concatenate([there, here], axis=1)
    )


def reduce_over_x(part, x):
    size = part.shape[0] // 4
    total = rows(part, x * size, size)
    for dx in range(1, 4):
        to = table(lambda z, yl, c, yh, x: (z, yl, c, yh, x + dx))
        total = total + f32(send(bf16(rows(part, (x + dx) % 4 * size, size)), to))
    return total


def on_device(tokens, cotangent, levels, scales):
    z, yl, c, yh, x = (lax.axis_index(name) for name in AXES)
    where = jnp.stack([c, yh, x, window(z, c, yh)]).astype(jnp.int32)
    count, features = tokens.shape
    kh = features // 2
    factor = float(count * 256) ** -0.5

    cot_pair = send(cotangent, PAIR)
    own = dequantize(where, levels, scales)
    left, right = send(own, X_UP), send(own, X_DOWN)
    token_out = lax.dynamic_slice_in_dim(after(tokens, own), (1 - yh) * kh, kh, 1)
    token_pair = send(token_out, PAIR)

    cot_own, token_own = after((cotangent, tokens), token_out)
    cot_sib, token_sib = send(cot_own, CORE), send(token_own, CORE)
    token_parts = (tokens, token_sib, token_pair, send(token_pair, CORE))
    cot_parts = (cotangent, cot_sib, cot_pair, send(cot_pair, CORE))

    half = own.shape[1] // 2
    far_left, far_right = left[:, :half], right[:, half:]
    cot_ready = after(cot_parts, left, right, far_left, far_right)
    chains = []
    for j in range(2):
        chains.append(gradient(where, token_parts, cot_ready, j))
        cot_ready = after(cot_ready, chains[-1])
    blocks = (own, left, right, send(far_left, X_UP), send(far_right, X_DOWN))
    for step in range(4):
        if step == 2:
            mine, other, away = forward_parts(where, token_parts, after(blocks, chains))
            back = f32(send(away, PAIR))
            held = after([chain[0] for chain in chains], away)
        if step == 3:
            part, give = backward_parts(where, cot_parts, after(blocks, chains))
            give = send(give, CORE)
            held = after([chain[0] for chain in chains], part)
            held[1] = after(held[1], back, give)
        for j in range(2):
            grad, up, down = chains[j]
            grad = held[j] if step >= 2 else grad
            got = hop(where, step, send(up, Z_UP), send(down, Z_DOWN), grad)
            chains[j] = (grad, *got)
    sums = [chain[1] for chain in chains]

    part = part + f32(give)
    grad_input = joined(bf16(part[:count]), send(bf16(part[count:]), PAIR), yh)
    there = send(bf16(other + back[count:]), CORE)
    forward = joined(bf16(mine + back[:count]), there, c)

    total = bf16(reduce_over_x(jnp.concatenate(sums, axis=1), x) * factor)
    size = total.shape[0] // 2
    got = [f32(send(rows(total, (yl ^ m) * size, size), OWNERS[m])) for m in range(2)]
    return forward, grad_input, got[0] + got[1]


def solution(mesh):
    fine = Mesh(mesh.devices.reshape(SIZES), AXES)
    token_spec, node_spec = P(AXES, None), P(("yh", "x"), None)
    return jax.shard_map(
        on_device,
        mesh=fine,
        in_specs=(token_spec, token_spec, node_spec, node_spec),
        out_specs=(token_spec, token_spec, token_spec),
        check_vma=False,
    )
```

```python
import functools

import jax
import jax.numpy as jnp
from jax import lax
from jax.experimental import pallas as pl
from jax.experimental.pallas import tpu as pltpu
from jax.sharding import Mesh, PartitionSpec as P

AXES = ("z", "yl", "c", "yh", "x")
SIZES = (8, 2, 2, 2, 4)
BLOCK_STEPS = (0, 3, 1, 2)


def table(move):
    pairs = []
    for z in range(8):
        for yl in range(2):
            for c in range(2):
                for yh in range(2):
                    for x in range(4):
                        pairs.append((place(z, yl, c, yh, x), place(*move(z, yl, c, yh, x))))
    return pairs


def place(z, yl, c, yh, x):
    return (((z % 8 * 2 + yl % 2) * 2 + c % 2) * 2 + yh % 2) * 4 + x % 4


def window(z, c, yh):
    return (z + 11 - 4 * yh - 2 * c) % 8


def owner(z, yl, c, yh, x, message):
    chunk = window(z, c, yh)
    return 4 * yh + 2 * c + chunk // 4, chunk % 4 // 2, chunk % 2, x // 2, x % 2 * 2 + (yl ^ message)


X_UP = table(lambda z, yl, c, yh, x: (z, yl, c, yh, x + 1))
X_DOWN = table(lambda z, yl, c, yh, x: (z, yl, c, yh, x - 1))
Z_UP = table(lambda z, yl, c, yh, x: (z + 1, yl, c, yh, x))
Z_DOWN = table(lambda z, yl, c, yh, x: (z - 1, yl, c, yh, x))
CORE = table(lambda z, yl, c, yh, x: (z, yl, c + 1, yh, x))
PAIR = table(lambda z, yl, c, yh, x: (z, yl + 1, c, yh + 1, x))
OWNERS = [
    table(lambda z, yl, c, yh, x: owner(z, yl, c, yh, x, message)) for message in range(2)
]


def send(value, pairs):
    return lax.ppermute(value, AXES, pairs)


def after(values, *earlier):
    return lax.optimization_barrier((values, earlier))[0]


def f32(value):
    return value.astype(jnp.float32)


def bf16(value):
    return value.astype(jnp.bfloat16)


def call(kernel, name, mib, where, grid, in_specs, out_specs, out_shape, scratch, flops, operands):
    moved = sum(v.size * v.dtype.itemsize for v in operands)
    moved += sum(v.size * v.dtype.itemsize for v in jax.tree.leaves(out_shape))
    return pl.pallas_call(
        kernel,
        name=name,
        grid_spec=pltpu.PrefetchScalarGridSpec(
            num_scalar_prefetch=1,
            grid=grid,
            in_specs=in_specs,
            out_specs=out_specs,
            scratch_shapes=scratch,
        ),
        out_shape=out_shape,
        compiler_params=pltpu.CompilerParams(vmem_limit_bytes=mib * 2**20),
        cost_estimate=pl.CostEstimate(flops=flops, bytes_accessed=moved, transcendentals=0),
    )(where, *operands)


def fixed(shape, at=lambda where: (0, 0)):
    return pl.BlockSpec(shape, lambda i, where: at(where))


def dequantize_kernel(where, levels, scales, out):
    c = where[0]
    count = scales.shape[1] // 2
    width = out.shape[1] // count
    for b in range(count):
        scale = jnp.where(c == 0, scales[:, b : b + 1], scales[:, count + b : count + b + 1])
        span = slice(b * width, (b + 1) * width)
        out[:, span] = bf16(f32(levels[:, span]) * scale)


def dequantize(where, levels, scales):
    row_count, nh = levels.shape[0], levels.shape[1] // 2
    size = row_count // 3
    return call(
        dequantize_kernel,
        "dequantize",
        60,
        where,
        (3,),
        [
            pl.BlockSpec((size, nh), lambda i, where: (i, where[0])),
            pl.BlockSpec((size, scales.shape[1]), lambda i, where: (i, 0)),
        ],
        pl.BlockSpec((size, nh), lambda i, where: (i, 0)),
        jax.ShapeDtypeStruct((row_count, nh), jnp.bfloat16),
        [],
        row_count * nh,
        (levels, scales),
    )


def pack_kernel(where, tokens, cotangent, out):
    kh = tokens.shape[1]
    out[:, :kh] = tokens[...]
    out[:, kh:] = cotangent[...]


def pack(where, tokens, cotangent):
    count, kh = tokens.shape[0], tokens.shape[1] // 2
    width = kh + cotangent.shape[1]
    return call(
        pack_kernel,
        "pack",
        60,
        where,
        (1,),
        [fixed((count, kh), lambda where: (0, 1 - where[1])), fixed(cotangent.shape)],
        fixed((count, width)),
        jax.ShapeDtypeStruct((count, width), jnp.bfloat16),
        [],
        0,
        (tokens, cotangent),
    )


def columns(ref, start, size):
    return ref[:, pl.ds(pl.multiple_of(start, 128), size)]


def gradient_kernel(where, own, sib, pair, psib, cot0, cot1, cot2, cot3, out, up, down, lhs):
    c, yh = where[0], where[1]
    count, size = own.shape[0], lhs.shape[1]

    @pl.when(pl.program_id(0) == 0)
    def _():
        for r, (ref, base) in enumerate(((own, yh), (sib, yh), (pair, 0), (psib, 0))):
            start = base * 2 * size + c * size
            lhs[r * count : (r + 1) * count] = columns(ref, start, size)

    rhs = jnp.concatenate([cot0[...], cot1[...], cot2[...], cot3[...]])
    out[...] = bf16(
        lax.dot_general(
            lhs[...], rhs, (((0,), (0,)), ((), ())), preferred_element_type=jnp.float32
        )
    )
    half = up.shape[0]
    start = pl.multiple_of((where[3] + 4) % 8 * (2 * half), 2 * half)
    up[...] = out[pl.ds(start, half)]
    down[...] = out[pl.ds(start + half, half)]


def gradient(where, token_parts, cot_parts):
    count, outputs = cot_parts[0].shape
    kh = token_parts[0].shape[1] // 2
    size, width = kh // 2, outputs // 4
    heights = (size, size // 16, size // 16)
    return call(
        gradient_kernel,
        "gradient",
        24,
        where,
        (4,),
        [fixed(v.shape) for v in token_parts[:2]]
        + [fixed((count, kh))] * 2
        + [pl.BlockSpec((count, width), lambda i, where: (0, i))] * 2
        + [pl.BlockSpec((count, width), lambda i, where: (0, i + 2))] * 2,
        [pl.BlockSpec((height, width), lambda i, where: (0, i)) for height in heights],
        [jax.ShapeDtypeStruct((height, outputs), jnp.bfloat16) for height in heights],
        [pltpu.VMEM((4 * count, size), jnp.bfloat16)],
        8 * count * size * outputs,
        (*token_parts, *cot_parts),
    )


def hop_kernel(where, *refs):
    *arrived, near, out = refs
    total = f32(near[...])
    for ref in arrived:
        total = total + f32(ref[...])
    out[...] = total.astype(out.dtype)


def first_hop_kernel(where, arrived, near, out, *, upper):
    half = arrived.shape[0]
    here, there = (slice(0, half), slice(half, 2 * half))[:: 1 if upper else -1]
    out[here] = bf16(f32(near[here]) + f32(arrived[...]))
    out[there] = near[there]


def hop(where, part, k, kernel, kind, *arrived):
    size, width = part.shape[0] // 8, part.shape[1]
    return call(
        kernel,
        "hop",
        8,
        where,
        (1,),
        [fixed(v.shape) for v in arrived]
        + [fixed((size, width), lambda where: ((where[3] + 8 + k) % 8, 0))],
        fixed((size, width)),
        jax.ShapeDtypeStruct((size, width), kind),
        [],
        2 * size * width,
        (*arrived, part),
    )


def forward_kernel(where, own, sib, pair, psib, w0, w1, w2, w3, w4, mine, other, away, lhs):
    yh, x = where[1], where[2]
    count, shard = own.shape[0], w0.shape[0]

    @pl.when(pl.program_id(0) == 0)
    def _():
        for r, (ref, base) in enumerate(((own, yh), (sib, yh), (pair, 0), (psib, 0))):
            for p, step in enumerate(BLOCK_STEPS):
                start = base * 4 * shard + (x + step) % 4 * shard
                lhs[r * count : (r + 1) * count, p * shard : (p + 1) * shard] = columns(
                    ref, start, shard
                )

    far = jnp.where(pl.program_id(0) == 0, w3[...], w4[...])
    rhs = jnp.concatenate([w0[...], w1[...], w2[...], far])
    out = jnp.dot(lhs[...], rhs, preferred_element_type=jnp.float32)
    mine[...] = out[:count]
    other[...] = out[count : 2 * count]
    away[...] = bf16(out[2 * count :])


def forward_parts(where, token_parts, blocks):
    count = token_parts[0].shape[0]
    shard, nh = blocks[0].shape
    width = nh // 2
    kinds = ((count, jnp.float32), (count, jnp.float32), (2 * count, jnp.bfloat16))
    return call(
        forward_kernel,
        "forward",
        28,
        where,
        (2,),
        [fixed(v.shape) for v in token_parts[:2]]
        + [fixed((count, 4 * shard))] * 2
        + [pl.BlockSpec((shard, width), lambda i, where: (0, i))] * 3
        + [fixed((shard, width))] * 2,
        [pl.BlockSpec((height, width), lambda i, where: (0, i)) for height, _ in kinds],
        [jax.ShapeDtypeStruct((height, nh), kind) for height, kind in kinds],
        [pltpu.VMEM((4 * count, 4 * shard), jnp.bfloat16)],
        32 * count * shard * nh,
        (*token_parts, *blocks),
    )


def backward_kernel(where, cot0, cot1, cot2, cot3, w0, w1, w2, w3, w4, mine, give, lhs):
    x = where[2]
    i = pl.program_id(0)
    count = cot0.shape[0]
    size, half = w3.shape

    @pl.when(i == 0)
    def _():
        for r, ref in enumerate((cot0, cot2, cot1, cot3)):
            lhs[r * count : (r + 1) * count] = ref[...]

    far = jnp.concatenate([w3[...], w4[...]], axis=1)
    rhs = jnp.concatenate([w0[...], w1[...], w2[...], far])
    out = lax.dot_general(
        lhs[...], rhs, (((1,), (1,)), ((), ())), preferred_element_type=jnp.float32
    )
    for p, step in enumerate(BLOCK_STEPS):
        start = pl.multiple_of((x + step) % 4 * 3 * size + i * size, 128)
        part = out[:, p * size : (p + 1) * size]
        mine[:, pl.ds(start, size)] = part[: 2 * count]
        give[:, pl.ds(start, size)] = bf16(part[2 * count :])


def backward_parts(where, cot_parts, blocks):
    count = cot_parts[0].shape[0]
    shard, nh = blocks[0].shape
    size = shard // 3
    types = (jnp.float32, jnp.bfloat16)
    return call(
        backward_kernel,
        "backward",
        28,
        where,
        (3,),
        [fixed((count, nh), lambda where: (0, where[0]))] * 2
        + [fixed((count, nh), lambda where: (0, 1 + where[0]))] * 2
        + [pl.BlockSpec((size, nh), lambda i, where: (i, 0))] * 3
        + [pl.BlockSpec((size, nh // 2), lambda i, where: (i, 0))] * 2,
        [fixed((2 * count, 4 * shard))] * 2,
        [jax.ShapeDtypeStruct((2 * count, 4 * shard), kind) for kind in types],
        [pltpu.VMEM((4 * count, nh), jnp.bfloat16)],
        32 * count * shard * nh,
        (*cot_parts, *blocks),
    )


def rows(value, start, size):
    return lax.dynamic_slice_in_dim(value, start, size, 0)


def joined(here, there, flag):
    return jnp.where(
        flag == 0, jnp.concatenate([here, there], axis=1), jnp.concatenate([there, here], axis=1)
    )


def reduce_over_x(part, x):
    size = part.shape[0] // 4
    total = rows(part, x * size, size)
    for dx in range(1, 4):
        to = table(lambda z, yl, c, yh, x: (z, yl, c, yh, x + dx))
        total = total + f32(send(bf16(rows(part, (x + dx) % 4 * size, size)), to))
    return total


def on_device(tokens, cotangent, levels, scales):
    z, yl, c, yh, x = (lax.axis_index(name) for name in AXES)
    where = jnp.stack([c, yh, x, window(z, c, yh)]).astype(jnp.int32)
    count = tokens.shape[0]
    factor = float(count * 256) ** -0.5

    packed = pack(where, tokens, cotangent)
    pair = send(packed, PAIR)

    levels, scales = after((levels, scales), packed)
    own = dequantize(where, levels, scales)
    left, right = send(own, X_UP), send(own, X_DOWN)

    cot_own, token_own = after((cotangent, tokens), own)
    cot_sib, token_sib = send(cot_own, CORE), send(token_own, CORE)
    cross = send(pair, CORE)
    token_parts = (tokens, token_sib, pair, cross)
    cot_parts = (cotangent, cot_sib, pair, cross)

    grad, up, down = gradient(where, token_parts, cot_parts)
    half = own.shape[1] // 2
    far_left, far_right = left[:, :half], right[:, half:]
    blocks = (own, left, right, send(far_left, X_UP), send(far_right, X_DOWN))
    up, down = send(up, Z_UP), send(down, Z_DOWN)
    up = hop(where, grad, 3, functools.partial(first_hop_kernel, upper=True), jnp.bfloat16, up)
    down = hop(where, grad, -3, functools.partial(first_hop_kernel, upper=False), jnp.bfloat16, down)
    mine, other, away = forward_parts(where, token_parts, after(blocks, up, down))
    up, down = send(up, Z_UP), send(down, Z_DOWN)
    back = f32(send(away, PAIR))
    grad = after(grad, away)
    up = hop(where, grad, 2, hop_kernel, jnp.bfloat16, up)
    down = hop(where, grad, -2, hop_kernel, jnp.bfloat16, down)
    part, give = backward_parts(where, cot_parts, after(blocks, up, down))
    up, down = send(up, Z_UP), send(down, Z_DOWN)
    give = send(give, CORE)
    grad = after(grad, give, back)
    up = hop(where, grad, 1, hop_kernel, jnp.bfloat16, up)
    down = hop(where, grad, -1, hop_kernel, jnp.bfloat16, down)
    up, down = send(up, Z_UP), send(down, Z_DOWN)
    total = hop(where, grad, 0, hop_kernel, jnp.float32, up, down)

    part = part + f32(give)
    grad_input = joined(bf16(part[:count]), send(bf16(part[count:]), PAIR), yh)
    there = send(bf16(other + back[count:]), CORE)
    forward = joined(bf16(mine + back[:count]), there, c)

    total = bf16(reduce_over_x(after(total, forward, part), x) * factor)
    size = total.shape[0] // 2
    got = [f32(send(rows(total, (yl ^ m) * size, size), OWNERS[m])) for m in range(2)]
    got, grad_input = after((got, grad_input))
    return forward, grad_input, got[0] + got[1]


def solution(mesh):
    fine = Mesh(mesh.devices.reshape(SIZES), AXES)
    token_spec, node_spec = P(AXES, None), P(("yh", "x"), None)
    return jax.shard_map(
        on_device,
        mesh=fine,
        in_specs=(token_spec, token_spec, node_spec, node_spec),
        out_specs=(token_spec, token_spec, token_spec),
        check_vma=False,
    )
```

```python
import functools
import math

import jax
import jax.numpy as jnp
from jax import lax
from jax.experimental import pallas as pl
from jax.experimental.pallas import tpu as pltpu
from jax.sharding import Mesh, PartitionSpec as P

AXES = ("z", "yl", "c", "yh", "x")
SIZES = (8, 2, 2, 2, 4)
BLOCK_STEPS = (0, 3, 1, 2)
HOPS = (3, -3, 2, -2, 1, -1, 0)


def table(move):
    pairs = []
    for z in range(8):
        for yl in range(2):
            for c in range(2):
                for yh in range(2):
                    for x in range(4):
                        pairs.append((place(z, yl, c, yh, x), place(*move(z, yl, c, yh, x))))
    return pairs


def place(z, yl, c, yh, x):
    return (((z % 8 * 2 + yl % 2) * 2 + c % 2) * 2 + yh % 2) * 4 + x % 4


def window(z, c, yh):
    return (z + 11 - 4 * yh - 2 * c) % 8


def owner(z, yl, c, yh, x, message):
    chunk = window(z, c, yh)
    return 4 * yh + 2 * c + chunk // 4, chunk % 4 // 2, chunk % 2, x // 2, x % 2 * 2 + (yl ^ message)


X_UP = table(lambda z, yl, c, yh, x: (z, yl, c, yh, x + 1))
X_DOWN = table(lambda z, yl, c, yh, x: (z, yl, c, yh, x - 1))
Z_UP = table(lambda z, yl, c, yh, x: (z + 1, yl, c, yh, x))
Z_DOWN = table(lambda z, yl, c, yh, x: (z - 1, yl, c, yh, x))
CORE = table(lambda z, yl, c, yh, x: (z, yl, c + 1, yh, x))
PAIR = table(lambda z, yl, c, yh, x: (z, yl + 1, c, yh + 1, x))
OWNERS = [
    table(lambda z, yl, c, yh, x: owner(z, yl, c, yh, x, message)) for message in range(2)
]


def send(value, pairs):
    return lax.ppermute(value, AXES, pairs)


def after(values, *earlier):
    return lax.optimization_barrier((values, earlier))[0]


def f32(value):
    return value.astype(jnp.float32)


def bf16(value):
    return value.astype(jnp.bfloat16)


def call(kernel, name, mib, where, grid, in_specs, out_specs, out_shape, scratch, flops, operands):
    moved = sum(v.size * v.dtype.itemsize for v in operands)
    moved += sum(math.prod(v.shape) * v.dtype.itemsize for v in jax.tree.leaves(out_shape))
    return pl.pallas_call(
        kernel,
        name=name,
        grid_spec=pltpu.PrefetchScalarGridSpec(
            num_scalar_prefetch=1,
            grid=grid,
            in_specs=in_specs,
            out_specs=out_specs,
            scratch_shapes=scratch,
        ),
        out_shape=out_shape,
        compiler_params=pltpu.CompilerParams(vmem_limit_bytes=mib * 2**20),
        cost_estimate=pl.CostEstimate(flops=flops, bytes_accessed=moved, transcendentals=0),
    )(where, *operands)


def fixed(shape, at=lambda where: (0, 0)):
    return pl.BlockSpec(shape, lambda i, where: at(where))


def dequantize_kernel(where, levels, scales, out):
    count = scales.shape[0] // 2
    width = out.shape[1] // count
    mine = jnp.where(where[0] == 0, scales[:count], scales[count:]).T
    for b in range(count):
        scale = mine[:, b : b + 1]
        span = slice(b * width, (b + 1) * width)
        out[:, span] = bf16(f32(levels[:, span]) * scale)


def dequantize(where, levels, scales):
    row_count, nh = levels.shape[0], levels.shape[1] // 2
    size = row_count // 3
    return call(
        dequantize_kernel,
        "dequantize",
        60,
        where,
        (3,),
        [
            pl.BlockSpec((size, nh), lambda i, where: (i, where[0])),
            pl.BlockSpec((scales.shape[0], size), lambda i, where: (0, i)),
        ],
        pl.BlockSpec((size, nh), lambda i, where: (i, 0)),
        jax.ShapeDtypeStruct((row_count, nh), jnp.bfloat16),
        [],
        row_count * nh,
        (levels, scales),
    )


def pack_kernel(tokens, cotangent, out, sems):
    kh = tokens.shape[1] // 2
    start = pl.multiple_of((1 - lax.axis_index("yh")) * kh, 128)
    copies = (
        pltpu.make_async_copy(tokens.at[:, pl.ds(start, kh)], out.at[:, pl.ds(0, kh)], sems.at[0]),
        pltpu.make_async_copy(cotangent, out.at[:, pl.ds(kh, cotangent.shape[1])], sems.at[1]),
    )
    for copy in copies:
        copy.start()
    for copy in copies:
        copy.wait()


def pack(tokens, cotangent):
    shape = (tokens.shape[0], tokens.shape[1] // 2 + cotangent.shape[1])
    return pl.pallas_call(
        pack_kernel,
        name="pack",
        in_specs=[pl.BlockSpec(memory_space=pl.ANY)] * 2,
        out_specs=pl.BlockSpec(memory_space=pl.ANY),
        out_shape=jax.ShapeDtypeStruct(shape, jnp.bfloat16),
        scratch_shapes=[pltpu.SemaphoreType.DMA((2,))],
        compiler_params=pltpu.CompilerParams(vmem_limit_bytes=60 * 2**20),
    )(tokens, cotangent)


def columns(ref, start, size):
    return ref[:, pl.ds(pl.multiple_of(start, 128), size)]


def gradient_kernel(where, own, sib, pair, psib, cot0, cot1, cot2, cot3, *refs):
    c, yh = where[0], where[1]
    *chunks, lhs, out = refs
    count, size = own.shape[0], lhs.shape[1]

    @pl.when(pl.program_id(0) == 0)
    def _():
        for r, (ref, base) in enumerate(((own, yh), (sib, yh), (pair, 0), (psib, 0))):
            start = base * 2 * size + c * size
            lhs[r * count : (r + 1) * count] = columns(ref, start, size)

    rhs = jnp.concatenate([cot0[...], cot1[...], cot2[...], cot3[...]])
    out[...] = bf16(
        lax.dot_general(
            lhs[...], rhs, (((0,), (0,)), ((), ())), preferred_element_type=jnp.float32
        )
    )
    height, start = size // 8, 0
    for k, ref in zip((4, 4, *HOPS), chunks):
        part = ref.shape[0]
        row = (where[3] + 8 + k) % 8 * height + start
        ref[...] = out[pl.ds(pl.multiple_of(row, 16), part)]
        start = (start + part) % height


def gradient(where, token_parts, cot_parts):
    count, outputs = cot_parts[0].shape
    kh = token_parts[0].shape[1] // 2
    size, width = kh // 2, outputs // 4
    heights = [size // 16] * 2 + [size // 8] * len(HOPS)
    return call(
        gradient_kernel,
        "gradient",
        24,
        where,
        (4,),
        [fixed(v.shape) for v in token_parts[:2]]
        + [fixed((count, kh))] * 2
        + [pl.BlockSpec((count, width), lambda i, where: (0, i))] * 2
        + [pl.BlockSpec((count, width), lambda i, where: (0, i + 2))] * 2,
        [pl.BlockSpec((height, width), lambda i, where: (0, i)) for height in heights],
        [jax.ShapeDtypeStruct((height, outputs), jnp.bfloat16) for height in heights],
        [pltpu.VMEM((4 * count, size), jnp.bfloat16), pltpu.VMEM((size, width), jnp.bfloat16)],
        8 * count * size * outputs,
        (*token_parts, *cot_parts),
    )


def hop_kernel(*refs):
    *arrived, part, out = refs
    total = f32(part[...])
    for ref in arrived:
        total = total + f32(ref[...])
    out[...] = total.astype(out.dtype)


def first_hop_kernel(arrived, part, out, *, upper):
    half = arrived.shape[0]
    here, there = (slice(0, half), slice(half, 2 * half))[:: 1 if upper else -1]
    out[here] = bf16(f32(part[here]) + f32(arrived[...]))
    out[there] = part[there]


def hop(part, *arrived, kernel=hop_kernel, kind=jnp.bfloat16):
    return pl.pallas_call(
        kernel,
        name="hop",
        out_shape=jax.ShapeDtypeStruct(part.shape, kind),
        compiler_params=pltpu.CompilerParams(vmem_limit_bytes=8 * 2**20),
        cost_estimate=pl.CostEstimate(
            flops=part.size, bytes_accessed=6 * part.size, transcendentals=0
        ),
    )(*arrived, part)


def forward_kernel(where, own, sib, pair, psib, w0, w1, w2, w3, w4, mine, other, away, lhs):
    yh, x = where[1], where[2]
    count, shard = own.shape[0], w0.shape[0]

    @pl.when(pl.program_id(0) == 0)
    def _():
        for r, (ref, base) in enumerate(((own, yh), (sib, yh), (pair, 0), (psib, 0))):
            for p, step in enumerate(BLOCK_STEPS):
                start = base * 4 * shard + (x + step) % 4 * shard
                lhs[r * count : (r + 1) * count, p * shard : (p + 1) * shard] = columns(
                    ref, start, shard
                )

    far = jnp.where(pl.program_id(0) == 0, w3[...], w4[...])
    rhs = jnp.concatenate([w0[...], w1[...], w2[...], far])
    out = jnp.dot(lhs[...], rhs, preferred_element_type=jnp.float32)
    mine[...] = out[:count]
    other[...] = out[count : 2 * count]
    away[...] = bf16(out[2 * count :])


def forward_parts(where, token_parts, blocks):
    count = token_parts[0].shape[0]
    shard, nh = blocks[0].shape
    width = nh // 2
    kinds = ((count, jnp.float32), (count, jnp.float32), (2 * count, jnp.bfloat16))
    return call(
        forward_kernel,
        "forward",
        28,
        where,
        (2,),
        [fixed(v.shape) for v in token_parts[:2]]
        + [fixed((count, 4 * shard))] * 2
        + [pl.BlockSpec((shard, width), lambda i, where: (0, i))] * 3
        + [fixed((shard, width))] * 2,
        [pl.BlockSpec((height, width), lambda i, where: (0, i)) for height, _ in kinds],
        [jax.ShapeDtypeStruct((height, nh), kind) for height, kind in kinds],
        [pltpu.VMEM((4 * count, 4 * shard), jnp.bfloat16)],
        32 * count * shard * nh,
        (*token_parts, *blocks),
    )


def backward_kernel(where, cot0, cot1, cot2, cot3, w0, w1, w2, w3, w4, mine, give, lhs):
    x = where[2]
    i = pl.program_id(0)
    count = cot0.shape[0]
    size, half = w3.shape

    @pl.when(i == 0)
    def _():
        for r, ref in enumerate((cot0, cot2, cot1, cot3)):
            lhs[r * count : (r + 1) * count] = ref[...]

    far = jnp.concatenate([w3[...], w4[...]], axis=1)
    rhs = jnp.concatenate([w0[...], w1[...], w2[...], far])
    out = lax.dot_general(
        lhs[...], rhs, (((1,), (1,)), ((), ())), preferred_element_type=jnp.float32
    )
    for p, step in enumerate(BLOCK_STEPS):
        start = pl.multiple_of((x + step) % 4 * 3 * size + i * size, 128)
        part = out[:, p * size : (p + 1) * size]
        mine[:, pl.ds(start, size)] = part[: 2 * count]
        give[:, pl.ds(start, size)] = bf16(part[2 * count :])


def backward_parts(where, cot_parts, blocks):
    count = cot_parts[0].shape[0]
    shard, nh = blocks[0].shape
    size = shard // 3
    types = (jnp.float32, jnp.bfloat16)
    return call(
        backward_kernel,
        "backward",
        28,
        where,
        (3,),
        [fixed((count, nh), lambda where: (0, where[0]))] * 2
        + [fixed((count, nh), lambda where: (0, 1 + where[0]))] * 2
        + [pl.BlockSpec((size, nh), lambda i, where: (i, 0))] * 3
        + [pl.BlockSpec((size, nh // 2), lambda i, where: (i, 0))] * 2,
        [fixed((2 * count, 4 * shard))] * 2,
        [jax.ShapeDtypeStruct((2 * count, 4 * shard), kind) for kind in types],
        [pltpu.VMEM((4 * count, nh), jnp.bfloat16)],
        32 * count * shard * nh,
        (*cot_parts, *blocks),
    )


def rows(value, start, size):
    return lax.dynamic_slice_in_dim(value, start, size, 0)


def joined(here, there, flag):
    return jnp.where(
        flag == 0, jnp.concatenate([here, there], axis=1), jnp.concatenate([there, here], axis=1)
    )


def reduce_over_x(part, x):
    size = part.shape[0] // 4
    total = rows(part, x * size, size)
    for dx in range(1, 4):
        to = table(lambda z, yl, c, yh, x: (z, yl, c, yh, x + dx))
        total = total + f32(send(bf16(rows(part, (x + dx) % 4 * size, size)), to))
    return total


def on_device(tokens, cotangent, levels, scales):
    z, yl, c, yh, x = (lax.axis_index(name) for name in AXES)
    where = jnp.stack([c, yh, x, window(z, c, yh)]).astype(jnp.int32)
    count = tokens.shape[0]
    factor = float(count * 256) ** -0.5

    packed = pack(tokens, cotangent)
    pair = send(packed, PAIR)

    levels, scales = after((levels, scales.T), packed)
    own = dequantize(where, levels, scales)
    left, right = send(own, X_UP), send(own, X_DOWN)

    cot_own, token_own = after((cotangent, tokens), own)
    cot_sib, token_sib = send(cot_own, CORE), send(token_own, CORE)
    cross = send(pair, CORE)
    token_parts = (tokens, token_sib, pair, cross)
    cot_parts = (cotangent, cot_sib, pair, cross)

    up, down, *grad = gradient(where, token_parts, cot_parts)
    half = own.shape[1] // 2
    blocks = (own, left, right, send(left[:, :half], X_UP), send(right[:, half:], X_DOWN))
    up, down = send(up, Z_UP), send(down, Z_DOWN)
    up = hop(grad[0], up, kernel=functools.partial(first_hop_kernel, upper=True))
    down = hop(grad[1], down, kernel=functools.partial(first_hop_kernel, upper=False))
    mine, other, away = forward_parts(where, token_parts, after(blocks, up, down))
    up, down = send(up, Z_UP), send(down, Z_DOWN)
    back = f32(send(away, PAIR))
    grad = after(grad, away)
    up, down = hop(grad[2], up), hop(grad[3], down)
    part, give = backward_parts(where, cot_parts, after(blocks, up, down))
    up, down = send(up, Z_UP), send(down, Z_DOWN)
    give = send(give, CORE)
    grad = after(grad, give, back)
    up, down = hop(grad[4], up), hop(grad[5], down)
    up, down = send(up, Z_UP), send(down, Z_DOWN)
    total = hop(grad[6], up, down, kind=jnp.float32)

    part = part + f32(give)
    grad_input = joined(bf16(part[:count]), send(bf16(part[count:]), PAIR), yh)
    there = send(bf16(other + back[count:]), CORE)
    forward = joined(bf16(mine + back[:count]), there, c)

    total = bf16(reduce_over_x(after(total, forward, part), x) * factor)
    size = total.shape[0] // 2
    got = [f32(send(rows(total, (yl ^ m) * size, size), OWNERS[m])) for m in range(2)]
    got, grad_input = after((got, grad_input))
    return forward, grad_input, got[0] + got[1]


def solution(mesh):
    fine = Mesh(mesh.devices.reshape(SIZES), AXES)
    token_spec, node_spec = P(AXES, None), P(("yh", "x"), None)
    return jax.shard_map(
        on_device,
        mesh=fine,
        in_specs=(token_spec, token_spec, node_spec, node_spec),
        out_specs=(token_spec, token_spec, token_spec),
        check_vma=False,
    )
```

```python
import functools
import math

import jax
import jax.numpy as jnp
from jax import lax
from jax.experimental import pallas as pl
from jax.experimental.pallas import tpu as pltpu
from jax.sharding import Mesh, PartitionSpec as P

AXES = ("z", "yl", "c", "yh", "x")
SIZES = (8, 2, 2, 2, 4)
BLOCK_STEPS = (0, 3, 1, 2)
HOPS = (3, -3, 2, -2, 1, -1, 0)


def table(move):
    pairs = []
    for z in range(8):
        for yl in range(2):
            for c in range(2):
                for yh in range(2):
                    for x in range(4):
                        pairs.append((place(z, yl, c, yh, x), place(*move(z, yl, c, yh, x))))
    return pairs


def place(z, yl, c, yh, x):
    return (((z % 8 * 2 + yl % 2) * 2 + c % 2) * 2 + yh % 2) * 4 + x % 4


def window(z, c, yh):
    return (z + 11 - 4 * yh - 2 * c) % 8


def owner(z, yl, c, yh, x, message):
    chunk = window(z, c, yh)
    return 4 * yh + 2 * c + chunk // 4, chunk % 4 // 2, chunk % 2, x // 2, x % 2 * 2 + (yl ^ message)


X_UP = table(lambda z, yl, c, yh, x: (z, yl, c, yh, x + 1))
X_DOWN = table(lambda z, yl, c, yh, x: (z, yl, c, yh, x - 1))
Z_UP = table(lambda z, yl, c, yh, x: (z + 1, yl, c, yh, x))
Z_DOWN = table(lambda z, yl, c, yh, x: (z - 1, yl, c, yh, x))
CORE = table(lambda z, yl, c, yh, x: (z, yl, c + 1, yh, x))
PAIR = table(lambda z, yl, c, yh, x: (z, yl + 1, c, yh + 1, x))
OWNERS = [
    table(lambda z, yl, c, yh, x: owner(z, yl, c, yh, x, message)) for message in range(2)
]


def send(value, pairs):
    return lax.ppermute(value, AXES, pairs)


def after(values, *earlier):
    return lax.optimization_barrier((values, earlier))[0]


def f32(value):
    return value.astype(jnp.float32)


def bf16(value):
    return value.astype(jnp.bfloat16)


def call(kernel, name, mib, where, grid, in_specs, out_specs, out_shape, scratch, flops, operands):
    moved = sum(v.size * v.dtype.itemsize for v in operands)
    moved += sum(math.prod(v.shape) * v.dtype.itemsize for v in jax.tree.leaves(out_shape))
    return pl.pallas_call(
        kernel,
        name=name,
        grid_spec=pltpu.PrefetchScalarGridSpec(
            num_scalar_prefetch=1,
            grid=grid,
            in_specs=in_specs,
            out_specs=out_specs,
            scratch_shapes=scratch,
        ),
        out_shape=out_shape,
        compiler_params=pltpu.CompilerParams(vmem_limit_bytes=mib * 2**20),
        cost_estimate=pl.CostEstimate(flops=flops, bytes_accessed=moved, transcendentals=0),
    )(where, *operands)


def fixed(shape, at=lambda where: (0, 0)):
    return pl.BlockSpec(shape, lambda i, where: at(where))


def dequantize_kernel(where, levels, scales, out):
    count = scales.shape[0] // 2
    width = out.shape[1] // count
    mine = jnp.where(where[0] == 0, scales[:count], scales[count:]).T
    for b in range(count):
        scale = mine[:, b : b + 1]
        span = slice(b * width, (b + 1) * width)
        out[:, span] = bf16(f32(levels[:, span]) * scale)


def dequantize(where, levels, scales):
    row_count, nh = levels.shape[0], levels.shape[1] // 2
    size = row_count // 3
    return call(
        dequantize_kernel,
        "dequantize",
        12,
        where,
        (3,),
        [
            pl.BlockSpec((size, nh), lambda i, where: (i, where[0])),
            pl.BlockSpec((scales.shape[0], size), lambda i, where: (0, i)),
        ],
        pl.BlockSpec((size, nh), lambda i, where: (i, 0)),
        jax.ShapeDtypeStruct((row_count, nh), jnp.bfloat16),
        [],
        row_count * nh,
        (levels, scales),
    )


def pack_kernel(tokens, cotangent, out, sems):
    kh = tokens.shape[1] // 2
    start = pl.multiple_of((1 - lax.axis_index("yh")) * kh, 128)
    copies = (
        pltpu.make_async_copy(tokens.at[:, pl.ds(start, kh)], out.at[:, pl.ds(0, kh)], sems.at[0]),
        pltpu.make_async_copy(cotangent, out.at[:, pl.ds(kh, cotangent.shape[1])], sems.at[1]),
    )
    for copy in copies:
        copy.start()
    for copy in copies:
        copy.wait()


def pack(tokens, cotangent):
    shape = (tokens.shape[0], tokens.shape[1] // 2 + cotangent.shape[1])
    return pl.pallas_call(
        pack_kernel,
        name="pack",
        in_specs=[pl.BlockSpec(memory_space=pl.ANY)] * 2,
        out_specs=pl.BlockSpec(memory_space=pltpu.VMEM),
        out_shape=jax.ShapeDtypeStruct(shape, jnp.bfloat16),
        scratch_shapes=[pltpu.SemaphoreType.DMA((2,))],
        compiler_params=pltpu.CompilerParams(vmem_limit_bytes=60 * 2**20),
    )(tokens, cotangent)


def columns(ref, start, size):
    return ref[:, pl.ds(pl.multiple_of(start, 128), size)]


def gradient_kernel(where, own, sib, pair, psib, cot0, cot1, cot2, cot3, *refs):
    c, yh = where[0], where[1]
    *chunks, lhs, out = refs
    count, size = own.shape[0], lhs.shape[1]

    @pl.when(pl.program_id(0) == 0)
    def _():
        for r, (ref, base) in enumerate(((own, yh), (sib, yh), (pair, 0), (psib, 0))):
            start = base * 2 * size + c * size
            lhs[r * count : (r + 1) * count] = columns(ref, start, size)

    rhs = jnp.concatenate([cot0[...], cot1[...], cot2[...], cot3[...]])
    out[...] = bf16(
        lax.dot_general(
            lhs[...], rhs, (((0,), (0,)), ((), ())), preferred_element_type=jnp.float32
        )
    )
    height, start = size // 8, 0
    for k, ref in zip((4, 4, *HOPS), chunks):
        part = ref.shape[0]
        row = (where[3] + 8 + k) % 8 * height + start
        ref[...] = out[pl.ds(pl.multiple_of(row, 16), part)]
        start = (start + part) % height


def gradient(where, token_parts, cot_parts):
    count, outputs = cot_parts[0].shape
    kh = token_parts[0].shape[1] // 2
    size, width = kh // 2, outputs // 4
    heights = [size // 16] * 2 + [size // 8] * len(HOPS)
    return call(
        gradient_kernel,
        "gradient",
        24,
        where,
        (4,),
        [fixed(v.shape) for v in token_parts[:2]]
        + [fixed((count, kh))] * 2
        + [pl.BlockSpec((count, width), lambda i, where: (0, i))] * 2
        + [pl.BlockSpec((count, width), lambda i, where: (0, i + 2))] * 2,
        [pl.BlockSpec((height, width), lambda i, where: (0, i)) for height in heights],
        [jax.ShapeDtypeStruct((height, outputs), jnp.bfloat16) for height in heights],
        [pltpu.VMEM((4 * count, size), jnp.bfloat16), pltpu.VMEM((size, width), jnp.bfloat16)],
        8 * count * size * outputs,
        (*token_parts, *cot_parts),
    )


def hop_kernel(*refs):
    *arrived, part, out = refs
    total = f32(part[...])
    for ref in arrived:
        total = total + f32(ref[...])
    out[...] = total.astype(out.dtype)


def first_hop_kernel(arrived, part, out, *, upper):
    half = arrived.shape[0]
    here, there = (slice(0, half), slice(half, 2 * half))[:: 1 if upper else -1]
    out[here] = bf16(f32(part[here]) + f32(arrived[...]))
    out[there] = part[there]


def hop(part, *arrived, kernel=hop_kernel, kind=jnp.bfloat16):
    return pl.pallas_call(
        kernel,
        name="hop",
        out_shape=jax.ShapeDtypeStruct(part.shape, kind),
        compiler_params=pltpu.CompilerParams(vmem_limit_bytes=8 * 2**20),
        cost_estimate=pl.CostEstimate(
            flops=part.size, bytes_accessed=6 * part.size, transcendentals=0
        ),
    )(*arrived, part)


def forward_kernel(where, own, sib, pair, psib, w0, w1, w2, w3, w4, mine, other, away, lhs):
    yh, x = where[1], where[2]
    count, shard = own.shape[0], w0.shape[0]

    @pl.when(pl.program_id(0) == 0)
    def _():
        for r, (ref, base) in enumerate(((own, yh), (sib, yh), (pair, 0), (psib, 0))):
            for p, step in enumerate(BLOCK_STEPS):
                start = base * 4 * shard + (x + step) % 4 * shard
                lhs[r * count : (r + 1) * count, p * shard : (p + 1) * shard] = columns(
                    ref, start, shard
                )

    far = jnp.where(pl.program_id(0) == 0, w3[...], w4[...])
    rhs = jnp.concatenate([w0[...], w1[...], w2[...], far])
    out = jnp.dot(lhs[...], rhs, preferred_element_type=jnp.float32)
    mine[...] = out[:count]
    other[...] = out[count : 2 * count]
    away[...] = bf16(out[2 * count :])


def forward_parts(where, token_parts, blocks):
    count = token_parts[0].shape[0]
    shard, nh = blocks[0].shape
    width = nh // 2
    kinds = ((count, jnp.float32), (count, jnp.float32), (2 * count, jnp.bfloat16))
    return call(
        forward_kernel,
        "forward",
        28,
        where,
        (2,),
        [fixed(v.shape) for v in token_parts[:2]]
        + [fixed((count, 4 * shard))] * 2
        + [pl.BlockSpec((shard, width), lambda i, where: (0, i))] * 3
        + [fixed((shard, width))] * 2,
        [pl.BlockSpec((height, width), lambda i, where: (0, i)) for height, _ in kinds],
        [jax.ShapeDtypeStruct((height, nh), kind) for height, kind in kinds],
        [pltpu.VMEM((4 * count, 4 * shard), jnp.bfloat16)],
        32 * count * shard * nh,
        (*token_parts, *blocks),
    )


def backward_kernel(where, cot0, cot1, cot2, cot3, w0, w1, w2, w3, w4, mine, give, lhs):
    x = where[2]
    i = pl.program_id(0)
    count = cot0.shape[0]
    size, half = w3.shape

    @pl.when(i == 0)
    def _():
        for r, ref in enumerate((cot0, cot2, cot1, cot3)):
            lhs[r * count : (r + 1) * count] = ref[...]

    far = jnp.concatenate([w3[...], w4[...]], axis=1)
    rhs = jnp.concatenate([w0[...], w1[...], w2[...], far])
    out = lax.dot_general(
        lhs[...], rhs, (((1,), (1,)), ((), ())), preferred_element_type=jnp.float32
    )
    for p, step in enumerate(BLOCK_STEPS):
        start = pl.multiple_of((x + step) % 4 * 3 * size + i * size, 128)
        part = out[:, p * size : (p + 1) * size]
        mine[:, pl.ds(start, size)] = part[: 2 * count]
        give[:, pl.ds(start, size)] = bf16(part[2 * count :])


def backward_parts(where, cot_parts, blocks):
    count = cot_parts[0].shape[0]
    shard, nh = blocks[0].shape
    size = shard // 3
    types = (jnp.float32, jnp.bfloat16)
    return call(
        backward_kernel,
        "backward",
        28,
        where,
        (3,),
        [fixed((count, nh), lambda where: (0, where[0]))] * 2
        + [fixed((count, nh), lambda where: (0, 1 + where[0]))] * 2
        + [pl.BlockSpec((size, nh), lambda i, where: (i, 0))] * 3
        + [pl.BlockSpec((size, nh // 2), lambda i, where: (i, 0))] * 2,
        [fixed((2 * count, 4 * shard))] * 2,
        [jax.ShapeDtypeStruct((2 * count, 4 * shard), kind) for kind in types],
        [pltpu.VMEM((4 * count, nh), jnp.bfloat16)],
        32 * count * shard * nh,
        (*cot_parts, *blocks),
    )


def rows(value, start, size):
    return lax.dynamic_slice_in_dim(value, start, size, 0)


def joined(here, there, flag):
    return jnp.where(
        flag == 0, jnp.concatenate([here, there], axis=1), jnp.concatenate([there, here], axis=1)
    )


def reduce_over_x(part, x):
    size = part.shape[0] // 4
    total = rows(part, x * size, size)
    for dx in range(1, 4):
        to = table(lambda z, yl, c, yh, x: (z, yl, c, yh, x + dx))
        total = total + f32(send(bf16(rows(part, (x + dx) % 4 * size, size)), to))
    return total


def on_device(tokens, cotangent, levels, scales):
    z, yl, c, yh, x = (lax.axis_index(name) for name in AXES)
    where = jnp.stack([c, yh, x, window(z, c, yh)]).astype(jnp.int32)
    count = tokens.shape[0]
    factor = float(count * 256) ** -0.5

    packed = pack(tokens, cotangent)
    pair = send(packed, PAIR)

    levels, scales = after((levels, scales.T), packed)
    own = dequantize(where, levels, scales)
    left, right = send(own, X_UP), send(own, X_DOWN)

    cot_own, token_own = after((cotangent, tokens), own)
    cot_sib, token_sib = send(cot_own, CORE), send(token_own, CORE)
    cross = send(pair, CORE)
    token_parts = (tokens, token_sib, pair, cross)
    cot_parts = (cotangent, cot_sib, pair, cross)

    up, down, *grad = gradient(where, token_parts, after(cot_parts, left, right))
    half = own.shape[1] // 2
    up, down = send(up, Z_UP), send(down, Z_DOWN)
    up = hop(grad[0], up, kernel=functools.partial(first_hop_kernel, upper=True))
    down = hop(grad[1], down, kernel=functools.partial(first_hop_kernel, upper=False))
    left, right = after((left, right), up, down)
    blocks = (own, left, right, send(left[:, :half], X_UP), send(right[:, half:], X_DOWN))
    up, down = send(up, Z_UP), send(down, Z_DOWN)
    up, down = hop(grad[2], up), hop(grad[3], down)
    mine, other, away = forward_parts(where, token_parts, after(blocks, up, down))
    up, down = send(up, Z_UP), send(down, Z_DOWN)
    back = f32(send(away, PAIR))
    grad = after(grad, away)
    up, down = hop(grad[4], up), hop(grad[5], down)
    part, give = backward_parts(where, cot_parts, after(blocks, up, down))
    up, down = send(up, Z_UP), send(down, Z_DOWN)
    give = send(give, CORE)
    grad = after(grad, part)
    total = hop(grad[6], up, down, kind=jnp.float32)

    part = part + f32(give)
    grad_input = joined(bf16(part[:count]), send(bf16(part[count:]), PAIR), yh)
    there = send(bf16(other + back[count:]), CORE)
    forward = joined(bf16(mine + back[:count]), there, c)

    total = bf16(reduce_over_x(after(total, forward, part), x) * factor)
    size = total.shape[0] // 2
    got = [f32(send(rows(total, (yl ^ m) * size, size), OWNERS[m])) for m in range(2)]
    got, grad_input = after((got, grad_input))
    return forward, grad_input, got[0] + got[1]


def solution(mesh):
    fine = Mesh(mesh.devices.reshape(SIZES), AXES)
    token_spec, node_spec = P(AXES, None), P(("yh", "x"), None)
    return jax.shard_map(
        on_device,
        mesh=fine,
        in_specs=(token_spec, token_spec, node_spec, node_spec),
        out_specs=(token_spec, token_spec, token_spec),
        check_vma=False,
    )
```

```python
import functools
import math

import jax
import jax.numpy as jnp
from jax import lax
from jax.experimental import pallas as pl
from jax.experimental.pallas import tpu as pltpu
from jax.sharding import Mesh, PartitionSpec as P

AXES = ("z", "yl", "c", "yh", "x")
SIZES = (8, 2, 2, 2, 4)
BLOCK_STEPS = (0, 3, 1, 2)
HOPS = (3, -3, 2, -2, 1, -1, 0)


def table(move):
    pairs = []
    for z in range(8):
        for yl in range(2):
            for c in range(2):
                for yh in range(2):
                    for x in range(4):
                        pairs.append((place(z, yl, c, yh, x), place(*move(z, yl, c, yh, x))))
    return pairs


def place(z, yl, c, yh, x):
    return (((z % 8 * 2 + yl % 2) * 2 + c % 2) * 2 + yh % 2) * 4 + x % 4


def window(z, c, yh):
    return (z + 11 - 4 * yh - 2 * c) % 8


def owner(z, yl, c, yh, x, message):
    chunk = window(z, c, yh)
    return 4 * yh + 2 * c + chunk // 4, chunk % 4 // 2, chunk % 2, yl ^ message, x


X_UP = table(lambda z, yl, c, yh, x: (z, yl, c, yh, x + 1))
X_DOWN = table(lambda z, yl, c, yh, x: (z, yl, c, yh, x - 1))
X_STEPS = [table(lambda z, yl, c, yh, x: (z, yl, c, yh, x + dx)) for dx in (1, 2, 3)]
Z_UP = table(lambda z, yl, c, yh, x: (z + 1, yl, c, yh, x))
Z_DOWN = table(lambda z, yl, c, yh, x: (z - 1, yl, c, yh, x))
CORE = table(lambda z, yl, c, yh, x: (z, yl, c + 1, yh, x))
PAIR = table(lambda z, yl, c, yh, x: (z, yl + 1, c, yh + 1, x))
OWNERS = [
    table(lambda z, yl, c, yh, x: owner(z, yl, c, yh, x, message)) for message in range(2)
]


def send(value, pairs):
    return lax.ppermute(value, AXES, pairs)


def after(values, *earlier):
    return lax.optimization_barrier((values, earlier))[0]


def f32(value):
    return value.astype(jnp.float32)


def bf16(value):
    return value.astype(jnp.bfloat16)


def call(kernel, name, mib, where, grid, in_specs, out_specs, out_shape, scratch, flops, operands):
    moved = sum(v.size * v.dtype.itemsize for v in operands)
    moved += sum(math.prod(v.shape) * v.dtype.itemsize for v in jax.tree.leaves(out_shape))
    return pl.pallas_call(
        kernel,
        name=name,
        grid_spec=pltpu.PrefetchScalarGridSpec(
            num_scalar_prefetch=1,
            grid=grid,
            in_specs=in_specs,
            out_specs=out_specs,
            scratch_shapes=scratch,
        ),
        out_shape=out_shape,
        compiler_params=pltpu.CompilerParams(vmem_limit_bytes=mib * 2**20),
        cost_estimate=pl.CostEstimate(flops=flops, bytes_accessed=moved, transcendentals=0),
    )(where, *operands)


def fixed(shape, at=lambda where: (0, 0)):
    return pl.BlockSpec(shape, lambda i, where: at(where))


def dequantize_kernel(where, levels, scales, out):
    count = scales.shape[0] // 2
    width = out.shape[1] // count
    mine = jnp.where(where[0] == 0, scales[:count], scales[count:]).T
    for b in range(count):
        scale = mine[:, b : b + 1]
        span = slice(b * width, (b + 1) * width)
        out[:, span] = bf16(f32(levels[:, span]) * scale)


def dequantize(where, levels, scales):
    row_count, nh = levels.shape[0], levels.shape[1] // 2
    size = row_count // 3
    return call(
        dequantize_kernel,
        "dequantize",
        12,
        where,
        (3,),
        [
            pl.BlockSpec((size, nh), lambda i, where: (i, where[0])),
            pl.BlockSpec((scales.shape[0], size), lambda i, where: (0, i)),
        ],
        pl.BlockSpec((size, nh), lambda i, where: (i, 0)),
        jax.ShapeDtypeStruct((row_count, nh), jnp.bfloat16),
        [],
        row_count * nh,
        (levels, scales),
    )


def pack_kernel(tokens, cotangent, out, sems):
    kh = tokens.shape[1] // 2
    start = pl.multiple_of((1 - lax.axis_index("yh")) * kh, 128)
    copies = (
        pltpu.make_async_copy(tokens.at[:, pl.ds(start, kh)], out.at[:, pl.ds(0, kh)], sems.at[0]),
        pltpu.make_async_copy(cotangent, out.at[:, pl.ds(kh, cotangent.shape[1])], sems.at[1]),
    )
    for copy in copies:
        copy.start()
    for copy in copies:
        copy.wait()


def pack(tokens, cotangent):
    shape = (tokens.shape[0], tokens.shape[1] // 2 + cotangent.shape[1])
    return pl.pallas_call(
        pack_kernel,
        name="pack",
        in_specs=[pl.BlockSpec(memory_space=pl.ANY)] * 2,
        out_specs=pl.BlockSpec(memory_space=pltpu.VMEM),
        out_shape=jax.ShapeDtypeStruct(shape, jnp.bfloat16),
        scratch_shapes=[pltpu.SemaphoreType.DMA((2,))],
        compiler_params=pltpu.CompilerParams(vmem_limit_bytes=60 * 2**20),
    )(tokens, cotangent)


def columns(ref, start, size):
    return ref[:, pl.ds(pl.multiple_of(start, 128), size)]


def gradient_kernel(where, own, sib, pair, psib, cot0, cot1, cot2, cot3, *refs):
    c, yh = where[0], where[1]
    *chunks, lhs, out = refs
    count, size = own.shape[0], lhs.shape[1]

    @pl.when(pl.program_id(0) == 0)
    def _():
        for r, (ref, base) in enumerate(((own, yh), (sib, yh), (pair, 0), (psib, 0))):
            start = base * 2 * size + c * size
            lhs[r * count : (r + 1) * count] = columns(ref, start, size)

    rhs = jnp.concatenate([cot0[...], cot1[...], cot2[...], cot3[...]])
    out[...] = bf16(
        lax.dot_general(
            lhs[...], rhs, (((0,), (0,)), ((), ())), preferred_element_type=jnp.float32
        )
    )
    height, start = size // 8, 0
    for k, ref in zip((4, 4, *HOPS), chunks):
        part = ref.shape[0]
        row = (where[3] + 8 + k) % 8 * height + start
        ref[...] = out[pl.ds(pl.multiple_of(row, 16), part)]
        start = (start + part) % height


def gradient(where, token_parts, cot_parts):
    count, outputs = cot_parts[0].shape
    kh = token_parts[0].shape[1] // 2
    size, width = kh // 2, outputs // 4
    heights = [size // 16] * 2 + [size // 8] * len(HOPS)
    return call(
        gradient_kernel,
        "gradient",
        24,
        where,
        (4,),
        [fixed(v.shape) for v in token_parts[:2]]
        + [fixed((count, kh))] * 2
        + [pl.BlockSpec((count, width), lambda i, where: (0, i))] * 2
        + [pl.BlockSpec((count, width), lambda i, where: (0, i + 2))] * 2,
        [pl.BlockSpec((height, width), lambda i, where: (0, i)) for height in heights],
        [jax.ShapeDtypeStruct((height, outputs), jnp.bfloat16) for height in heights],
        [pltpu.VMEM((4 * count, size), jnp.bfloat16), pltpu.VMEM((size, width), jnp.bfloat16)],
        8 * count * size * outputs,
        (*token_parts, *cot_parts),
    )


def hop_kernel(*refs):
    *arrived, part, out = refs
    total = f32(part[...])
    for ref in arrived:
        total = total + f32(ref[...])
    out[...] = total.astype(out.dtype)


def first_hop_kernel(arrived, part, out, *, upper):
    half = arrived.shape[0]
    here, there = (slice(0, half), slice(half, 2 * half))[:: 1 if upper else -1]
    out[here] = bf16(f32(part[here]) + f32(arrived[...]))
    out[there] = part[there]


def hop(part, *arrived, kernel=hop_kernel, kind=jnp.bfloat16):
    return pl.pallas_call(
        kernel,
        name="hop",
        out_shape=jax.ShapeDtypeStruct(part.shape, kind),
        compiler_params=pltpu.CompilerParams(vmem_limit_bytes=8 * 2**20),
        cost_estimate=pl.CostEstimate(
            flops=part.size, bytes_accessed=6 * part.size, transcendentals=0
        ),
    )(*arrived, part)


def last_hop_kernel(where, up, down, part, own, *refs):
    *pieces, total = refs
    size = own.shape[0]
    for x in range(4):
        for yh in range(2):
            here = slice((yh * 4 + x) * (size // 2), (yh * 4 + x + 1) * (size // 2))
            there = slice((x * 2 + yh) * (size // 2), (x * 2 + yh + 1) * (size // 2))
            total[there] = f32(part[here]) + f32(up[here]) + f32(down[here])
    for dx, ref in enumerate((own, *pieces)):
        start = pl.multiple_of((where[2] + dx) % 4 * size, 8)
        ref[...] = total[pl.ds(start, size)].astype(ref.dtype)


def last_hop(where, part, up, down):
    size, outputs = part.shape
    width = outputs // 2
    kinds = (jnp.float32, *[jnp.bfloat16] * 3)
    return call(
        last_hop_kernel,
        "last_hop",
        8,
        where,
        (2,),
        [pl.BlockSpec((size, width), lambda i, where: (0, i))] * 3,
        [pl.BlockSpec((size // 4, width), lambda i, where: (0, i)) for _ in kinds],
        [jax.ShapeDtypeStruct((size // 4, outputs), kind) for kind in kinds],
        [pltpu.VMEM((size, width), jnp.float32)],
        2 * part.size,
        (up, down, part),
    )


def sum_kernel(where, own, one, two, three, same, other, total, *, factor):
    size = same.shape[0]
    total[...] = (own[...] + f32(one[...]) + f32(two[...]) + f32(three[...])) * factor
    first, second = bf16(total[:size]), bf16(total[size:])
    yl = where[4]
    same[...] = jnp.where(yl == 0, first, second)
    other[...] = jnp.where(yl == 0, second, first)


def sum_over_x(where, factor, own, *arrived):
    size, outputs = own.shape
    return call(
        functools.partial(sum_kernel, factor=factor),
        "sum_over_x",
        8,
        where,
        (1,),
        [fixed(own.shape)] * 4,
        [fixed((size // 2, outputs))] * 2,
        [jax.ShapeDtypeStruct((size // 2, outputs), jnp.bfloat16)] * 2,
        [pltpu.VMEM((size, outputs), jnp.float32)],
        4 * own.size,
        (own, *arrived),
    )


def forward_kernel(where, own, sib, pair, psib, w0, w1, w2, w3, w4, mine, other, away, lhs):
    yh, x = where[1], where[2]
    count, shard = own.shape[0], w0.shape[0]

    @pl.when(pl.program_id(0) == 0)
    def _():
        for r, (ref, base) in enumerate(((own, yh), (sib, yh), (pair, 0), (psib, 0))):
            for p, step in enumerate(BLOCK_STEPS):
                start = base * 4 * shard + (x + step) % 4 * shard
                lhs[r * count : (r + 1) * count, p * shard : (p + 1) * shard] = columns(
                    ref, start, shard
                )

    far = jnp.where(pl.program_id(0) == 0, w3[...], w4[...])
    rhs = jnp.concatenate([w0[...], w1[...], w2[...], far])
    out = jnp.dot(lhs[...], rhs, preferred_element_type=jnp.float32)
    mine[...] = out[:count]
    other[...] = out[count : 2 * count]
    away[...] = bf16(out[2 * count :])


def forward_parts(where, token_parts, blocks):
    count = token_parts[0].shape[0]
    shard, nh = blocks[0].shape
    width = nh // 2
    kinds = ((count, jnp.float32), (count, jnp.float32), (2 * count, jnp.bfloat16))
    return call(
        forward_kernel,
        "forward",
        28,
        where,
        (2,),
        [fixed(v.shape) for v in token_parts[:2]]
        + [fixed((count, 4 * shard))] * 2
        + [pl.BlockSpec((shard, width), lambda i, where: (0, i))] * 3
        + [fixed((shard, width))] * 2,
        [pl.BlockSpec((height, width), lambda i, where: (0, i)) for height, _ in kinds],
        [jax.ShapeDtypeStruct((height, nh), kind) for height, kind in kinds],
        [pltpu.VMEM((4 * count, 4 * shard), jnp.bfloat16)],
        32 * count * shard * nh,
        (*token_parts, *blocks),
    )


def backward_kernel(where, cot0, cot1, cot2, cot3, w0, w1, w2, w3, w4, mine, give, lhs):
    x = where[2]
    i = pl.program_id(0)
    count = cot0.shape[0]
    size, half = w3.shape

    @pl.when(i == 0)
    def _():
        for r, ref in enumerate((cot0, cot2, cot1, cot3)):
            lhs[r * count : (r + 1) * count] = ref[...]

    far = jnp.concatenate([w3[...], w4[...]], axis=1)
    rhs = jnp.concatenate([w0[...], w1[...], w2[...], far])
    out = lax.dot_general(
        lhs[...], rhs, (((1,), (1,)), ((), ())), preferred_element_type=jnp.float32
    )
    for p, step in enumerate(BLOCK_STEPS):
        start = pl.multiple_of((x + step) % 4 * 3 * size + i * size, 128)
        part = out[:, p * size : (p + 1) * size]
        mine[:, pl.ds(start, size)] = part[: 2 * count]
        give[:, pl.ds(start, size)] = bf16(part[2 * count :])


def backward_parts(where, cot_parts, blocks):
    count = cot_parts[0].shape[0]
    shard, nh = blocks[0].shape
    size = shard // 3
    types = (jnp.float32, jnp.bfloat16)
    return call(
        backward_kernel,
        "backward",
        28,
        where,
        (3,),
        [fixed((count, nh), lambda where: (0, where[0]))] * 2
        + [fixed((count, nh), lambda where: (0, 1 + where[0]))] * 2
        + [pl.BlockSpec((size, nh), lambda i, where: (i, 0))] * 3
        + [pl.BlockSpec((size, nh // 2), lambda i, where: (i, 0))] * 2,
        [fixed((2 * count, 4 * shard))] * 2,
        [jax.ShapeDtypeStruct((2 * count, 4 * shard), kind) for kind in types],
        [pltpu.VMEM((4 * count, nh), jnp.bfloat16)],
        32 * count * shard * nh,
        (*cot_parts, *blocks),
    )


def joined(here, there, flag):
    return jnp.where(
        flag == 0, jnp.concatenate([here, there], axis=1), jnp.concatenate([there, here], axis=1)
    )


def on_device(tokens, cotangent, levels, scales):
    z, yl, c, yh, x = (lax.axis_index(name) for name in AXES)
    where = jnp.stack([c, yh, x, window(z, c, yh), yl]).astype(jnp.int32)
    count = tokens.shape[0]
    factor = float(count * 256) ** -0.5

    packed = pack(tokens, cotangent)
    pair = send(packed, PAIR)

    levels, scales = after((levels, scales.T), packed)
    own = dequantize(where, levels, scales)
    left, right = send(own, X_UP), send(own, X_DOWN)

    cot_own, token_own = after((cotangent, tokens), own)
    cot_sib, token_sib = send(cot_own, CORE), send(token_own, CORE)
    cross = send(pair, CORE)
    token_parts = (tokens, token_sib, pair, cross)
    cot_parts = (cotangent, cot_sib, pair, cross)

    up, down, *grad = gradient(where, token_parts, after(cot_parts, left, right))
    half = own.shape[1] // 2
    up, down = send(up, Z_UP), send(down, Z_DOWN)
    up = hop(grad[0], up, kernel=functools.partial(first_hop_kernel, upper=True))
    down = hop(grad[1], down, kernel=functools.partial(first_hop_kernel, upper=False))
    left, right = after((left, right), up, down)
    blocks = (own, left, right, send(left[:, :half], X_UP), send(right[:, half:], X_DOWN))
    up, down = send(up, Z_UP), send(down, Z_DOWN)
    up, down = hop(grad[2], up), hop(grad[3], down)
    mine, other, away = forward_parts(where, token_parts, after(blocks, up, down))
    up, down = send(up, Z_UP), send(down, Z_DOWN)
    back = f32(send(away, PAIR))
    grad = after(grad, away)
    up, down = hop(grad[4], up), hop(grad[5], down)
    part, give = backward_parts(where, cot_parts, after(blocks, up, down))
    up, down = send(up, Z_UP), send(down, Z_DOWN)
    give = send(give, CORE)
    own_piece, *pieces = last_hop(where, after(grad[6], part), up, down)
    arrived = [send(piece, to) for piece, to in zip(pieces, X_STEPS)]
    back = after(back, own_piece)
    here = bf16(mine + back[:count])
    there = send(bf16(other + back[count:]), CORE)
    part, give = after((part, give), own_piece)
    part = part + f32(give)
    grad_here, grad_away = bf16(part[:count]), bf16(part[count:])
    grad_there = send(grad_away, PAIR)
    same, swapped = sum_over_x(where, factor, own_piece, *after(arrived, grad_away))
    got = send(same, OWNERS[0]), send(swapped, OWNERS[1])
    forward = joined(after(here, same), there, c)
    grad_input = joined(after(grad_here, same), grad_there, yh)
    one, two = after(got, forward, grad_input)
    return forward, grad_input, f32(one) + f32(two)


def solution(mesh):
    fine = Mesh(mesh.devices.reshape(SIZES), AXES)
    token_spec, node_spec = P(AXES, None), P(("yh", "x"), None)
    return jax.shard_map(
        on_device,
        mesh=fine,
        in_specs=(token_spec, token_spec, node_spec, node_spec),
        out_specs=(token_spec, token_spec, token_spec),
        check_vma=False,
    )
```

```python
import functools
import math

import jax
import jax.numpy as jnp
from jax import lax
from jax.experimental import pallas as pl
from jax.experimental.pallas import tpu as pltpu
from jax.sharding import Mesh, PartitionSpec as P

AXES = ("z", "yl", "c", "yh", "x")
SIZES = (8, 2, 2, 2, 4)
BLOCK_STEPS = (0, 3, 1, 2)
HOPS = (3, -3, 2, -2, 1, -1, 0)


def table(move):
    pairs = []
    for z in range(8):
        for yl in range(2):
            for c in range(2):
                for yh in range(2):
                    for x in range(4):
                        pairs.append((place(z, yl, c, yh, x), place(*move(z, yl, c, yh, x))))
    return pairs


def place(z, yl, c, yh, x):
    return (((z % 8 * 2 + yl % 2) * 2 + c % 2) * 2 + yh % 2) * 4 + x % 4


def window(z, c, yh):
    return (z + 11 - 4 * yh - 2 * c) % 8


def owner(z, yl, c, yh, x, message):
    chunk = window(z, c, yh)
    return 4 * yh + 2 * c + chunk // 4, chunk % 4 // 2, chunk % 2, yl ^ message, x


X_UP = table(lambda z, yl, c, yh, x: (z, yl, c, yh, x + 1))
X_DOWN = table(lambda z, yl, c, yh, x: (z, yl, c, yh, x - 1))
X_STEPS = [table(lambda z, yl, c, yh, x: (z, yl, c, yh, x + dx)) for dx in (1, 2, 3)]
Z_UP = table(lambda z, yl, c, yh, x: (z + 1, yl, c, yh, x))
Z_DOWN = table(lambda z, yl, c, yh, x: (z - 1, yl, c, yh, x))
CORE = table(lambda z, yl, c, yh, x: (z, yl, c + 1, yh, x))
PAIR = table(lambda z, yl, c, yh, x: (z, yl + 1, c, yh + 1, x))
OWNERS = [
    table(lambda z, yl, c, yh, x: owner(z, yl, c, yh, x, message)) for message in range(2)
]


def send(value, pairs):
    return lax.ppermute(value, AXES, pairs)


def after(values, *earlier):
    return lax.optimization_barrier((values, earlier))[0]


def f32(value):
    return value.astype(jnp.float32)


def bf16(value):
    return value.astype(jnp.bfloat16)


def call(kernel, name, mib, where, grid, in_specs, out_specs, out_shape, scratch, flops, operands):
    moved = sum(v.size * v.dtype.itemsize for v in operands)
    moved += sum(math.prod(v.shape) * v.dtype.itemsize for v in jax.tree.leaves(out_shape))
    return pl.pallas_call(
        kernel,
        name=name,
        grid_spec=pltpu.PrefetchScalarGridSpec(
            num_scalar_prefetch=1,
            grid=grid,
            in_specs=in_specs,
            out_specs=out_specs,
            scratch_shapes=scratch,
        ),
        out_shape=out_shape,
        compiler_params=pltpu.CompilerParams(vmem_limit_bytes=mib * 2**20),
        cost_estimate=pl.CostEstimate(flops=flops, bytes_accessed=moved, transcendentals=0),
    )(where, *operands)


def fixed(shape, at=lambda where: (0, 0)):
    return pl.BlockSpec(shape, lambda i, where: at(where))


def dequantize_kernel(where, levels, scales, out):
    count = scales.shape[0] // 2
    width = out.shape[1] // count
    mine = jnp.where(where[0] == 0, scales[:count], scales[count:]).T
    for b in range(count):
        scale = mine[:, b : b + 1]
        span = slice(b * width, (b + 1) * width)
        out[:, span] = bf16(f32(levels[:, span]) * scale)


def dequantize(where, levels, scales):
    row_count, nh = levels.shape[0], levels.shape[1] // 2
    size = row_count // 3
    return call(
        dequantize_kernel,
        "dequantize",
        12,
        where,
        (3,),
        [
            pl.BlockSpec((size, nh), lambda i, where: (i, where[0])),
            pl.BlockSpec((scales.shape[0], size), lambda i, where: (0, i)),
        ],
        pl.BlockSpec((size, nh), lambda i, where: (i, 0)),
        jax.ShapeDtypeStruct((row_count, nh), jnp.bfloat16),
        [],
        row_count * nh,
        (levels, scales),
    )


def columns(ref, start, size):
    return ref[:, pl.ds(pl.multiple_of(start, 128), size)]


def product(parts, starts, cots, lhs):
    count, size = parts[0].shape[0], lhs.shape[1]

    @pl.when(pl.program_id(0) == 0)
    def _():
        for r, (ref, start) in enumerate(zip(parts, starts)):
            lhs[r * count : (r + 1) * count] = columns(ref, start, size)

    rhs = jnp.concatenate([cot[...] for cot in cots])
    return bf16(
        lax.dot_general(
            lhs[...], rhs, (((0,), (0,)), ((), ())), preferred_element_type=jnp.float32
        )
    )


def gradient_kernel(where, own, sib, pair, psib, cot0, cot1, cot2, cot3, *refs):
    *chunks, lhs, out = refs
    c, yh = where[0], where[1]
    size = lhs.shape[1]
    starts = [base * 2 * size + c * size for base in (yh, yh, 0, 0)]
    out[...] = product((own, sib, pair, psib), starts, (cot0, cot1, cot2, cot3), lhs)
    height = size // 8
    for k, ref in zip(HOPS, chunks):
        row = pl.multiple_of((where[3] + 8 + k) % 8 * height, 16)
        ref[...] = out[pl.ds(row, height)]


def far_kernel(where, own, sib, pair, psib, cot0, cot1, cot2, cot3, up, down, lhs, out):
    c, yh = where[0], where[1]
    window, half = lhs.shape[1], up.shape[0]
    size, chunk, tile = 3 * window, 2 * half, window // 2
    row = (where[3] + 4) % 8 * chunk
    first = jnp.minimum(row // tile * tile, size - window)
    starts = [base * 2 * size + c * size + first for base in (yh, yh, 0, 0)]
    out[...] = product((own, sib, pair, psib), starts, (cot0, cot1, cot2, cot3), lhs)
    skip = pl.multiple_of(row - first, 16)
    up[...] = out[pl.ds(skip, half)]
    down[...] = out[pl.ds(skip + half, half)]


def gradient(where, token_parts, cot_parts, far):
    count, outputs = cot_parts[0].shape
    kh = token_parts[0].shape[1] // 2
    size, width = kh // 2, outputs // 4
    window = size // 3 if far else size
    heights = [size // 16] * 2 if far else [size // 8] * len(HOPS)
    return call(
        far_kernel if far else gradient_kernel,
        "far" if far else "gradient",
        24,
        where,
        (4,),
        [fixed(v.shape) for v in token_parts[:2]]
        + [fixed((count, kh))] * 2
        + [pl.BlockSpec((count, width), lambda i, where: (0, i))] * 4,
        [pl.BlockSpec((height, width), lambda i, where: (0, i)) for height in heights],
        [jax.ShapeDtypeStruct((height, outputs), jnp.bfloat16) for height in heights],
        [pltpu.VMEM((4 * count, window), jnp.bfloat16), pltpu.VMEM((window, width), jnp.bfloat16)],
        8 * count * window * outputs,
        (*token_parts, *cot_parts),
    )


def hop_kernel(*refs):
    *arrived, part, out = refs
    total = f32(part[...])
    for ref in arrived:
        total = total + f32(ref[...])
    out[...] = total.astype(out.dtype)


def first_hop_kernel(arrived, part, out, *, upper):
    half = arrived.shape[0]
    here, there = (slice(0, half), slice(half, 2 * half))[:: 1 if upper else -1]
    out[here] = bf16(f32(part[here]) + f32(arrived[...]))
    out[there] = part[there]


def hop(part, *arrived, kernel=hop_kernel, kind=jnp.bfloat16):
    return pl.pallas_call(
        kernel,
        name="hop",
        out_shape=jax.ShapeDtypeStruct(part.shape, kind),
        compiler_params=pltpu.CompilerParams(vmem_limit_bytes=8 * 2**20),
        cost_estimate=pl.CostEstimate(
            flops=part.size, bytes_accessed=6 * part.size, transcendentals=0
        ),
    )(*arrived, part)


def last_hop_kernel(where, up, down, part, own, *refs):
    *pieces, total = refs
    size = own.shape[0]
    for x in range(4):
        for yh in range(2):
            here = slice((yh * 4 + x) * (size // 2), (yh * 4 + x + 1) * (size // 2))
            there = slice((x * 2 + yh) * (size // 2), (x * 2 + yh + 1) * (size // 2))
            total[there] = f32(part[here]) + f32(up[here]) + f32(down[here])
    for dx, ref in enumerate((own, *pieces)):
        start = pl.multiple_of((where[2] + dx) % 4 * size, 8)
        ref[...] = total[pl.ds(start, size)].astype(ref.dtype)


def last_hop(where, part, up, down):
    size, outputs = part.shape
    width = outputs // 2
    kinds = (jnp.float32, *[jnp.bfloat16] * 3)
    return call(
        last_hop_kernel,
        "last_hop",
        8,
        where,
        (2,),
        [pl.BlockSpec((size, width), lambda i, where: (0, i))] * 3,
        [pl.BlockSpec((size // 4, width), lambda i, where: (0, i)) for _ in kinds],
        [jax.ShapeDtypeStruct((size // 4, outputs), kind) for kind in kinds],
        [pltpu.VMEM((size, width), jnp.float32)],
        2 * part.size,
        (up, down, part),
    )


def sum_kernel(where, own, one, two, three, same, other, total, *, factor):
    size = same.shape[0]
    total[...] = (own[...] + f32(one[...]) + f32(two[...]) + f32(three[...])) * factor
    first, second = bf16(total[:size]), bf16(total[size:])
    yl = where[4]
    same[...] = jnp.where(yl == 0, first, second)
    other[...] = jnp.where(yl == 0, second, first)


def sum_over_x(where, factor, own, *arrived):
    size, outputs = own.shape
    return call(
        functools.partial(sum_kernel, factor=factor),
        "sum_over_x",
        8,
        where,
        (1,),
        [fixed(own.shape)] * 4,
        [fixed((size // 2, outputs))] * 2,
        [jax.ShapeDtypeStruct((size // 2, outputs), jnp.bfloat16)] * 2,
        [pltpu.VMEM((size, outputs), jnp.float32)],
        4 * own.size,
        (own, *arrived),
    )


def forward_kernel(where, own, sib, pair, psib, w0, w1, w2, w3, w4, mine, other, away, lhs):
    yh, x = where[1], where[2]
    count, shard = own.shape[0], w0.shape[0]

    @pl.when(pl.program_id(0) == 0)
    def _():
        for r, (ref, base) in enumerate(((own, yh), (sib, yh), (pair, 0), (psib, 0))):
            for p, step in enumerate(BLOCK_STEPS):
                start = base * 4 * shard + (x + step) % 4 * shard
                lhs[r * count : (r + 1) * count, p * shard : (p + 1) * shard] = columns(
                    ref, start, shard
                )

    far = jnp.where(pl.program_id(0) == 0, w3[...], w4[...])
    rhs = jnp.concatenate([w0[...], w1[...], w2[...], far])
    out = jnp.dot(lhs[...], rhs, preferred_element_type=jnp.float32)
    mine[...] = out[:count]
    other[...] = out[count : 2 * count]
    away[...] = bf16(out[2 * count :])


def forward_parts(where, token_parts, blocks):
    count = token_parts[0].shape[0]
    shard, nh = blocks[0].shape
    width = nh // 2
    kinds = ((count, jnp.float32), (count, jnp.float32), (2 * count, jnp.bfloat16))
    return call(
        forward_kernel,
        "forward",
        28,
        where,
        (2,),
        [fixed(v.shape) for v in token_parts[:2]]
        + [fixed((count, 4 * shard))] * 2
        + [pl.BlockSpec((shard, width), lambda i, where: (0, i))] * 3
        + [fixed((shard, width))] * 2,
        [pl.BlockSpec((height, width), lambda i, where: (0, i)) for height, _ in kinds],
        [jax.ShapeDtypeStruct((height, nh), kind) for height, kind in kinds],
        [pltpu.VMEM((4 * count, 4 * shard), jnp.bfloat16)],
        32 * count * shard * nh,
        (*token_parts, *blocks),
    )


def backward_kernel(where, cot0, cot1, cot2, cot3, w0, w1, w2, w3, w4, mine, give, lhs):
    x = where[2]
    i = pl.program_id(0)
    count = cot0.shape[0]
    size, half = w3.shape

    @pl.when(i == 0)
    def _():
        for r, ref in enumerate((cot0, cot2, cot1, cot3)):
            lhs[r * count : (r + 1) * count] = ref[...]

    far = jnp.concatenate([w3[...], w4[...]], axis=1)
    rhs = jnp.concatenate([w0[...], w1[...], w2[...], far])
    out = lax.dot_general(
        lhs[...], rhs, (((1,), (1,)), ((), ())), preferred_element_type=jnp.float32
    )
    for p, step in enumerate(BLOCK_STEPS):
        start = pl.multiple_of((x + step) % 4 * 3 * size + i * size, 128)
        part = out[:, p * size : (p + 1) * size]
        mine[:, pl.ds(start, size)] = part[: 2 * count]
        give[:, pl.ds(start, size)] = bf16(part[2 * count :])


def backward_parts(where, cot_parts, blocks):
    count = cot_parts[0].shape[0]
    shard, nh = blocks[0].shape
    size = shard // 3
    types = (jnp.float32, jnp.bfloat16)
    return call(
        backward_kernel,
        "backward",
        28,
        where,
        (3,),
        [fixed((count, nh), lambda where: (0, where[0]))] * 4
        + [pl.BlockSpec((size, nh), lambda i, where: (i, 0))] * 3
        + [pl.BlockSpec((size, nh // 2), lambda i, where: (i, 0))] * 2,
        [fixed((2 * count, 4 * shard))] * 2,
        [jax.ShapeDtypeStruct((2 * count, 4 * shard), kind) for kind in types],
        [pltpu.VMEM((4 * count, nh), jnp.bfloat16)],
        32 * count * shard * nh,
        (*cot_parts, *blocks),
    )


def joined(here, there, flag):
    return jnp.where(
        flag == 0, jnp.concatenate([here, there], axis=1), jnp.concatenate([there, here], axis=1)
    )


def on_device(tokens, cotangent, levels, scales):
    z, yl, c, yh, x = (lax.axis_index(name) for name in AXES)
    where = jnp.stack([c, yh, x, window(z, c, yh), yl]).astype(jnp.int32)
    count = tokens.shape[0]
    factor = float(count * 256) ** -0.5

    cot_pair = send(cotangent, PAIR)
    kh = tokens.shape[1] // 2

    own = dequantize(where, levels, scales.T)
    left, right = send(own, X_UP), send(own, X_DOWN)

    token_out = lax.dynamic_slice_in_dim(after(tokens, own), (1 - yh) * kh, kh, 1)
    token_pair = send(token_out, PAIR)
    cot_own, token_own = after((cotangent, tokens), token_out)
    cot_sib, token_sib = send(cot_own, CORE), send(token_own, CORE)
    token_parts = (tokens, token_sib, token_pair, send(token_pair, CORE))
    cot_parts = (cotangent, cot_sib, cot_pair, send(cot_pair, CORE))

    up, down = gradient(where, token_parts, after(cot_parts, left, right), True)
    grad = gradient(where, token_parts, after(cot_parts, up), False)
    half = own.shape[1] // 2
    up, down = send(up, Z_UP), send(down, Z_DOWN)
    up = hop(grad[0], up, kernel=functools.partial(first_hop_kernel, upper=True))
    down = hop(grad[1], down, kernel=functools.partial(first_hop_kernel, upper=False))
    left, right = after((left, right), up, down)
    blocks = (own, left, right, send(left[:, :half], X_UP), send(right[:, half:], X_DOWN))
    up, down = send(up, Z_UP), send(down, Z_DOWN)
    up, down = hop(grad[2], up), hop(grad[3], down)
    mine, other, away = forward_parts(where, token_parts, after(blocks, up, down))
    up, down = send(up, Z_UP), send(down, Z_DOWN)
    back = f32(send(away, PAIR))
    grad = after(grad, away)
    up, down = hop(grad[4], up), hop(grad[5], down)
    part, give = backward_parts(where, cot_parts, after(blocks, up, down))
    up, down = send(up, Z_UP), send(down, Z_DOWN)
    give = send(give, CORE)
    own_piece, *pieces = last_hop(where, after(grad[6], part), up, down)
    arrived = [send(piece, to) for piece, to in zip(pieces, X_STEPS)]
    back = after(back, own_piece)
    here = bf16(mine + back[:count])
    there = send(bf16(other + back[count:]), CORE)
    part, give = after((part, give), own_piece)
    part = part + f32(give)
    grad_here, grad_away = bf16(part[:count]), bf16(part[count:])
    grad_there = send(grad_away, PAIR)
    same, swapped = sum_over_x(where, factor, own_piece, *after(arrived, grad_away))
    got = send(same, OWNERS[0]), send(swapped, OWNERS[1])
    forward = joined(after(here, same), there, c)
    grad_input = joined(after(grad_here, same), grad_there, yh)
    one, two = after(got, forward, grad_input)
    return forward, grad_input, f32(one) + f32(two)


def solution(mesh):
    fine = Mesh(mesh.devices.reshape(SIZES), AXES)
    token_spec, node_spec = P(AXES, None), P(("yh", "x"), None)
    return jax.shard_map(
        on_device,
        mesh=fine,
        in_specs=(token_spec, token_spec, node_spec, node_spec),
        out_specs=(token_spec, token_spec, token_spec),
        check_vma=False,
    )
```

```python
import functools
import math

import jax
import jax.numpy as jnp
from jax import lax
from jax.experimental import pallas as pl
from jax.experimental.pallas import tpu as pltpu
from jax.sharding import Mesh, PartitionSpec as P

AXES = ("z", "yl", "c", "yh", "x")
SIZES = (8, 2, 2, 2, 4)
BLOCK_STEPS = (0, 3, 1, 2)
HOPS = (3, -3, 2, -2, 1, -1, 0)


def table(move):
    pairs = []
    for z in range(8):
        for yl in range(2):
            for c in range(2):
                for yh in range(2):
                    for x in range(4):
                        pairs.append((place(z, yl, c, yh, x), place(*move(z, yl, c, yh, x))))
    return pairs


def place(z, yl, c, yh, x):
    return (((z % 8 * 2 + yl % 2) * 2 + c % 2) * 2 + yh % 2) * 4 + x % 4


def window(z, c, yh):
    return (z + 11 - 4 * yh - 2 * c) % 8


def owner(z, yl, c, yh, x, message):
    chunk = window(z, c, yh)
    return 4 * yh + 2 * c + chunk // 4, chunk % 4 // 2, chunk % 2, yl ^ message, x


X_UP = table(lambda z, yl, c, yh, x: (z, yl, c, yh, x + 1))
X_DOWN = table(lambda z, yl, c, yh, x: (z, yl, c, yh, x - 1))
X_STEPS = [table(lambda z, yl, c, yh, x: (z, yl, c, yh, x + dx)) for dx in (1, 2, 3)]
Z_UP = table(lambda z, yl, c, yh, x: (z + 1, yl, c, yh, x))
Z_DOWN = table(lambda z, yl, c, yh, x: (z - 1, yl, c, yh, x))
CORE = table(lambda z, yl, c, yh, x: (z, yl, c + 1, yh, x))
PAIR = table(lambda z, yl, c, yh, x: (z, yl + 1, c, yh + 1, x))
OWNERS = [
    table(lambda z, yl, c, yh, x: owner(z, yl, c, yh, x, message)) for message in range(2)
]


def send(value, pairs):
    return lax.ppermute(value, AXES, pairs)


def after(values, *earlier):
    return lax.optimization_barrier((values, earlier))[0]


def f32(value):
    return value.astype(jnp.float32)


def bf16(value):
    return value.astype(jnp.bfloat16)


def call(kernel, name, mib, where, grid, in_specs, out_specs, out_shape, scratch, flops, operands):
    moved = sum(v.size * v.dtype.itemsize for v in operands)
    moved += sum(math.prod(v.shape) * v.dtype.itemsize for v in jax.tree.leaves(out_shape))
    return pl.pallas_call(
        kernel,
        name=name,
        grid_spec=pltpu.PrefetchScalarGridSpec(
            num_scalar_prefetch=1,
            grid=grid,
            in_specs=in_specs,
            out_specs=out_specs,
            scratch_shapes=scratch,
        ),
        out_shape=out_shape,
        compiler_params=pltpu.CompilerParams(vmem_limit_bytes=mib * 2**20),
        cost_estimate=pl.CostEstimate(flops=flops, bytes_accessed=moved, transcendentals=0),
    )(where, *operands)


def fixed(shape, at=lambda where: (0, 0)):
    return pl.BlockSpec(shape, lambda i, where: at(where))


def dequantize_kernel(where, levels, scales, out):
    count = scales.shape[0] // 2
    width = out.shape[1] // count
    mine = jnp.where(where[0] == 0, scales[:count], scales[count:]).T
    for b in range(count):
        scale = mine[:, b : b + 1]
        span = slice(b * width, (b + 1) * width)
        out[:, span] = bf16(f32(levels[:, span]) * scale)


def dequantize(where, levels, scales):
    row_count, nh = levels.shape[0], levels.shape[1] // 2
    size = row_count // 3
    return call(
        dequantize_kernel,
        "dequantize",
        12,
        where,
        (3,),
        [
            pl.BlockSpec((size, nh), lambda i, where: (i, where[0])),
            pl.BlockSpec((scales.shape[0], size), lambda i, where: (0, i)),
        ],
        pl.BlockSpec((size, nh), lambda i, where: (i, 0)),
        jax.ShapeDtypeStruct((row_count, nh), jnp.bfloat16),
        [],
        row_count * nh,
        (levels, scales),
    )


def columns(ref, start, size):
    return ref[:, pl.ds(pl.multiple_of(start, 128), size)]


def product(parts, starts, cots, lhs):
    count, size = parts[0].shape[0], lhs.shape[1]

    @pl.when(pl.program_id(0) == 0)
    def _():
        for r, (ref, start) in enumerate(zip(parts, starts)):
            lhs[r * count : (r + 1) * count] = columns(ref, start, size)

    rhs = jnp.concatenate([cot[...] for cot in cots])
    return bf16(
        lax.dot_general(
            lhs[...], rhs, (((0,), (0,)), ((), ())), preferred_element_type=jnp.float32
        )
    )


def gradient_kernel(where, own, sib, pair, psib, cot0, cot1, cot2, cot3, *refs):
    *chunks, lhs, out = refs
    c, yh = where[0], where[1]
    size = lhs.shape[1]
    starts = [base * 2 * size + c * size for base in (yh, yh, 0, 0)]
    out[...] = product((own, sib, pair, psib), starts, (cot0, cot1, cot2, cot3), lhs)
    height = size // 8
    for k, ref in zip(HOPS, chunks):
        row = pl.multiple_of((where[3] + 8 + k) % 8 * height, 16)
        ref[...] = out[pl.ds(row, height)]


def far_kernel(where, own, sib, pair, psib, cot0, cot1, cot2, cot3, up, down, lhs, out):
    c, yh = where[0], where[1]
    window, half = lhs.shape[1], up.shape[0]
    size, chunk, tile = 3 * window, 2 * half, window // 2
    row = (where[3] + 4) % 8 * chunk
    first = jnp.minimum(row // tile * tile, size - window)
    starts = [base * 2 * size + c * size + first for base in (yh, yh, 0, 0)]
    out[...] = product((own, sib, pair, psib), starts, (cot0, cot1, cot2, cot3), lhs)
    skip = pl.multiple_of(row - first, 16)
    up[...] = out[pl.ds(skip, half)]
    down[...] = out[pl.ds(skip + half, half)]


def gradient(where, token_parts, cot_parts, far):
    count, outputs = cot_parts[0].shape
    kh = token_parts[0].shape[1] // 2
    size, width = kh // 2, outputs // 4
    window = size // 3 if far else size
    heights = [size // 16] * 2 if far else [size // 8] * len(HOPS)
    return call(
        far_kernel if far else gradient_kernel,
        "far" if far else "gradient",
        24,
        where,
        (4,),
        [fixed(v.shape) for v in token_parts[:2]]
        + [fixed((count, kh))] * 2
        + [pl.BlockSpec((count, width), lambda i, where: (0, i))] * 4,
        [pl.BlockSpec((height, width), lambda i, where: (0, i)) for height in heights],
        [jax.ShapeDtypeStruct((height, outputs), jnp.bfloat16) for height in heights],
        [pltpu.VMEM((4 * count, window), jnp.bfloat16), pltpu.VMEM((window, width), jnp.bfloat16)],
        8 * count * window * outputs,
        (*token_parts, *cot_parts),
    )


def hop_kernel(*refs):
    *arrived, part, out = refs
    total = f32(part[...])
    for ref in arrived:
        total = total + f32(ref[...])
    out[...] = total.astype(out.dtype)


def first_hop_kernel(arrived, part, out, *, upper):
    half = arrived.shape[0]
    here, there = (slice(0, half), slice(half, 2 * half))[:: 1 if upper else -1]
    out[here] = bf16(f32(part[here]) + f32(arrived[...]))
    out[there] = part[there]


def hop(part, *arrived, kernel=hop_kernel, kind=jnp.bfloat16):
    return pl.pallas_call(
        kernel,
        name="hop",
        out_shape=jax.ShapeDtypeStruct(part.shape, kind),
        compiler_params=pltpu.CompilerParams(vmem_limit_bytes=8 * 2**20),
        cost_estimate=pl.CostEstimate(
            flops=part.size, bytes_accessed=6 * part.size, transcendentals=0
        ),
    )(*arrived, part)


def last_hop_kernel(where, up, down, part, own, *refs):
    *pieces, total = refs
    size = own.shape[0]
    for x in range(4):
        for yh in range(2):
            here = slice((yh * 4 + x) * (size // 2), (yh * 4 + x + 1) * (size // 2))
            there = slice((x * 2 + yh) * (size // 2), (x * 2 + yh + 1) * (size // 2))
            total[there] = f32(part[here]) + f32(up[here]) + f32(down[here])
    for dx, ref in enumerate((own, *pieces)):
        start = pl.multiple_of((where[2] + dx) % 4 * size, 8)
        ref[...] = total[pl.ds(start, size)].astype(ref.dtype)


def last_hop(where, part, up, down):
    size, outputs = part.shape
    width = outputs // 2
    kinds = (jnp.float32, *[jnp.bfloat16] * 3)
    return call(
        last_hop_kernel,
        "last_hop",
        8,
        where,
        (2,),
        [pl.BlockSpec((size, width), lambda i, where: (0, i))] * 3,
        [pl.BlockSpec((size // 4, width), lambda i, where: (0, i)) for _ in kinds],
        [jax.ShapeDtypeStruct((size // 4, outputs), kind) for kind in kinds],
        [pltpu.VMEM((size, width), jnp.float32)],
        2 * part.size,
        (up, down, part),
    )


def sum_kernel(where, own, one, two, three, same, other, total, *, factor):
    size = same.shape[0]
    total[...] = (own[...] + f32(one[...]) + f32(two[...]) + f32(three[...])) * factor
    first, second = bf16(total[:size]), bf16(total[size:])
    yl = where[4]
    same[...] = jnp.where(yl == 0, first, second)
    other[...] = jnp.where(yl == 0, second, first)


def sum_over_x(where, factor, own, *arrived):
    size, outputs = own.shape
    return call(
        functools.partial(sum_kernel, factor=factor),
        "sum_over_x",
        8,
        where,
        (1,),
        [fixed(own.shape)] * 4,
        [fixed((size // 2, outputs))] * 2,
        [jax.ShapeDtypeStruct((size // 2, outputs), jnp.bfloat16)] * 2,
        [pltpu.VMEM((size, outputs), jnp.float32)],
        4 * own.size,
        (own, *arrived),
    )


def forward_kernel(where, own, sib, pair, psib, w0, w1, w2, w3, w4, mine, other, away, lhs):
    yh, x = where[1], where[2]
    count, shard = own.shape[0], w0.shape[0]

    @pl.when(pl.program_id(0) == 0)
    def _():
        for r, (ref, base) in enumerate(((own, yh), (sib, yh), (pair, 0), (psib, 0))):
            for p, step in enumerate(BLOCK_STEPS):
                start = base * 4 * shard + (x + step) % 4 * shard
                lhs[r * count : (r + 1) * count, p * shard : (p + 1) * shard] = columns(
                    ref, start, shard
                )

    far = jnp.where(pl.program_id(0) == 0, w3[...], w4[...])
    rhs = jnp.concatenate([w0[...], w1[...], w2[...], far])
    out = jnp.dot(lhs[...], rhs, preferred_element_type=jnp.float32)
    mine[...] = out[:count]
    other[...] = out[count : 2 * count]
    away[...] = bf16(out[2 * count :])


def forward_parts(where, token_parts, blocks):
    count = token_parts[0].shape[0]
    shard, nh = blocks[0].shape
    width = nh // 2
    kinds = ((count, jnp.float32), (count, jnp.float32), (2 * count, jnp.bfloat16))
    return call(
        forward_kernel,
        "forward",
        28,
        where,
        (2,),
        [fixed(v.shape) for v in token_parts[:2]]
        + [fixed((count, 4 * shard))] * 2
        + [pl.BlockSpec((shard, width), lambda i, where: (0, i))] * 3
        + [fixed((shard, width))] * 2,
        [pl.BlockSpec((height, width), lambda i, where: (0, i)) for height, _ in kinds],
        [jax.ShapeDtypeStruct((height, nh), kind) for height, kind in kinds],
        [pltpu.VMEM((4 * count, 4 * shard), jnp.bfloat16)],
        32 * count * shard * nh,
        (*token_parts, *blocks),
    )


def backward_kernel(where, cot0, cot1, cot2, cot3, w0, w1, w2, w3, w4, mine, give, lhs):
    x = where[2]
    i = pl.program_id(0)
    count = cot0.shape[0]
    size, half = w3.shape

    @pl.when(i == 0)
    def _():
        for r, ref in enumerate((cot0, cot2, cot1, cot3)):
            lhs[r * count : (r + 1) * count] = ref[...]

    far = jnp.concatenate([w3[...], w4[...]], axis=1)
    rhs = jnp.concatenate([w0[...], w1[...], w2[...], far])
    out = lax.dot_general(
        lhs[...], rhs, (((1,), (1,)), ((), ())), preferred_element_type=jnp.float32
    )
    for p, step in enumerate(BLOCK_STEPS):
        start = pl.multiple_of((x + step) % 4 * 3 * size + i * size, 128)
        part = out[:, p * size : (p + 1) * size]
        mine[:, pl.ds(start, size)] = part[: 2 * count]
        give[:, pl.ds(start, size)] = bf16(part[2 * count :])


def backward_parts(where, cot_parts, blocks):
    count = cot_parts[0].shape[0]
    shard, nh = blocks[0].shape
    size = shard // 3
    types = (jnp.float32, jnp.bfloat16)
    return call(
        backward_kernel,
        "backward",
        28,
        where,
        (3,),
        [fixed((count, nh), lambda where: (0, where[0]))] * 4
        + [pl.BlockSpec((size, nh), lambda i, where: (i, 0))] * 3
        + [pl.BlockSpec((size, nh // 2), lambda i, where: (i, 0))] * 2,
        [fixed((2 * count, 4 * shard))] * 2,
        [jax.ShapeDtypeStruct((2 * count, 4 * shard), kind) for kind in types],
        [pltpu.VMEM((4 * count, nh), jnp.bfloat16)],
        32 * count * shard * nh,
        (*cot_parts, *blocks),
    )


def joined(here, there, flag):
    return jnp.where(
        flag == 0, jnp.concatenate([here, there], axis=1), jnp.concatenate([there, here], axis=1)
    )


def on_device(tokens, cotangent, levels, scales):
    z, yl, c, yh, x = (lax.axis_index(name) for name in AXES)
    where = jnp.stack([c, yh, x, window(z, c, yh), yl]).astype(jnp.int32)
    count = tokens.shape[0]
    factor = float(count * 256) ** -0.5

    cot_pair = send(cotangent, PAIR)
    kh = tokens.shape[1] // 2

    own = dequantize(where, levels, scales.T)
    left, right = send(own, X_UP), send(own, X_DOWN)

    token_out = lax.dynamic_slice_in_dim(after(tokens, own), (1 - yh) * kh, kh, 1)
    token_pair = send(token_out, PAIR)
    cot_own, token_own = after((cotangent, tokens), token_out)
    cot_sib, token_sib = send(cot_own, CORE), send(token_own, CORE)
    token_parts = (tokens, token_sib, token_pair, send(token_pair, CORE))
    cot_parts = (cotangent, cot_sib, cot_pair, send(cot_pair, CORE))

    up, down = gradient(where, token_parts, cot_parts, True)
    grad = gradient(where, token_parts, after(cot_parts, up, left, right), False)
    half = own.shape[1] // 2
    up, down = send(up, Z_UP), send(down, Z_DOWN)
    up = hop(grad[0], up, kernel=functools.partial(first_hop_kernel, upper=True))
    down = hop(grad[1], down, kernel=functools.partial(first_hop_kernel, upper=False))
    left, right = after((left, right), up, down)
    blocks = (own, left, right, send(left[:, :half], X_UP), send(right[:, half:], X_DOWN))
    up, down = send(up, Z_UP), send(down, Z_DOWN)
    up, down = hop(grad[2], up), hop(grad[3], down)
    mine, other, away = forward_parts(where, token_parts, after(blocks, up, down))
    up, down = send(up, Z_UP), send(down, Z_DOWN)
    back = f32(send(away, PAIR))
    grad = after(grad, away)
    up, down = hop(grad[4], up), hop(grad[5], down)
    part, give = backward_parts(where, cot_parts, after(blocks, up, down))
    up, down = send(up, Z_UP), send(down, Z_DOWN)
    give = send(give, CORE)
    own_piece, *pieces = last_hop(where, after(grad[6], part), up, down)
    arrived = [send(piece, to) for piece, to in zip(pieces, X_STEPS)]
    back = after(back, own_piece)
    here = bf16(mine + back[:count])
    there = send(bf16(other + back[count:]), CORE)
    part, give = after((part, give), own_piece)
    part = part + f32(give)
    grad_here, grad_away = bf16(part[:count]), bf16(part[count:])
    grad_there = send(grad_away, PAIR)
    same, swapped = sum_over_x(where, factor, own_piece, *after(arrived, grad_away))
    got = send(same, OWNERS[0]), send(swapped, OWNERS[1])
    forward = joined(after(here, same), there, c)
    grad_input = joined(after(grad_here, same), grad_there, yh)
    one, two = after(got, forward, grad_input)
    return forward, grad_input, f32(one) + f32(two)


def solution(mesh):
    fine = Mesh(mesh.devices.reshape(SIZES), AXES)
    token_spec, node_spec = P(AXES, None), P(("yh", "x"), None)
    return jax.shard_map(
        on_device,
        mesh=fine,
        in_specs=(token_spec, token_spec, node_spec, node_spec),
        out_specs=(token_spec, token_spec, token_spec),
        check_vma=False,
    )
```

```python
import functools
import math

import jax
import jax.numpy as jnp
from jax import lax
from jax.experimental import pallas as pl
from jax.experimental.pallas import tpu as pltpu
from jax.sharding import Mesh, PartitionSpec as P

AXES = ("z", "yl", "c", "yh", "x")
SIZES = (8, 2, 2, 2, 4)
BLOCK_STEPS = (0, 3, 1, 2)
HOPS = (3, -3, 2, -2, 1, -1, 0)


def table(move):
    pairs = []
    for z in range(8):
        for yl in range(2):
            for c in range(2):
                for yh in range(2):
                    for x in range(4):
                        pairs.append((place(z, yl, c, yh, x), place(*move(z, yl, c, yh, x))))
    return pairs


def place(z, yl, c, yh, x):
    return (((z % 8 * 2 + yl % 2) * 2 + c % 2) * 2 + yh % 2) * 4 + x % 4


def window(z, c, yh):
    return (z + 11 - 4 * yh - 2 * c) % 8


def owner(z, yl, c, yh, x, message):
    chunk = window(z, c, yh)
    return 4 * yh + 2 * c + chunk // 4, chunk % 4 // 2, chunk % 2, yl ^ message, x


X_UP = table(lambda z, yl, c, yh, x: (z, yl, c, yh, x + 1))
X_DOWN = table(lambda z, yl, c, yh, x: (z, yl, c, yh, x - 1))
X_STEPS = [table(lambda z, yl, c, yh, x: (z, yl, c, yh, x + dx)) for dx in (1, 2, 3)]
Z_UP = table(lambda z, yl, c, yh, x: (z + 1, yl, c, yh, x))
Z_DOWN = table(lambda z, yl, c, yh, x: (z - 1, yl, c, yh, x))
CORE = table(lambda z, yl, c, yh, x: (z, yl, c + 1, yh, x))
PAIR = table(lambda z, yl, c, yh, x: (z, yl + 1, c, yh + 1, x))
OWNERS = [
    table(lambda z, yl, c, yh, x: owner(z, yl, c, yh, x, message)) for message in range(2)
]


def send(value, pairs):
    return lax.ppermute(value, AXES, pairs)


def after(values, *earlier):
    return lax.optimization_barrier((values, earlier))[0]


def f32(value):
    return value.astype(jnp.float32)


def bf16(value):
    return value.astype(jnp.bfloat16)


def call(kernel, name, mib, where, grid, in_specs, out_specs, out_shape, scratch, flops, operands):
    moved = sum(v.size * v.dtype.itemsize for v in operands)
    moved += sum(math.prod(v.shape) * v.dtype.itemsize for v in jax.tree.leaves(out_shape))
    return pl.pallas_call(
        kernel,
        name=name,
        grid_spec=pltpu.PrefetchScalarGridSpec(
            num_scalar_prefetch=1,
            grid=grid,
            in_specs=in_specs,
            out_specs=out_specs,
            scratch_shapes=scratch,
        ),
        out_shape=out_shape,
        compiler_params=pltpu.CompilerParams(vmem_limit_bytes=mib * 2**20),
        cost_estimate=pl.CostEstimate(flops=flops, bytes_accessed=moved, transcendentals=0),
    )(where, *operands)


def fixed(shape, at=lambda where: (0, 0)):
    return pl.BlockSpec(shape, lambda i, where: at(where))


def dequantize_kernel(where, levels, scales, out):
    count = scales.shape[0] // 2
    width = out.shape[1] // count
    mine = jnp.where(where[0] == 0, scales[:count], scales[count:]).T
    for b in range(count):
        scale = mine[:, b : b + 1]
        span = slice(b * width, (b + 1) * width)
        out[:, span] = bf16(f32(levels[:, span]) * scale)


def dequantize(where, levels, scales):
    row_count, nh = levels.shape[0], levels.shape[1] // 2
    size = row_count // 3
    return call(
        dequantize_kernel,
        "dequantize",
        12,
        where,
        (3,),
        [
            pl.BlockSpec((size, nh), lambda i, where: (i, where[0])),
            pl.BlockSpec((scales.shape[0], size), lambda i, where: (0, i)),
        ],
        pl.BlockSpec((size, nh), lambda i, where: (i, 0)),
        jax.ShapeDtypeStruct((row_count, nh), jnp.bfloat16),
        [],
        row_count * nh,
        (levels, scales),
    )


def columns(ref, start, size):
    return ref[:, pl.ds(pl.multiple_of(start, 128), size)]


def product(parts, starts, cots, lhs):
    count, size = parts[0].shape[0], lhs.shape[1]

    @pl.when(pl.program_id(0) == 0)
    def _():
        for r, (ref, start) in enumerate(zip(parts, starts)):
            lhs[r * count : (r + 1) * count] = columns(ref, start, size)

    rhs = jnp.concatenate([cot[...] for cot in cots])
    return bf16(
        lax.dot_general(
            lhs[...], rhs, (((0,), (0,)), ((), ())), preferred_element_type=jnp.float32
        )
    )


def gradient_kernel(where, own, sib, pair, psib, cot0, cot1, cot2, cot3, *refs):
    *chunks, lhs, out = refs
    c, yh = where[0], where[1]
    size = lhs.shape[1]
    starts = [base * 2 * size + c * size for base in (yh, yh, 0, 0)]
    out[...] = product((own, sib, pair, psib), starts, (cot0, cot1, cot2, cot3), lhs)
    height = size // 8
    for k, ref in zip(HOPS, chunks):
        row = pl.multiple_of((where[3] + 8 + k) % 8 * height, 16)
        ref[...] = out[pl.ds(row, height)]


def far_kernel(where, own, sib, pair, psib, cot0, cot1, cot2, cot3, up, down, lhs, out):
    c, yh = where[0], where[1]
    window, half = lhs.shape[1], up.shape[0]
    size, chunk, tile = 3 * window, 2 * half, window // 2
    row = (where[3] + 4) % 8 * chunk
    first = jnp.minimum(row // tile * tile, size - window)
    starts = [base * 2 * size + c * size + first for base in (yh, yh, 0, 0)]
    out[...] = product((own, sib, pair, psib), starts, (cot0, cot1, cot2, cot3), lhs)
    skip = pl.multiple_of(row - first, 16)
    up[...] = out[pl.ds(skip, half)]
    down[...] = out[pl.ds(skip + half, half)]


def gradient(where, token_parts, cot_parts, far):
    count, outputs = cot_parts[0].shape
    kh = token_parts[0].shape[1] // 2
    size, width = kh // 2, outputs // 4
    window = size // 3 if far else size
    heights = [size // 16] * 2 if far else [size // 8] * len(HOPS)
    return call(
        far_kernel if far else gradient_kernel,
        "far" if far else "gradient",
        24,
        where,
        (4,),
        [fixed(v.shape) for v in token_parts[:2]]
        + [fixed((count, kh))] * 2
        + [pl.BlockSpec((count, width), lambda i, where: (0, i))] * 4,
        [pl.BlockSpec((height, width), lambda i, where: (0, i)) for height in heights],
        [jax.ShapeDtypeStruct((height, outputs), jnp.bfloat16) for height in heights],
        [pltpu.VMEM((4 * count, window), jnp.bfloat16), pltpu.VMEM((window, width), jnp.bfloat16)],
        8 * count * window * outputs,
        (*token_parts, *cot_parts),
    )


def hop_kernel(*refs):
    *arrived, part, out = refs
    total = f32(part[...])
    for ref in arrived:
        total = total + f32(ref[...])
    out[...] = total.astype(out.dtype)


def first_hop_kernel(arrived, part, out, *, upper):
    half = arrived.shape[0]
    here, there = (slice(0, half), slice(half, 2 * half))[:: 1 if upper else -1]
    out[here] = bf16(f32(part[here]) + f32(arrived[...]))
    out[there] = part[there]


def hop(part, *arrived, kernel=hop_kernel, kind=jnp.bfloat16):
    return pl.pallas_call(
        kernel,
        name="hop",
        out_shape=jax.ShapeDtypeStruct(part.shape, kind),
        compiler_params=pltpu.CompilerParams(vmem_limit_bytes=8 * 2**20),
        cost_estimate=pl.CostEstimate(
            flops=part.size, bytes_accessed=6 * part.size, transcendentals=0
        ),
    )(*arrived, part)


def last_hop_kernel(where, up, down, part, own, *refs):
    *pieces, total = refs
    size = own.shape[0]
    for x in range(4):
        for yh in range(2):
            here = slice((yh * 4 + x) * (size // 2), (yh * 4 + x + 1) * (size // 2))
            there = slice((x * 2 + yh) * (size // 2), (x * 2 + yh + 1) * (size // 2))
            total[there] = f32(part[here]) + f32(up[here]) + f32(down[here])
    for dx, ref in enumerate((own, *pieces)):
        start = pl.multiple_of((where[2] + dx) % 4 * size, 8)
        ref[...] = total[pl.ds(start, size)].astype(ref.dtype)


def last_hop(where, part, up, down):
    size, outputs = part.shape
    width = outputs // 2
    kinds = (jnp.float32, *[jnp.bfloat16] * 3)
    return call(
        last_hop_kernel,
        "last_hop",
        8,
        where,
        (2,),
        [pl.BlockSpec((size, width), lambda i, where: (0, i))] * 3,
        [pl.BlockSpec((size // 4, width), lambda i, where: (0, i)) for _ in kinds],
        [jax.ShapeDtypeStruct((size // 4, outputs), kind) for kind in kinds],
        [pltpu.VMEM((size, width), jnp.float32)],
        2 * part.size,
        (up, down, part),
    )


def sum_kernel(where, own, one, two, three, same, other, total, *, factor):
    size = same.shape[0]
    total[...] = (own[...] + f32(one[...]) + f32(two[...]) + f32(three[...])) * factor
    first, second = bf16(total[:size]), bf16(total[size:])
    yl = where[4]
    same[...] = jnp.where(yl == 0, first, second)
    other[...] = jnp.where(yl == 0, second, first)


def sum_over_x(where, factor, own, *arrived):
    size, outputs = own.shape
    return call(
        functools.partial(sum_kernel, factor=factor),
        "sum_over_x",
        8,
        where,
        (1,),
        [fixed(own.shape)] * 4,
        [fixed((size // 2, outputs))] * 2,
        [jax.ShapeDtypeStruct((size // 2, outputs), jnp.bfloat16)] * 2,
        [pltpu.VMEM((size, outputs), jnp.float32)],
        4 * own.size,
        (own, *arrived),
    )


def forward_kernel(where, own, sib, pair, psib, w0, w1, w2, w3, w4, mine, other, away, lhs):
    yh, x = where[1], where[2]
    count, shard = own.shape[0], w0.shape[0]

    @pl.when(pl.program_id(0) == 0)
    def _():
        for r, (ref, base) in enumerate(((own, yh), (sib, yh), (pair, 0), (psib, 0))):
            for p, step in enumerate(BLOCK_STEPS):
                start = base * 4 * shard + (x + step) % 4 * shard
                lhs[r * count : (r + 1) * count, p * shard : (p + 1) * shard] = columns(
                    ref, start, shard
                )

    far = jnp.where(pl.program_id(0) == 0, w3[...], w4[...])
    rhs = jnp.concatenate([w0[...], w1[...], w2[...], far])
    out = jnp.dot(lhs[...], rhs, preferred_element_type=jnp.float32)
    mine[...] = out[:count]
    other[...] = out[count : 2 * count]
    away[...] = bf16(out[2 * count :])


def forward_parts(where, token_parts, blocks):
    count = token_parts[0].shape[0]
    shard, nh = blocks[0].shape
    width = nh // 2
    kinds = ((count, jnp.float32), (count, jnp.float32), (2 * count, jnp.bfloat16))
    return call(
        forward_kernel,
        "forward",
        28,
        where,
        (2,),
        [fixed(v.shape) for v in token_parts[:2]]
        + [fixed((count, 4 * shard))] * 2
        + [pl.BlockSpec((shard, width), lambda i, where: (0, i))] * 3
        + [fixed((shard, width))] * 2,
        [pl.BlockSpec((height, width), lambda i, where: (0, i)) for height, _ in kinds],
        [jax.ShapeDtypeStruct((height, nh), kind) for height, kind in kinds],
        [pltpu.VMEM((4 * count, 4 * shard), jnp.bfloat16)],
        32 * count * shard * nh,
        (*token_parts, *blocks),
    )


def backward_kernel(where, cot0, cot1, cot2, cot3, w0, w1, w2, w3, w4, mine, give, lhs):
    x = where[2]
    i = pl.program_id(0)
    count = cot0.shape[0]
    size, half = w3.shape

    @pl.when(i == 0)
    def _():
        for r, ref in enumerate((cot0, cot2, cot1, cot3)):
            lhs[r * count : (r + 1) * count] = ref[...]

    far = jnp.concatenate([w3[...], w4[...]], axis=1)
    rhs = jnp.concatenate([w0[...], w1[...], w2[...], far])
    out = lax.dot_general(
        lhs[...], rhs, (((1,), (1,)), ((), ())), preferred_element_type=jnp.float32
    )
    for p, step in enumerate(BLOCK_STEPS):
        start = pl.multiple_of((x + step) % 4 * 3 * size + i * size, 128)
        part = out[:, p * size : (p + 1) * size]
        mine[:, pl.ds(start, size)] = part[: 2 * count]
        give[:, pl.ds(start, size)] = bf16(part[2 * count :])


def backward_parts(where, cot_parts, blocks):
    count = cot_parts[0].shape[0]
    shard, nh = blocks[0].shape
    size = shard // 3
    types = (jnp.float32, jnp.bfloat16)
    return call(
        backward_kernel,
        "backward",
        28,
        where,
        (3,),
        [fixed((count, nh), lambda where: (0, where[0]))] * 4
        + [pl.BlockSpec((size, nh), lambda i, where: (i, 0))] * 3
        + [pl.BlockSpec((size, nh // 2), lambda i, where: (i, 0))] * 2,
        [fixed((2 * count, 4 * shard))] * 2,
        [jax.ShapeDtypeStruct((2 * count, 4 * shard), kind) for kind in types],
        [pltpu.VMEM((4 * count, nh), jnp.bfloat16)],
        32 * count * shard * nh,
        (*cot_parts, *blocks),
    )


def joined(here, there, flag):
    return jnp.where(
        flag == 0, jnp.concatenate([here, there], axis=1), jnp.concatenate([there, here], axis=1)
    )


def on_device(tokens, cotangent, levels, scales):
    z, yl, c, yh, x = (lax.axis_index(name) for name in AXES)
    where = jnp.stack([c, yh, x, window(z, c, yh), yl]).astype(jnp.int32)
    count = tokens.shape[0]
    factor = float(count * 256) ** -0.5

    cot_pair = send(cotangent, PAIR)
    kh = tokens.shape[1] // 2

    own = dequantize(where, levels, scales.T)
    left, right = send(own, X_UP), send(own, X_DOWN)

    token_out = lax.dynamic_slice_in_dim(after(tokens, own), (1 - yh) * kh, kh, 1)
    token_pair = send(token_out, PAIR)
    cot_own, token_own = after((cotangent, tokens), token_out)
    cot_sib, token_sib = send(cot_own, CORE), send(token_own, CORE)
    token_parts = (tokens, token_sib, token_pair, send(token_pair, CORE))
    cot_parts = (cotangent, cot_sib, cot_pair, send(cot_pair, CORE))

    up, down = gradient(where, token_parts, after(cot_parts, cotangent), True)
    grad = gradient(where, token_parts, after(cot_parts, up, left, right), False)
    half = own.shape[1] // 2
    up, down = send(up, Z_UP), send(down, Z_DOWN)
    up = hop(grad[0], up, kernel=functools.partial(first_hop_kernel, upper=True))
    down = hop(grad[1], down, kernel=functools.partial(first_hop_kernel, upper=False))
    left, right = after((left, right), up, down)
    blocks = (own, left, right, send(left[:, :half], X_UP), send(right[:, half:], X_DOWN))
    up, down = send(up, Z_UP), send(down, Z_DOWN)
    up, down = hop(grad[2], up), hop(grad[3], down)
    mine, other, away = forward_parts(where, token_parts, after(blocks, up, down))
    up, down = send(up, Z_UP), send(down, Z_DOWN)
    back = f32(send(away, PAIR))
    grad = after(grad, away)
    up, down = hop(grad[4], up), hop(grad[5], down)
    part, give = backward_parts(where, cot_parts, after(blocks, up, down))
    up, down = send(up, Z_UP), send(down, Z_DOWN)
    give = send(give, CORE)
    own_piece, *pieces = last_hop(where, after(grad[6], part), up, down)
    arrived = [send(piece, to) for piece, to in zip(pieces, X_STEPS)]
    back = after(back, own_piece)
    here = bf16(mine + back[:count])
    there = send(bf16(other + back[count:]), CORE)
    part, give = after((part, give), own_piece)
    part = part + f32(give)
    grad_here, grad_away = bf16(part[:count]), bf16(part[count:])
    grad_there = send(grad_away, PAIR)
    same, swapped = sum_over_x(where, factor, own_piece, *after(arrived, grad_away))
    got = send(same, OWNERS[0]), send(swapped, OWNERS[1])
    forward = joined(after(here, same), there, c)
    grad_input = joined(after(grad_here, same), grad_there, yh)
    one, two = after(got, forward, grad_input)
    return forward, grad_input, f32(one) + f32(two)


def solution(mesh):
    fine = Mesh(mesh.devices.reshape(SIZES), AXES)
    token_spec, node_spec = P(AXES, None), P(("yh", "x"), None)
    return jax.shard_map(
        on_device,
        mesh=fine,
        in_specs=(token_spec, token_spec, node_spec, node_spec),
        out_specs=(token_spec, token_spec, token_spec),
        check_vma=False,
    )
```

```python
import functools
import math

import jax
import jax.numpy as jnp
from jax import lax
from jax.experimental import pallas as pl
from jax.experimental.pallas import tpu as pltpu
from jax.sharding import Mesh, PartitionSpec as P

AXES = ("z", "yl", "c", "yh", "x")
SIZES = (8, 2, 2, 2, 4)
BLOCK_STEPS = (0, 3, 1, 2)
HOPS = (3, -3, 2, -2, 1, -1, 0)


def table(move):
    pairs = []
    for z in range(8):
        for yl in range(2):
            for c in range(2):
                for yh in range(2):
                    for x in range(4):
                        pairs.append((place(z, yl, c, yh, x), place(*move(z, yl, c, yh, x))))
    return pairs


def place(z, yl, c, yh, x):
    return (((z % 8 * 2 + yl % 2) * 2 + c % 2) * 2 + yh % 2) * 4 + x % 4


def window(z, c, yh):
    return (z + 11 - 4 * yh - 2 * c) % 8


def owner(z, yl, c, yh, x, message):
    chunk = window(z, c, yh)
    return 4 * yh + 2 * c + chunk // 4, chunk % 4 // 2, chunk % 2, yl ^ message, x


X_UP = table(lambda z, yl, c, yh, x: (z, yl, c, yh, x + 1))
X_DOWN = table(lambda z, yl, c, yh, x: (z, yl, c, yh, x - 1))
X_STEPS = [table(lambda z, yl, c, yh, x: (z, yl, c, yh, x + dx)) for dx in (1, 2, 3)]
Z_UP = table(lambda z, yl, c, yh, x: (z + 1, yl, c, yh, x))
Z_DOWN = table(lambda z, yl, c, yh, x: (z - 1, yl, c, yh, x))
CORE = table(lambda z, yl, c, yh, x: (z, yl, c + 1, yh, x))
PAIR = table(lambda z, yl, c, yh, x: (z, yl + 1, c, yh + 1, x))
OWNERS = [
    table(lambda z, yl, c, yh, x: owner(z, yl, c, yh, x, message)) for message in range(2)
]


def send(value, pairs):
    return lax.ppermute(value, AXES, pairs)


def after(values, *earlier):
    return lax.optimization_barrier((values, earlier))[0]


def f32(value):
    return value.astype(jnp.float32)


def bf16(value):
    return value.astype(jnp.bfloat16)


def call(kernel, name, mib, where, grid, in_specs, out_specs, out_shape, scratch, flops, operands):
    moved = sum(v.size * v.dtype.itemsize for v in operands)
    moved += sum(math.prod(v.shape) * v.dtype.itemsize for v in jax.tree.leaves(out_shape))
    return pl.pallas_call(
        kernel,
        name=name,
        grid_spec=pltpu.PrefetchScalarGridSpec(
            num_scalar_prefetch=1,
            grid=grid,
            in_specs=in_specs,
            out_specs=out_specs,
            scratch_shapes=scratch,
        ),
        out_shape=out_shape,
        compiler_params=pltpu.CompilerParams(vmem_limit_bytes=mib * 2**20),
        cost_estimate=pl.CostEstimate(flops=flops, bytes_accessed=moved, transcendentals=0),
    )(where, *operands)


def fixed(shape, at=lambda where: (0, 0)):
    return pl.BlockSpec(shape, lambda i, where: at(where))


def dequantize_kernel(where, levels, scales, out):
    count = scales.shape[0] // 2
    width = out.shape[1] // count
    mine = jnp.where(where[0] == 0, scales[:count], scales[count:]).T
    for b in range(count):
        scale = mine[:, b : b + 1]
        span = slice(b * width, (b + 1) * width)
        out[:, span] = bf16(f32(levels[:, span]) * scale)


def dequantize(where, levels, scales):
    row_count, nh = levels.shape[0], levels.shape[1] // 2
    size = row_count // 3
    return call(
        dequantize_kernel,
        "dequantize",
        60,
        where,
        (3,),
        [
            pl.BlockSpec((size, nh), lambda i, where: (i, where[0])),
            pl.BlockSpec((scales.shape[0], size), lambda i, where: (0, i)),
        ],
        pl.BlockSpec((size, nh), lambda i, where: (i, 0)),
        jax.ShapeDtypeStruct((row_count, nh), jnp.bfloat16),
        [],
        row_count * nh,
        (levels, scales),
    )


def columns(ref, start, size):
    return ref[:, pl.ds(pl.multiple_of(start, 128), size)]


def product(parts, starts, cots, lhs):
    count, size = parts[0].shape[0], lhs.shape[1]

    @pl.when(pl.program_id(0) == 0)
    def _():
        for r, (ref, start) in enumerate(zip(parts, starts)):
            lhs[r * count : (r + 1) * count] = columns(ref, start, size)

    rhs = jnp.concatenate([cot[...] for cot in cots])
    return bf16(
        lax.dot_general(
            lhs[...], rhs, (((0,), (0,)), ((), ())), preferred_element_type=jnp.float32
        )
    )


def gradient_kernel(where, own, sib, pair, psib, cot0, cot1, cot2, cot3, *refs):
    *chunks, lhs, out = refs
    c, yh = where[0], where[1]
    size = lhs.shape[1]
    starts = [base * 2 * size + c * size for base in (yh, yh, 0, 0)]
    out[...] = product((own, sib, pair, psib), starts, (cot0, cot1, cot2, cot3), lhs)
    height = size // 8
    for k, ref in zip(HOPS, chunks):
        row = pl.multiple_of((where[3] + 8 + k) % 8 * height, 16)
        ref[...] = out[pl.ds(row, height)]


def far_kernel(where, own, sib, pair, psib, cot0, cot1, cot2, cot3, up, down, lhs, out):
    c, yh = where[0], where[1]
    window, half = lhs.shape[1], up.shape[0]
    size, chunk, tile = 3 * window, 2 * half, window // 2
    row = (where[3] + 4) % 8 * chunk
    first = jnp.minimum(row // tile * tile, size - window)
    starts = [base * 2 * size + c * size + first for base in (yh, yh, 0, 0)]
    out[...] = product((own, sib, pair, psib), starts, (cot0, cot1, cot2, cot3), lhs)
    skip = pl.multiple_of(row - first, 16)
    up[...] = out[pl.ds(skip, half)]
    down[...] = out[pl.ds(skip + half, half)]


def gradient(where, token_parts, cot_parts, far):
    count, outputs = cot_parts[0].shape
    kh = token_parts[0].shape[1] // 2
    size, width = kh // 2, outputs // 4
    window = size // 3 if far else size
    heights = [size // 16] * 2 if far else [size // 8] * len(HOPS)
    return call(
        far_kernel if far else gradient_kernel,
        "far" if far else "gradient",
        24,
        where,
        (4,),
        [fixed(v.shape) for v in token_parts[:2]]
        + [fixed((count, kh))] * 2
        + [pl.BlockSpec((count, width), lambda i, where: (0, i))] * 4,
        [pl.BlockSpec((height, width), lambda i, where: (0, i)) for height in heights],
        [jax.ShapeDtypeStruct((height, outputs), jnp.bfloat16) for height in heights],
        [pltpu.VMEM((4 * count, window), jnp.bfloat16), pltpu.VMEM((window, width), jnp.bfloat16)],
        8 * count * window * outputs,
        (*token_parts, *cot_parts),
    )


def hop_kernel(*refs):
    *arrived, part, out = refs
    total = f32(part[...])
    for ref in arrived:
        total = total + f32(ref[...])
    out[...] = total.astype(out.dtype)


def first_hop_kernel(arrived, part, out, *, upper):
    half = arrived.shape[0]
    here, there = (slice(0, half), slice(half, 2 * half))[:: 1 if upper else -1]
    out[here] = bf16(f32(part[here]) + f32(arrived[...]))
    out[there] = part[there]


def hop(part, *arrived, kernel=hop_kernel, kind=jnp.bfloat16):
    return pl.pallas_call(
        kernel,
        name="hop",
        out_shape=jax.ShapeDtypeStruct(part.shape, kind),
        compiler_params=pltpu.CompilerParams(vmem_limit_bytes=8 * 2**20),
        cost_estimate=pl.CostEstimate(
            flops=part.size, bytes_accessed=6 * part.size, transcendentals=0
        ),
    )(*arrived, part)


def last_hop_kernel(where, up, down, part, own, *refs):
    *pieces, total = refs
    size = own.shape[0]
    for x in range(4):
        for yh in range(2):
            here = slice((yh * 4 + x) * (size // 2), (yh * 4 + x + 1) * (size // 2))
            there = slice((x * 2 + yh) * (size // 2), (x * 2 + yh + 1) * (size // 2))
            total[there] = f32(part[here]) + f32(up[here]) + f32(down[here])
    for dx, ref in enumerate((own, *pieces)):
        start = pl.multiple_of((where[2] + dx) % 4 * size, 8)
        ref[...] = total[pl.ds(start, size)].astype(ref.dtype)


def last_hop(where, part, up, down):
    size, outputs = part.shape
    width = outputs // 2
    kinds = (jnp.float32, *[jnp.bfloat16] * 3)
    return call(
        last_hop_kernel,
        "last_hop",
        8,
        where,
        (2,),
        [pl.BlockSpec((size, width), lambda i, where: (0, i))] * 3,
        [pl.BlockSpec((size // 4, width), lambda i, where: (0, i)) for _ in kinds],
        [jax.ShapeDtypeStruct((size // 4, outputs), kind) for kind in kinds],
        [pltpu.VMEM((size, width), jnp.float32)],
        2 * part.size,
        (up, down, part),
    )


def sum_kernel(where, own, one, two, three, same, other, total, *, factor):
    size = same.shape[0]
    total[...] = (own[...] + f32(one[...]) + f32(two[...]) + f32(three[...])) * factor
    first, second = bf16(total[:size]), bf16(total[size:])
    yl = where[4]
    same[...] = jnp.where(yl == 0, first, second)
    other[...] = jnp.where(yl == 0, second, first)


def sum_over_x(where, factor, own, *arrived):
    size, outputs = own.shape
    return call(
        functools.partial(sum_kernel, factor=factor),
        "sum_over_x",
        8,
        where,
        (1,),
        [fixed(own.shape)] * 4,
        [fixed((size // 2, outputs))] * 2,
        [jax.ShapeDtypeStruct((size // 2, outputs), jnp.bfloat16)] * 2,
        [pltpu.VMEM((size, outputs), jnp.float32)],
        4 * own.size,
        (own, *arrived),
    )


def forward_kernel(where, own, sib, pair, psib, w0, w1, w2, w3, w4, mine, other, away, lhs):
    yh, x = where[1], where[2]
    count, shard = own.shape[0], w0.shape[0]

    @pl.when(pl.program_id(0) == 0)
    def _():
        for r, (ref, base) in enumerate(((own, yh), (sib, yh), (pair, 0), (psib, 0))):
            for p, step in enumerate(BLOCK_STEPS):
                start = base * 4 * shard + (x + step) % 4 * shard
                lhs[r * count : (r + 1) * count, p * shard : (p + 1) * shard] = columns(
                    ref, start, shard
                )

    far = jnp.where(pl.program_id(0) == 0, w3[...], w4[...])
    rhs = jnp.concatenate([w0[...], w1[...], w2[...], far])
    out = jnp.dot(lhs[...], rhs, preferred_element_type=jnp.float32)
    mine[...] = out[:count]
    other[...] = out[count : 2 * count]
    away[...] = bf16(out[2 * count :])


def forward_parts(where, token_parts, blocks):
    count = token_parts[0].shape[0]
    shard, nh = blocks[0].shape
    width = nh // 2
    kinds = ((count, jnp.float32), (count, jnp.float32), (2 * count, jnp.bfloat16))
    return call(
        forward_kernel,
        "forward",
        28,
        where,
        (2,),
        [fixed(v.shape) for v in token_parts[:2]]
        + [fixed((count, 4 * shard))] * 2
        + [pl.BlockSpec((shard, width), lambda i, where: (0, i))] * 3
        + [fixed((shard, width))] * 2,
        [pl.BlockSpec((height, width), lambda i, where: (0, i)) for height, _ in kinds],
        [jax.ShapeDtypeStruct((height, nh), kind) for height, kind in kinds],
        [pltpu.VMEM((4 * count, 4 * shard), jnp.bfloat16)],
        32 * count * shard * nh,
        (*token_parts, *blocks),
    )


def backward_kernel(where, cot0, cot1, cot2, cot3, w0, w1, w2, w3, w4, mine, give, lhs):
    x = where[2]
    i = pl.program_id(0)
    count = cot0.shape[0]
    size, half = w3.shape

    @pl.when(i == 0)
    def _():
        for r, ref in enumerate((cot0, cot2, cot1, cot3)):
            lhs[r * count : (r + 1) * count] = ref[...]

    far = jnp.concatenate([w3[...], w4[...]], axis=1)
    rhs = jnp.concatenate([w0[...], w1[...], w2[...], far])
    out = lax.dot_general(
        lhs[...], rhs, (((1,), (1,)), ((), ())), preferred_element_type=jnp.float32
    )
    for p, step in enumerate(BLOCK_STEPS):
        start = pl.multiple_of((x + step) % 4 * 3 * size + i * size, 128)
        part = out[:, p * size : (p + 1) * size]
        mine[:, pl.ds(start, size)] = part[: 2 * count]
        give[:, pl.ds(start, size)] = bf16(part[2 * count :])


def backward_parts(where, cot_parts, blocks):
    count = cot_parts[0].shape[0]
    shard, nh = blocks[0].shape
    size = shard // 3
    types = (jnp.float32, jnp.bfloat16)
    return call(
        backward_kernel,
        "backward",
        28,
        where,
        (3,),
        [fixed((count, nh), lambda where: (0, where[0]))] * 4
        + [pl.BlockSpec((size, nh), lambda i, where: (i, 0))] * 3
        + [pl.BlockSpec((size, nh // 2), lambda i, where: (i, 0))] * 2,
        [fixed((2 * count, 4 * shard))] * 2,
        [jax.ShapeDtypeStruct((2 * count, 4 * shard), kind) for kind in types],
        [pltpu.VMEM((4 * count, nh), jnp.bfloat16)],
        32 * count * shard * nh,
        (*cot_parts, *blocks),
    )


def joined(here, there, flag):
    return jnp.where(
        flag == 0, jnp.concatenate([here, there], axis=1), jnp.concatenate([there, here], axis=1)
    )


def on_device(tokens, cotangent, levels, scales):
    z, yl, c, yh, x = (lax.axis_index(name) for name in AXES)
    where = jnp.stack([c, yh, x, window(z, c, yh), yl]).astype(jnp.int32)
    count = tokens.shape[0]
    factor = float(count * 256) ** -0.5

    cot_pair = send(cotangent, PAIR)
    kh = tokens.shape[1] // 2

    own = dequantize(where, levels, scales.T)
    left, right = send(own, X_UP), send(own, X_DOWN)

    token_out = lax.dynamic_slice_in_dim(after(tokens, own), (1 - yh) * kh, kh, 1)
    token_pair = send(token_out, PAIR)
    cot_own, token_own = after((cotangent, tokens), token_out)
    cot_sib, token_sib = send(cot_own, CORE), send(token_own, CORE)
    token_parts = (tokens, token_sib, token_pair, send(token_pair, CORE))
    cot_parts = (cotangent, cot_sib, cot_pair, send(cot_pair, CORE))

    up, down = gradient(where, token_parts, after(cot_parts, left, right), True)
    grad = gradient(where, token_parts, after(cot_parts, up), False)
    half = own.shape[1] // 2
    up, down = send(up, Z_UP), send(down, Z_DOWN)
    up = hop(grad[0], up, kernel=functools.partial(first_hop_kernel, upper=True))
    down = hop(grad[1], down, kernel=functools.partial(first_hop_kernel, upper=False))
    left, right = after((left, right), up, down)
    blocks = (own, left, right, send(left[:, :half], X_UP), send(right[:, half:], X_DOWN))
    up, down = send(up, Z_UP), send(down, Z_DOWN)
    up, down = hop(grad[2], up), hop(grad[3], down)
    mine, other, away = forward_parts(where, token_parts, after(blocks, up, down))
    up, down = send(up, Z_UP), send(down, Z_DOWN)
    back = f32(send(away, PAIR))
    grad = after(grad, away)
    up, down = hop(grad[4], up), hop(grad[5], down)
    part, give = backward_parts(where, cot_parts, after(blocks, up, down))
    up, down = send(up, Z_UP), send(down, Z_DOWN)
    give = send(give, CORE)
    own_piece, *pieces = last_hop(where, after(grad[6], part), up, down)
    arrived = [send(piece, to) for piece, to in zip(pieces, X_STEPS)]
    back = after(back, own_piece)
    here = bf16(mine + back[:count])
    there = send(bf16(other + back[count:]), CORE)
    part, give = after((part, give), own_piece)
    part = part + f32(give)
    grad_here, grad_away = bf16(part[:count]), bf16(part[count:])
    grad_there = send(grad_away, PAIR)
    same, swapped = sum_over_x(where, factor, own_piece, *after(arrived, grad_away))
    got = send(same, OWNERS[0]), send(swapped, OWNERS[1])
    forward = joined(after(here, same), there, c)
    grad_input = joined(after(grad_here, same), grad_there, yh)
    one, two = after(got, forward, grad_input)
    return forward, grad_input, f32(one) + f32(two)


def solution(mesh):
    fine = Mesh(mesh.devices.reshape(SIZES), AXES)
    token_spec, node_spec = P(AXES, None), P(("yh", "x"), None)
    return jax.shard_map(
        on_device,
        mesh=fine,
        in_specs=(token_spec, token_spec, node_spec, node_spec),
        out_specs=(token_spec, token_spec, token_spec),
        check_vma=False,
    )
```

```python
import functools
import math

import jax
import jax.numpy as jnp
from jax import lax
from jax.experimental import pallas as pl
from jax.experimental.pallas import tpu as pltpu
from jax.sharding import Mesh, PartitionSpec as P

AXES = ("z", "yl", "c", "yh", "x")
SIZES = (8, 2, 2, 2, 4)
BLOCK_STEPS = (0, 3, 1, 2)
HOPS = (3, -3, 2, -2, 1, -1, 0)


def table(move):
    pairs = []
    for z in range(8):
        for yl in range(2):
            for c in range(2):
                for yh in range(2):
                    for x in range(4):
                        pairs.append((place(z, yl, c, yh, x), place(*move(z, yl, c, yh, x))))
    return pairs


def place(z, yl, c, yh, x):
    return (((z % 8 * 2 + yl % 2) * 2 + c % 2) * 2 + yh % 2) * 4 + x % 4


def window(z, c, yh):
    return (z + 11 - 4 * yh - 2 * c) % 8


def owner(z, yl, c, yh, x, message):
    chunk = window(z, c, yh)
    return 4 * yh + 2 * c + chunk // 4, chunk % 4 // 2, chunk % 2, yl ^ message, x


X_UP = table(lambda z, yl, c, yh, x: (z, yl, c, yh, x + 1))
X_DOWN = table(lambda z, yl, c, yh, x: (z, yl, c, yh, x - 1))
X_STEPS = [table(lambda z, yl, c, yh, x: (z, yl, c, yh, x + dx)) for dx in (1, 2, 3)]
Z_UP = table(lambda z, yl, c, yh, x: (z + 1, yl, c, yh, x))
Z_DOWN = table(lambda z, yl, c, yh, x: (z - 1, yl, c, yh, x))
CORE = table(lambda z, yl, c, yh, x: (z, yl, c + 1, yh, x))
PAIR = table(lambda z, yl, c, yh, x: (z, yl + 1, c, yh + 1, x))
OWNERS = [
    table(lambda z, yl, c, yh, x: owner(z, yl, c, yh, x, message)) for message in range(2)
]


def send(value, pairs):
    return lax.ppermute(value, AXES, pairs)


def after(values, *earlier):
    return lax.optimization_barrier((values, earlier))[0]


def f32(value):
    return value.astype(jnp.float32)


def bf16(value):
    return value.astype(jnp.bfloat16)


def call(kernel, name, mib, where, grid, in_specs, out_specs, out_shape, scratch, flops, operands):
    moved = sum(v.size * v.dtype.itemsize for v in operands)
    moved += sum(math.prod(v.shape) * v.dtype.itemsize for v in jax.tree.leaves(out_shape))
    return pl.pallas_call(
        kernel,
        name=name,
        grid_spec=pltpu.PrefetchScalarGridSpec(
            num_scalar_prefetch=1,
            grid=grid,
            in_specs=in_specs,
            out_specs=out_specs,
            scratch_shapes=scratch,
        ),
        out_shape=out_shape,
        compiler_params=pltpu.CompilerParams(vmem_limit_bytes=mib * 2**20),
        cost_estimate=pl.CostEstimate(flops=flops, bytes_accessed=moved, transcendentals=0),
    )(where, *operands)


def fixed(shape, at=lambda where: (0, 0)):
    return pl.BlockSpec(shape, lambda i, where: at(where))


def dequantize_kernel(where, levels, scales, out):
    count = scales.shape[0] // 2
    width = out.shape[1] // count
    mine = jnp.where(where[0] == 0, scales[:count], scales[count:]).T
    for b in range(count):
        scale = mine[:, b : b + 1]
        span = slice(b * width, (b + 1) * width)
        out[:, span] = bf16(f32(levels[:, span]) * scale)


def dequantize(where, levels, scales):
    row_count, nh = levels.shape[0], levels.shape[1] // 2
    size = row_count // 3
    return call(
        dequantize_kernel,
        "dequantize",
        60,
        where,
        (3,),
        [
            pl.BlockSpec((size, nh), lambda i, where: (i, where[0])),
            pl.BlockSpec((scales.shape[0], size), lambda i, where: (0, i)),
        ],
        pl.BlockSpec((size, nh), lambda i, where: (i, 0)),
        jax.ShapeDtypeStruct((row_count, nh), jnp.bfloat16),
        [],
        row_count * nh,
        (levels, scales),
    )


def columns(ref, start, size):
    return ref[:, pl.ds(pl.multiple_of(start, 128), size)]


def product(parts, starts, cots, lhs):
    count, size = parts[0].shape[0], lhs.shape[1]

    @pl.when(pl.program_id(0) == 0)
    def _():
        for r, (ref, start) in enumerate(zip(parts, starts)):
            lhs[r * count : (r + 1) * count] = columns(ref, start, size)

    rhs = jnp.concatenate([cot[...] for cot in cots])
    return bf16(
        lax.dot_general(
            lhs[...], rhs, (((0,), (0,)), ((), ())), preferred_element_type=jnp.float32
        )
    )


def gradient_kernel(where, own, sib, pair, psib, cot0, cot1, cot2, cot3, *refs):
    *chunks, lhs, out = refs
    c, yh = where[0], where[1]
    size = lhs.shape[1]
    starts = [base * 2 * size + c * size for base in (yh, yh, 0, 0)]
    out[...] = product((own, sib, pair, psib), starts, (cot0, cot1, cot2, cot3), lhs)
    height = size // 8
    for k, ref in zip(HOPS, chunks):
        row = pl.multiple_of((where[3] + 8 + k) % 8 * height, 16)
        ref[...] = out[pl.ds(row, height)]


def far_kernel(where, own, sib, pair, psib, cot0, cot1, cot2, cot3, up, down, lhs, out):
    c, yh = where[0], where[1]
    window, half = lhs.shape[1], up.shape[0]
    size, chunk, tile = 3 * window, 2 * half, window // 2
    row = (where[3] + 4) % 8 * chunk
    first = jnp.minimum(row // tile * tile, size - window)
    starts = [base * 2 * size + c * size + first for base in (yh, yh, 0, 0)]
    out[...] = product((own, sib, pair, psib), starts, (cot0, cot1, cot2, cot3), lhs)
    skip = pl.multiple_of(row - first, 16)
    up[...] = out[pl.ds(skip, half)]
    down[...] = out[pl.ds(skip + half, half)]


def gradient(where, token_parts, cot_parts, far):
    count, outputs = cot_parts[0].shape
    kh = token_parts[0].shape[1] // 2
    size, width = kh // 2, outputs // 4
    window = size // 3 if far else size
    heights = [size // 16] * 2 if far else [size // 8] * len(HOPS)
    return call(
        far_kernel if far else gradient_kernel,
        "far" if far else "gradient",
        24,
        where,
        (4,),
        [fixed(v.shape) for v in token_parts[:2]]
        + [fixed((count, kh))] * 2
        + [pl.BlockSpec((count, width), lambda i, where: (0, i))] * 4,
        [pl.BlockSpec((height, width), lambda i, where: (0, i)) for height in heights],
        [jax.ShapeDtypeStruct((height, outputs), jnp.bfloat16) for height in heights],
        [pltpu.VMEM((4 * count, window), jnp.bfloat16), pltpu.VMEM((window, width), jnp.bfloat16)],
        8 * count * window * outputs,
        (*token_parts, *cot_parts),
    )


def hop_kernel(*refs):
    *arrived, part, out = refs
    total = f32(part[...])
    for ref in arrived:
        total = total + f32(ref[...])
    out[...] = total.astype(out.dtype)


def first_hop_kernel(arrived, part, out, *, upper):
    half = arrived.shape[0]
    here, there = (slice(0, half), slice(half, 2 * half))[:: 1 if upper else -1]
    out[here] = bf16(f32(part[here]) + f32(arrived[...]))
    out[there] = part[there]


def hop(part, *arrived, kernel=hop_kernel, kind=jnp.bfloat16):
    return pl.pallas_call(
        kernel,
        name="hop",
        out_shape=jax.ShapeDtypeStruct(part.shape, kind),
        compiler_params=pltpu.CompilerParams(vmem_limit_bytes=8 * 2**20),
        cost_estimate=pl.CostEstimate(
            flops=part.size, bytes_accessed=6 * part.size, transcendentals=0
        ),
    )(*arrived, part)


def last_hop_kernel(where, up, down, part, own, *refs):
    *pieces, total = refs
    size = own.shape[0]
    sums = f32(part[...]) + f32(up[...]) + f32(down[...])
    for x in range(4):
        for yh in range(2):
            here = slice((yh * 4 + x) * (size // 2), (yh * 4 + x + 1) * (size // 2))
            there = slice((x * 2 + yh) * (size // 2), (x * 2 + yh + 1) * (size // 2))
            total[there] = sums[here]
    for dx, ref in enumerate((own, *pieces)):
        start = pl.multiple_of((where[2] + dx) % 4 * size, 8)
        ref[...] = total[pl.ds(start, size)].astype(ref.dtype)


def last_hop(where, part, up, down):
    size, outputs = part.shape
    width = outputs // 2
    kinds = (jnp.float32, *[jnp.bfloat16] * 3)
    return call(
        last_hop_kernel,
        "last_hop",
        8,
        where,
        (2,),
        [pl.BlockSpec((size, width), lambda i, where: (0, i))] * 3,
        [pl.BlockSpec((size // 4, width), lambda i, where: (0, i)) for _ in kinds],
        [jax.ShapeDtypeStruct((size // 4, outputs), kind) for kind in kinds],
        [pltpu.VMEM((size, width), jnp.float32)],
        2 * part.size,
        (up, down, part),
    )


def sum_kernel(where, own, one, two, three, same, other, total, *, factor):
    size = same.shape[0]
    total[...] = (own[...] + f32(one[...]) + f32(two[...]) + f32(three[...])) * factor
    first, second = bf16(total[:size]), bf16(total[size:])
    yl = where[4]
    same[...] = jnp.where(yl == 0, first, second)
    other[...] = jnp.where(yl == 0, second, first)


def sum_over_x(where, factor, own, *arrived):
    size, outputs = own.shape
    return call(
        functools.partial(sum_kernel, factor=factor),
        "sum_over_x",
        8,
        where,
        (1,),
        [fixed(own.shape)] * 4,
        [fixed((size // 2, outputs))] * 2,
        [jax.ShapeDtypeStruct((size // 2, outputs), jnp.bfloat16)] * 2,
        [pltpu.VMEM((size, outputs), jnp.float32)],
        4 * own.size,
        (own, *arrived),
    )


def forward_kernel(where, own, sib, pair, psib, w0, w1, w2, w3, w4, mine, other, away, lhs):
    yh, x = where[1], where[2]
    count, shard = own.shape[0], w0.shape[0]

    @pl.when(pl.program_id(0) == 0)
    def _():
        for r, (ref, base) in enumerate(((own, yh), (sib, yh), (pair, 0), (psib, 0))):
            for p, step in enumerate(BLOCK_STEPS):
                start = base * 4 * shard + (x + step) % 4 * shard
                lhs[r * count : (r + 1) * count, p * shard : (p + 1) * shard] = columns(
                    ref, start, shard
                )

    far = jnp.where(pl.program_id(0) == 0, w3[...], w4[...])
    rhs = jnp.concatenate([w0[...], w1[...], w2[...], far])
    out = jnp.dot(lhs[...], rhs, preferred_element_type=jnp.float32)
    mine[...] = out[:count]
    other[...] = out[count : 2 * count]
    away[...] = bf16(out[2 * count :])


def forward_parts(where, token_parts, blocks):
    count = token_parts[0].shape[0]
    shard, nh = blocks[0].shape
    width = nh // 2
    kinds = ((count, jnp.float32), (count, jnp.float32), (2 * count, jnp.bfloat16))
    return call(
        forward_kernel,
        "forward",
        28,
        where,
        (2,),
        [fixed(v.shape) for v in token_parts[:2]]
        + [fixed((count, 4 * shard))] * 2
        + [pl.BlockSpec((shard, width), lambda i, where: (0, i))] * 3
        + [fixed((shard, width))] * 2,
        [pl.BlockSpec((height, width), lambda i, where: (0, i)) for height, _ in kinds],
        [jax.ShapeDtypeStruct((height, nh), kind) for height, kind in kinds],
        [pltpu.VMEM((4 * count, 4 * shard), jnp.bfloat16)],
        32 * count * shard * nh,
        (*token_parts, *blocks),
    )


def backward_kernel(where, cot0, cot1, cot2, cot3, w0, w1, w2, w3, w4, mine, give, lhs):
    x = where[2]
    i = pl.program_id(0)
    count = cot0.shape[0]
    size, half = w3.shape

    @pl.when(i == 0)
    def _():
        for r, ref in enumerate((cot0, cot2, cot1, cot3)):
            lhs[r * count : (r + 1) * count] = ref[...]

    far = jnp.concatenate([w3[...], w4[...]], axis=1)
    rhs = jnp.concatenate([w0[...], w1[...], w2[...], far])
    out = lax.dot_general(
        lhs[...], rhs, (((1,), (1,)), ((), ())), preferred_element_type=jnp.float32
    )
    for p, step in enumerate(BLOCK_STEPS):
        start = pl.multiple_of((x + step) % 4 * 3 * size + i * size, 128)
        part = out[:, p * size : (p + 1) * size]
        mine[:, pl.ds(start, size)] = part[: 2 * count]
        give[:, pl.ds(start, size)] = bf16(part[2 * count :])


def backward_parts(where, cot_parts, blocks):
    count = cot_parts[0].shape[0]
    shard, nh = blocks[0].shape
    size = shard // 3
    types = (jnp.float32, jnp.bfloat16)
    return call(
        backward_kernel,
        "backward",
        28,
        where,
        (3,),
        [fixed((count, nh), lambda where: (0, where[0]))] * 4
        + [pl.BlockSpec((size, nh), lambda i, where: (i, 0))] * 3
        + [pl.BlockSpec((size, nh // 2), lambda i, where: (i, 0))] * 2,
        [fixed((2 * count, 4 * shard))] * 2,
        [jax.ShapeDtypeStruct((2 * count, 4 * shard), kind) for kind in types],
        [pltpu.VMEM((4 * count, nh), jnp.bfloat16)],
        32 * count * shard * nh,
        (*cot_parts, *blocks),
    )


def joined(here, there, flag):
    return jnp.where(
        flag == 0, jnp.concatenate([here, there], axis=1), jnp.concatenate([there, here], axis=1)
    )


def on_device(tokens, cotangent, levels, scales):
    z, yl, c, yh, x = (lax.axis_index(name) for name in AXES)
    where = jnp.stack([c, yh, x, window(z, c, yh), yl]).astype(jnp.int32)
    count = tokens.shape[0]
    factor = float(count * 256) ** -0.5

    cot_pair = send(cotangent, PAIR)
    kh = tokens.shape[1] // 2

    own = dequantize(where, levels, scales.T)
    left, right = send(own, X_UP), send(own, X_DOWN)

    token_out = lax.dynamic_slice_in_dim(after(tokens, own), (1 - yh) * kh, kh, 1)
    token_pair = send(token_out, PAIR)
    cot_own, token_own = after((cotangent, tokens), token_out)
    cot_sib, token_sib = send(cot_own, CORE), send(token_own, CORE)
    token_parts = (tokens, token_sib, token_pair, send(token_pair, CORE))
    cot_parts = (cotangent, cot_sib, cot_pair, send(cot_pair, CORE))

    up, down = gradient(where, token_parts, after(cot_parts, left, right), True)
    grad = gradient(where, token_parts, after(cot_parts, up), False)
    half = own.shape[1] // 2
    up, down = send(up, Z_UP), send(down, Z_DOWN)
    up = hop(grad[0], up, kernel=functools.partial(first_hop_kernel, upper=True))
    down = hop(grad[1], down, kernel=functools.partial(first_hop_kernel, upper=False))
    left, right = after((left, right), up, down)
    blocks = (own, left, right, send(left[:, :half], X_UP), send(right[:, half:], X_DOWN))
    up, down = send(up, Z_UP), send(down, Z_DOWN)
    up, down = hop(grad[2], up), hop(grad[3], down)
    mine, other, away = forward_parts(where, token_parts, after(blocks, up, down))
    up, down = send(up, Z_UP), send(down, Z_DOWN)
    back = f32(send(away, PAIR))
    grad = after(grad, away)
    up, down = hop(grad[4], up), hop(grad[5], down)
    part, give = backward_parts(where, cot_parts, after(blocks, up, down))
    up, down = send(up, Z_UP), send(down, Z_DOWN)
    give = send(give, CORE)
    own_piece, *pieces = last_hop(where, after(grad[6], part), up, down)
    arrived = [send(piece, to) for piece, to in zip(pieces, X_STEPS)]
    back = after(back, own_piece)
    here = bf16(mine + back[:count])
    there = send(bf16(other + back[count:]), CORE)
    part, give = after((part, give), own_piece)
    part = part + f32(give)
    grad_here, grad_away = bf16(part[:count]), bf16(part[count:])
    grad_there = send(grad_away, PAIR)
    same, swapped = sum_over_x(where, factor, own_piece, *after(arrived, grad_away))
    got = send(same, OWNERS[0]), send(swapped, OWNERS[1])
    forward = joined(after(here, same), there, c)
    grad_input = joined(after(grad_here, same), grad_there, yh)
    one, two = after(got, forward, grad_input)
    return forward, grad_input, f32(one) + f32(two)


def solution(mesh):
    fine = Mesh(mesh.devices.reshape(SIZES), AXES)
    token_spec, node_spec = P(AXES, None), P(("yh", "x"), None)
    return jax.shard_map(
        on_device,
        mesh=fine,
        in_specs=(token_spec, token_spec, node_spec, node_spec),
        out_specs=(token_spec, token_spec, token_spec),
        check_vma=False,
    )
```

```python
import functools
import math

import jax
import jax.numpy as jnp
from jax import lax
from jax.experimental import pallas as pl
from jax.experimental.pallas import tpu as pltpu
from jax.sharding import Mesh, PartitionSpec as P

AXES = ("z", "yl", "c", "yh", "x")
SIZES = (8, 2, 2, 2, 4)
BLOCK_STEPS = (0, 3, 1, 2)
HOPS = (3, -3, 2, -2, 1, -1, 0)


def table(move):
    pairs = []
    for z in range(8):
        for yl in range(2):
            for c in range(2):
                for yh in range(2):
                    for x in range(4):
                        pairs.append((place(z, yl, c, yh, x), place(*move(z, yl, c, yh, x))))
    return pairs


def place(z, yl, c, yh, x):
    return (((z % 8 * 2 + yl % 2) * 2 + c % 2) * 2 + yh % 2) * 4 + x % 4


def window(z, c, yh):
    return (z + 11 - 4 * yh - 2 * c) % 8


def owner(z, yl, c, yh, x, message):
    chunk = window(z, c, yh)
    return 4 * yh + 2 * c + chunk // 4, chunk % 4 // 2, chunk % 2, yl ^ message, x


X_UP = table(lambda z, yl, c, yh, x: (z, yl, c, yh, x + 1))
X_DOWN = table(lambda z, yl, c, yh, x: (z, yl, c, yh, x - 1))
X_STEPS = [table(lambda z, yl, c, yh, x: (z, yl, c, yh, x + dx)) for dx in (1, 2, 3)]
Z_UP = table(lambda z, yl, c, yh, x: (z + 1, yl, c, yh, x))
Z_DOWN = table(lambda z, yl, c, yh, x: (z - 1, yl, c, yh, x))
CORE = table(lambda z, yl, c, yh, x: (z, yl, c + 1, yh, x))
PAIR = table(lambda z, yl, c, yh, x: (z, yl + 1, c, yh + 1, x))
OWNERS = [
    table(lambda z, yl, c, yh, x: owner(z, yl, c, yh, x, message)) for message in range(2)
]


def send(value, pairs):
    return lax.ppermute(value, AXES, pairs)


def after(values, *earlier):
    return lax.optimization_barrier((values, earlier))[0]


def f32(value):
    return value.astype(jnp.float32)


def bf16(value):
    return value.astype(jnp.bfloat16)


def call(kernel, name, mib, where, grid, in_specs, out_specs, out_shape, scratch, flops, operands):
    moved = sum(v.size * v.dtype.itemsize for v in operands)
    moved += sum(math.prod(v.shape) * v.dtype.itemsize for v in jax.tree.leaves(out_shape))
    return pl.pallas_call(
        kernel,
        name=name,
        grid_spec=pltpu.PrefetchScalarGridSpec(
            num_scalar_prefetch=1,
            grid=grid,
            in_specs=in_specs,
            out_specs=out_specs,
            scratch_shapes=scratch,
        ),
        out_shape=out_shape,
        compiler_params=pltpu.CompilerParams(vmem_limit_bytes=mib * 2**20),
        cost_estimate=pl.CostEstimate(flops=flops, bytes_accessed=moved, transcendentals=0),
    )(where, *operands)


def fixed(shape, at=lambda where: (0, 0)):
    return pl.BlockSpec(shape, lambda i, where: at(where))


def dequantize_kernel(where, levels, scales, out):
    count = scales.shape[0] // 2
    width = out.shape[1] // count
    mine = jnp.where(where[0] == 0, scales[:count], scales[count:]).T
    for b in range(count):
        scale = mine[:, b : b + 1]
        span = slice(b * width, (b + 1) * width)
        out[:, span] = bf16(f32(levels[:, span]) * scale)


def dequantize(where, levels, scales):
    row_count, nh = levels.shape[0], levels.shape[1] // 2
    size = row_count // 3
    return call(
        dequantize_kernel,
        "dequantize",
        60,
        where,
        (3,),
        [
            pl.BlockSpec((size, nh), lambda i, where: (i, where[0])),
            pl.BlockSpec((scales.shape[0], size), lambda i, where: (0, i)),
        ],
        pl.BlockSpec((size, nh), lambda i, where: (i, 0)),
        jax.ShapeDtypeStruct((row_count, nh), jnp.bfloat16),
        [],
        row_count * nh,
        (levels, scales),
    )


def columns(ref, start, size):
    return ref[:, pl.ds(pl.multiple_of(start, 128), size)]


def product(parts, starts, cots, lhs):
    count, size = parts[0].shape[0], lhs.shape[1]

    @pl.when(pl.program_id(0) == 0)
    def _():
        for r, (ref, start) in enumerate(zip(parts, starts)):
            lhs[r * count : (r + 1) * count] = columns(ref, start, size)

    rhs = jnp.concatenate([cot[...] for cot in cots])
    return bf16(
        lax.dot_general(
            lhs[...], rhs, (((0,), (0,)), ((), ())), preferred_element_type=jnp.float32
        )
    )


def gradient_kernel(where, own, sib, pair, psib, cot0, cot1, cot2, cot3, *refs):
    *chunks, lhs, out = refs
    c, yh = where[0], where[1]
    size = lhs.shape[1]
    starts = [base * 2 * size + c * size for base in (yh, yh, 0, 0)]
    out[...] = product((own, sib, pair, psib), starts, (cot0, cot1, cot2, cot3), lhs)
    height = size // 8
    for k, ref in zip(HOPS, chunks):
        row = pl.multiple_of((where[3] + 8 + k) % 8 * height, 16)
        ref[...] = out[pl.ds(row, height)]


def far_kernel(where, own, sib, pair, psib, cot0, cot1, cot2, cot3, up, down, lhs, out):
    c, yh = where[0], where[1]
    window, half = lhs.shape[1], up.shape[0]
    size, chunk, tile = 3 * window, 2 * half, window // 2
    row = (where[3] + 4) % 8 * chunk
    first = jnp.minimum(row // tile * tile, size - window)
    starts = [base * 2 * size + c * size + first for base in (yh, yh, 0, 0)]
    out[...] = product((own, sib, pair, psib), starts, (cot0, cot1, cot2, cot3), lhs)
    skip = pl.multiple_of(row - first, 16)
    up[...] = out[pl.ds(skip, half)]
    down[...] = out[pl.ds(skip + half, half)]


def gradient(where, token_parts, cot_parts, far):
    count, outputs = cot_parts[0].shape
    kh = token_parts[0].shape[1] // 2
    size, width = kh // 2, outputs // 4
    window = size // 3 if far else size
    heights = [size // 16] * 2 if far else [size // 8] * len(HOPS)
    return call(
        far_kernel if far else gradient_kernel,
        "far" if far else "gradient",
        24,
        where,
        (4,),
        [fixed(v.shape) for v in token_parts[:2]]
        + [fixed((count, kh))] * 2
        + [pl.BlockSpec((count, width), lambda i, where: (0, i))] * 4,
        [pl.BlockSpec((height, width), lambda i, where: (0, i)) for height in heights],
        [jax.ShapeDtypeStruct((height, outputs), jnp.bfloat16) for height in heights],
        [pltpu.VMEM((4 * count, window), jnp.bfloat16), pltpu.VMEM((window, width), jnp.bfloat16)],
        8 * count * window * outputs,
        (*token_parts, *cot_parts),
    )


def hop_kernel(*refs):
    *arrived, part, out = refs
    total = f32(part[...])
    for ref in arrived:
        total = total + f32(ref[...])
    out[...] = total.astype(out.dtype)


def first_hop_kernel(arrived, part, out, *, upper):
    half = arrived.shape[0]
    here, there = (slice(0, half), slice(half, 2 * half))[:: 1 if upper else -1]
    out[here] = bf16(f32(part[here]) + f32(arrived[...]))
    out[there] = part[there]


def hop(part, *arrived, kernel=hop_kernel, kind=jnp.bfloat16):
    return pl.pallas_call(
        kernel,
        name="hop",
        out_shape=jax.ShapeDtypeStruct(part.shape, kind),
        compiler_params=pltpu.CompilerParams(vmem_limit_bytes=8 * 2**20),
        cost_estimate=pl.CostEstimate(
            flops=part.size, bytes_accessed=6 * part.size, transcendentals=0
        ),
    )(*arrived, part)


def last_hop_kernel(where, up, down, part, own, *refs):
    *pieces, total = refs
    size = own.shape[0]
    sums = f32(part[...]) + f32(up[...]) + f32(down[...])
    for x in range(4):
        for yh in range(2):
            here = slice((yh * 4 + x) * (size // 2), (yh * 4 + x + 1) * (size // 2))
            there = slice((x * 2 + yh) * (size // 2), (x * 2 + yh + 1) * (size // 2))
            total[there] = sums[here]
    for dx, ref in enumerate((own, *pieces)):
        start = pl.multiple_of((where[2] + dx) % 4 * size, 8)
        ref[...] = total[pl.ds(start, size)].astype(ref.dtype)


def last_hop(where, part, up, down):
    size, outputs = part.shape
    width = outputs // 2
    kinds = (jnp.float32, *[jnp.bfloat16] * 3)
    return call(
        last_hop_kernel,
        "last_hop",
        8,
        where,
        (2,),
        [pl.BlockSpec((size, width), lambda i, where: (0, i))] * 3,
        [pl.BlockSpec((size // 4, width), lambda i, where: (0, i)) for _ in kinds],
        [jax.ShapeDtypeStruct((size // 4, outputs), kind) for kind in kinds],
        [pltpu.VMEM((size, width), jnp.float32)],
        2 * part.size,
        (up, down, part),
    )


def sum_kernel(where, own, one, two, three, same, other, total, *, factor):
    size = same.shape[0]
    total[...] = (own[...] + f32(one[...]) + f32(two[...]) + f32(three[...])) * factor
    first, second = bf16(total[:size]), bf16(total[size:])
    yl = where[4]
    same[...] = jnp.where(yl == 0, first, second)
    other[...] = jnp.where(yl == 0, second, first)


def sum_over_x(where, factor, own, *arrived):
    size, outputs = own.shape
    return call(
        functools.partial(sum_kernel, factor=factor),
        "sum_over_x",
        8,
        where,
        (1,),
        [fixed(own.shape)] * 4,
        [fixed((size // 2, outputs))] * 2,
        [jax.ShapeDtypeStruct((size // 2, outputs), jnp.bfloat16)] * 2,
        [pltpu.VMEM((size, outputs), jnp.float32)],
        4 * own.size,
        (own, *arrived),
    )


def forward_kernel(where, own, sib, pair, psib, w0, w1, w2, w3, w4, mine, other, away, lhs):
    yh, x = where[1], where[2]
    count, shard = own.shape[0], w0.shape[0]

    @pl.when(pl.program_id(0) == 0)
    def _():
        for r, (ref, base) in enumerate(((own, yh), (sib, yh), (pair, 0), (psib, 0))):
            for p, step in enumerate(BLOCK_STEPS):
                start = base * 4 * shard + (x + step) % 4 * shard
                lhs[r * count : (r + 1) * count, p * shard : (p + 1) * shard] = columns(
                    ref, start, shard
                )

    far = jnp.where(pl.program_id(0) == 0, w3[...], w4[...])
    rhs = jnp.concatenate([w0[...], w1[...], w2[...], far])
    out = jnp.dot(lhs[...], rhs, preferred_element_type=jnp.float32)
    mine[...] = out[:count]
    other[...] = out[count : 2 * count]
    away[...] = bf16(out[2 * count :])


def forward_parts(where, token_parts, blocks):
    count = token_parts[0].shape[0]
    shard, nh = blocks[0].shape
    width = nh // 2
    kinds = ((count, jnp.float32), (count, jnp.float32), (2 * count, jnp.bfloat16))
    return call(
        forward_kernel,
        "forward",
        28,
        where,
        (2,),
        [fixed(v.shape) for v in token_parts[:2]]
        + [fixed((count, 4 * shard))] * 2
        + [pl.BlockSpec((shard, width), lambda i, where: (0, i))] * 3
        + [fixed((shard, width))] * 2,
        [pl.BlockSpec((height, width), lambda i, where: (0, i)) for height, _ in kinds],
        [jax.ShapeDtypeStruct((height, nh), kind) for height, kind in kinds],
        [pltpu.VMEM((4 * count, 4 * shard), jnp.bfloat16)],
        32 * count * shard * nh,
        (*token_parts, *blocks),
    )


def backward_kernel(where, cot0, cot1, cot2, cot3, w0, w1, w2, w3, w4, mine, give, lhs):
    x = where[2]
    i = pl.program_id(0)
    count = cot0.shape[0]
    size, half = w3.shape

    @pl.when(i == 0)
    def _():
        for r, ref in enumerate((cot0, cot2, cot1, cot3)):
            lhs[r * count : (r + 1) * count] = ref[...]

    far = jnp.concatenate([w3[...], w4[...]], axis=1)
    rhs = jnp.concatenate([w0[...], w1[...], w2[...], far])
    out = lax.dot_general(
        lhs[...], rhs, (((1,), (1,)), ((), ())), preferred_element_type=jnp.float32
    )
    for p, step in enumerate(BLOCK_STEPS):
        start = pl.multiple_of((x + step) % 4 * 3 * size + i * size, 128)
        part = out[:, p * size : (p + 1) * size]
        mine[:, pl.ds(start, size)] = part[: 2 * count]
        give[:, pl.ds(start, size)] = bf16(part[2 * count :])


def backward_parts(where, cot_parts, blocks):
    count = cot_parts[0].shape[0]
    shard, nh = blocks[0].shape
    size = shard // 3
    types = (jnp.float32, jnp.bfloat16)
    return call(
        backward_kernel,
        "backward",
        28,
        where,
        (3,),
        [fixed((count, nh), lambda where: (0, where[0]))] * 4
        + [pl.BlockSpec((size, nh), lambda i, where: (i, 0))] * 3
        + [pl.BlockSpec((size, nh // 2), lambda i, where: (i, 0))] * 2,
        [fixed((2 * count, 4 * shard))] * 2,
        [jax.ShapeDtypeStruct((2 * count, 4 * shard), kind) for kind in types],
        [pltpu.VMEM((4 * count, nh), jnp.bfloat16)],
        32 * count * shard * nh,
        (*cot_parts, *blocks),
    )


def joined(here, there, flag):
    return jnp.where(
        flag == 0, jnp.concatenate([here, there], axis=1), jnp.concatenate([there, here], axis=1)
    )


def on_device(tokens, cotangent, levels, scales):
    z, yl, c, yh, x = (lax.axis_index(name) for name in AXES)
    where = jnp.stack([c, yh, x, window(z, c, yh), yl]).astype(jnp.int32)
    count = tokens.shape[0]
    factor = float(count * 256) ** -0.5

    cot_pair = send(cotangent, PAIR)
    kh = tokens.shape[1] // 2

    own = dequantize(where, levels, scales.T)
    left, right = send(own, X_UP), send(own, X_DOWN)

    token_out = lax.dynamic_slice_in_dim(after(tokens, own), (1 - yh) * kh, kh, 1)
    token_pair = send(token_out, PAIR)
    cot_own, token_own = after((cotangent, tokens), token_out)
    cot_sib, token_sib = send(cot_own, CORE), send(token_own, CORE)
    token_parts = (tokens, token_sib, token_pair, send(token_pair, CORE))
    cot_parts = (cotangent, cot_sib, cot_pair, send(cot_pair, CORE))

    up, down = gradient(where, token_parts, after(cot_parts, left), True)
    grad = gradient(where, token_parts, after(cot_parts, up, right), False)
    half = own.shape[1] // 2
    up, down = send(up, Z_UP), send(down, Z_DOWN)
    up = hop(grad[0], up, kernel=functools.partial(first_hop_kernel, upper=True))
    down = hop(grad[1], down, kernel=functools.partial(first_hop_kernel, upper=False))
    left, right = after((left, right), up, down)
    blocks = (own, left, right, send(left[:, :half], X_UP), send(right[:, half:], X_DOWN))
    up, down = send(up, Z_UP), send(down, Z_DOWN)
    up, down = hop(grad[2], up), hop(grad[3], down)
    mine, other, away = forward_parts(where, token_parts, after(blocks, up, down))
    up, down = send(up, Z_UP), send(down, Z_DOWN)
    back = f32(send(away, PAIR))
    grad = after(grad, away)
    up, down = hop(grad[4], up), hop(grad[5], down)
    part, give = backward_parts(where, cot_parts, after(blocks, up, down))
    up, down = send(up, Z_UP), send(down, Z_DOWN)
    give = send(give, CORE)
    own_piece, *pieces = last_hop(where, after(grad[6], part), up, down)
    arrived = [send(piece, to) for piece, to in zip(pieces, X_STEPS)]
    back = after(back, own_piece)
    here = bf16(mine + back[:count])
    there = send(bf16(other + back[count:]), CORE)
    part, give = after((part, give), own_piece)
    part = part + f32(give)
    grad_here, grad_away = bf16(part[:count]), bf16(part[count:])
    grad_there = send(grad_away, PAIR)
    same, swapped = sum_over_x(where, factor, own_piece, *after(arrived, grad_away))
    got = send(same, OWNERS[0]), send(swapped, OWNERS[1])
    forward = joined(after(here, same), there, c)
    grad_input = joined(after(grad_here, same), grad_there, yh)
    one, two = after(got, forward, grad_input)
    return forward, grad_input, f32(one) + f32(two)


def solution(mesh):
    fine = Mesh(mesh.devices.reshape(SIZES), AXES)
    token_spec, node_spec = P(AXES, None), P(("yh", "x"), None)
    return jax.shard_map(
        on_device,
        mesh=fine,
        in_specs=(token_spec, token_spec, node_spec, node_spec),
        out_specs=(token_spec, token_spec, token_spec),
        check_vma=False,
    )
```
